128 devices in a mesh: ctx: 16 (over x, z_lo, core), grp: 8 (over y, z_hi).
Axes of the slice: x: 4, y: 4, z: 4 (z_hi: 2, z_lo: 2; z = z_hi * 2 + z_lo), core: 2. Of those that a mesh axis runs over, the one named last changes fastest.
Arguments:
- queries: bfloat16 [8, 4096, 6144], P('grp', 'ctx'), may hold values from -48 to 48
- key_states: bfloat16 [8, 4096, 6144], P('grp', 'ctx'), may hold values from -6 to 6
- value_states: bfloat16 [8, 4096, 4096], P('grp', 'ctx'), may hold values from -6 to 6
- out_grad: bfloat16 [8, 4096, 4096], P('grp', 'ctx'), may hold values from -6 to 6
- lse_rest: float32 [8, 32, 4096], P('grp', None, 'ctx'), may hold values from 5 to 9
- out_dot: float32 [8, 32, 4096], P('grp', None, 'ctx'), may hold values from -16 to 16
- moe_acts: bfloat16 [8, 9, 7168, 256], P('grp', None, 'ctx'), may hold values from -6 to 6
- moe_grads: bfloat16 [8, 9, 256, 1024], P('grp', None, 'ctx'), may hold values from -0.375 to 0.375
- counts: int32 [8, 9], replicated, may hold values from 64 to 256, as said below
- replica_list: int32 [8, 7], replicated, may hold values from 0 to 1
Outputs:
- query_grad: bfloat16 [8, 4096, 6144], P('grp', 'ctx')
- key_grad: bfloat16 [8, 4096, 6144], P('grp', 'ctx')
- value_grad: bfloat16 [8, 4096, 4096], P('grp', 'ctx')
- expert_grad: float32 [8, 2, 7168, 1024], P('grp', None, 'ctx')
The draws below stay inside these ranges and needn't reach their ends.
Inputs may be any that keep to these rules, and one draw needn't show every extreme that they name: `counts`: in every group one slot holds exactly 256 live rows; every other slot holds between 64 and 128. Replica slot r of group g holds expert replica_list[g, r] of the 2 experts owned by group (g + r + 1) mod 8.
All inputs are finite; a program needn't handle non-finite values.
Results may differ from the reference program's by a relative error of at most 0.0075.
Values may be sent and summed in bfloat16 or wider, within the bound.
A program may use at most 256 MiB of HBM per device.

```python
import jax
import jax.numpy as jnp
from jax import lax

D = 7168
QK_DIM = 192
V_DIM = 128
HEADS = 32
FF = 1024
OWN = 2
TQ = 256
CAP = 256
SEQ = 4096
BATCH = 8
REP = 7
SLOTS = 9
N_CTX = 16
N_GRP = 8


def normal_rows(key, limit_value):
    return jnp.clip(jax.random.normal(key, (BATCH, SEQ, HEADS * QK_DIM), jnp.float32), -limit_value, limit_value)


def draw_key_states(key, part):
    key = jax.random.fold_in(key, 31)
    return normal_rows(key, 6.0).astype(jnp.bfloat16)


def draw_queries(key, part):
    key = jax.random.fold_in(key, 37)
    return normal_rows(key, 6.0).astype(jnp.bfloat16)


def draw_counts(key, part):
    key = jax.random.fold_in(key, 3)
    low_key, full_key = jax.random.split(key)
    base_values = jax.random.randint(low_key, (N_GRP, SLOTS), CAP // 4, CAP // 2 + 1)
    full_slot = jax.random.randint(full_key, (N_GRP, 1), 0, SLOTS)
    return jnp.where(jnp.arange(SLOTS)[None, :] == full_slot, CAP, base_values).astype(jnp.int32)


def touch_ends(drawn, stream_key, least, largest):
    place = [jax.random.randint(jax.random.fold_in(stream_key, axis), (), 0, length) for axis, length in enumerate(drawn.shape)]
    longest = drawn.shape.index(max(drawn.shape))
    beside = place[:longest] + [(place[longest] + 1) % drawn.shape[longest]] + place[longest + 1:]
    return drawn.at[tuple(place)].set(least).at[tuple(beside)].set(largest)


def shard_levels(stream_key, shape, shards, smallest, top_value):
    level = 1.0
    for axis_at, parts in shards:
        heights = jax.random.uniform(jax.random.fold_in(jax.random.fold_in(stream_key, 6), axis_at), (parts,), jnp.float32, smallest / len(shards), top_value / len(shards))
        level = level * jnp.repeat(jnp.exp(heights), shape[axis_at] // parts).reshape((-1,) + (1,) * (len(shape) - 1 - axis_at))
    return level


def bell_draw(own_key, dims, spread, bound, cuts=(), held_as=jnp.bfloat16):
    entries = spread * jax.random.normal(own_key, dims, jnp.float32)
    if cuts:
        entries = entries * shard_levels(own_key, dims, cuts, -0.22, 0.18)
    return jnp.clip(entries, -bound, bound).astype(held_as)


def setup_inputs(seed: int = 0) -> dict:
    key_of = jax.random.split(jax.random.key(seed), 11)
    return {
        "queries": draw_queries(jax.random.fold_in(key_of[10], 71), 0),
        "key_states": draw_key_states(jax.random.fold_in(key_of[10], 71), 0),
        "value_states": bell_draw(key_of[2], (BATCH, SEQ, HEADS * V_DIM), 1.0, 6.0, ((0, 8), (1, 16))),
        "out_grad": bell_draw(key_of[3], (BATCH, SEQ, HEADS * V_DIM), 1.0, 6.0, ((0, 8), (1, 16))),
        "lse_rest": jnp.clip(5.0 + 4.0 * jax.random.uniform(key_of[4], (BATCH, HEADS, SEQ), jnp.float32) ** shard_levels(key_of[4], (BATCH, HEADS, SEQ), ((0, 8), (2, 16)), -0.2, 0.2), 5.0, 9.0),
        "out_dot": bell_draw(key_of[5], (BATCH, HEADS, SEQ), 4.0, 16.0, ((0, 8), (2, 16)), jnp.float32),
        "moe_acts": bell_draw(key_of[6], (N_GRP, SLOTS, D, CAP), 1.0, 6.0, ((0, 8), (2, 16))),
        "moe_grads": bell_draw(key_of[7], (N_GRP, SLOTS, CAP, FF), 0.0625, 0.375, ((0, 8), (2, 16))),
        "counts": draw_counts(jax.random.fold_in(key_of[10], 71), 0),
        "replica_list": touch_ends(jax.random.randint(key_of[9], (N_GRP, REP), 0, OWN), jax.random.fold_in(key_of[9], 1), 0, OWN - 1).astype(jnp.int32),
    }


def as_float(source_array):
    return source_array.astype(jnp.float32)


def rounded(value_in):
    return lax.optimization_barrier(value_in.astype(jnp.bfloat16)).astype(jnp.float32)


def window_mask(position, block_rows):
    query_pos = lax.iota(jnp.int32, block_rows)[:, None]
    key_pos = lax.iota(jnp.int32, 3 * block_rows)[None, :]
    behind = 2 - key_pos // block_rows
    present = position - behind >= 0
    causal = (behind > 0) | (key_pos - 2 * block_rows <= query_pos)
    return present & causal


def pair_grads(query_rows, key_rows, value_rows, grad_rows, rest_rows, dot_rows, allowed):
    score_scale = query_rows.shape[2] ** -0.5
    block_rows = query_rows.shape[0]
    scores = jnp.einsum('qhd,khd->hqk', as_float(query_rows), as_float(key_rows)) * score_scale
    masked = jnp.where(allowed[None], scores, -1e30)
    row_max = jnp.max(masked, axis=2, keepdims=True)
    window = row_max[:, :, 0] + jnp.log(jnp.sum(jnp.exp(masked - row_max), axis=2))
    combined = jnp.logaddexp(window, rest_rows)
    attn_prob = jnp.where(allowed[None], jnp.exp(masked - combined[:, :, None]), 0.0)
    prob_grad = jnp.einsum('qhv,khv->hqk', as_float(grad_rows), as_float(value_rows))
    dscore = (attn_prob * (prob_grad - dot_rows[:, :, None])).astype(jnp.bfloat16)
    prob_half = attn_prob.astype(jnp.bfloat16)

    def query_term(offset):
        return jnp.einsum('hqk,khd->qhd', as_float(dscore[:, :, offset:offset + block_rows]), as_float(key_rows[offset:offset + block_rows])) * score_scale

    query_grad = query_term(2 * block_rows) + rounded(query_term(block_rows)) + rounded(query_term(0))
    key_grad = jnp.einsum('hqk,qhd->khd', as_float(dscore), as_float(query_rows)) * score_scale
    value_grad = jnp.einsum('hqk,qhv->khv', as_float(prob_half), as_float(grad_rows))
    return query_grad, key_grad, value_grad


def sequence_grads(inputs):
    query_seq, key_seq, value_seq, grad_seq, rest_seq, dot_seq = inputs
    key_pad = jnp.concatenate([jnp.zeros((2 * TQ, key_seq.shape[1]), key_seq.dtype), key_seq], 0)
    value_pad = jnp.concatenate([jnp.zeros((2 * TQ, value_seq.shape[1]), value_seq.dtype), value_seq], 0)

    def block_step(pending, position):
        first_sum, second_sum = pending
        offset = position * TQ
        query_rows = lax.dynamic_slice_in_dim(query_seq, offset, TQ, 0).reshape(TQ, HEADS, QK_DIM)
        key_rows = lax.dynamic_slice_in_dim(key_pad, offset, 3 * TQ, 0).reshape(3 * TQ, HEADS, QK_DIM)
        value_rows = lax.dynamic_slice_in_dim(value_pad, offset, 3 * TQ, 0).reshape(3 * TQ, HEADS, V_DIM)
        grad_rows = lax.dynamic_slice_in_dim(grad_seq, offset, TQ, 0).reshape(TQ, HEADS, V_DIM)
        rest_rows = lax.dynamic_slice_in_dim(rest_seq, offset, TQ, 1)
        dot_rows = lax.dynamic_slice_in_dim(dot_seq, offset, TQ, 1)
        query_grad, key_grad, value_grad = pair_grads(query_rows, key_rows, value_rows, grad_rows, rest_rows, dot_rows, window_mask(position, TQ))
        finished = (second_sum[0] + rounded(key_grad[:TQ]), second_sum[1] + rounded(value_grad[:TQ]))
        moved_up = (first_sum[0] + rounded(key_grad[TQ:2 * TQ]), first_sum[1] + rounded(value_grad[TQ:2 * TQ]))
        fresh = (key_grad[2 * TQ:], value_grad[2 * TQ:])
        outputs = (query_grad.astype(jnp.bfloat16), finished[0].astype(jnp.bfloat16), finished[1].astype(jnp.bfloat16))
        return (fresh, moved_up), outputs

    zero_keys = jnp.zeros((TQ, HEADS, QK_DIM), jnp.float32)
    zero_values = jnp.zeros((TQ, HEADS, V_DIM), jnp.float32)
    start_state = ((zero_keys, zero_values), (zero_keys, zero_values))
    final_state, outputs = lax.scan(block_step, start_state, lax.iota(jnp.int32, N_CTX))
    last_sum, second_last = final_state
    query_out, key_done, value_done = outputs
    key_out = jnp.concatenate([key_done[2:], second_last[0].astype(jnp.bfloat16)[None], last_sum[0].astype(jnp.bfloat16)[None]], 0)
    value_out = jnp.concatenate([value_done[2:], second_last[1].astype(jnp.bfloat16)[None], last_sum[1].astype(jnp.bfloat16)[None]], 0)
    return (query_out.reshape(SEQ, HEADS * QK_DIM), key_out.reshape(SEQ, HEADS * QK_DIM), value_out.reshape(SEQ, HEADS * V_DIM))


def slot_partial(activations, hidden_grads, live_count):
    live_rows = lax.iota(jnp.int32, hidden_grads.shape[0])[:, None] < live_count
    masked = jnp.where(live_rows, hidden_grads, jnp.zeros_like(hidden_grads))
    return jnp.dot(activations, masked, preferred_element_type=jnp.float32)


def reference(queries, key_states, value_states, out_grad, lse_rest, out_dot, moe_acts, moe_grads, counts, replica_list):
    query_grad, key_grad, value_grad = lax.map(sequence_grads, (queries, key_states, value_states, out_grad, lse_rest, out_dot))

    def owner_grads(group_index):
        summed = jnp.stack([slot_partial(moe_acts[group_index, own_slot], moe_grads[group_index, own_slot], counts[group_index, own_slot]) for own_slot in range(OWN)])
        for replica in range(REP):
            source = (group_index - 1 - replica) % N_GRP
            incoming = slot_partial(moe_acts[source, OWN + replica], moe_grads[source, OWN + replica], counts[source, OWN + replica])
            chosen = replica_list[source, replica]
            weight = (lax.iota(jnp.int32, OWN) == chosen).astype(jnp.float32)
            summed = summed + weight[:, None, None] * incoming[None]
        return summed

    expert_grad = lax.map(owner_grads, lax.iota(jnp.int32, N_GRP))
    return query_grad, key_grad, value_grad, expert_grad
```

```python
import functools

import jax
import jax.numpy as jnp
from jax import lax
from jax.experimental import pallas as pl
from jax.experimental.pallas import tpu as pltpu
from jax.sharding import PartitionSpec as P

QK_DIM = 192
V_DIM = 128
PAIR_QK = 2 * QK_DIM
PAIR_V = 2 * V_DIM
AHEAD = 3
SCALE = QK_DIM**-0.5
LOW = -1e38
MESH = pl.DeviceIdType.MESH

M_Q, M_G, M_K, M_V, M_DQ, M_MS, M_W, M_DK, M_DV, M_DOT = range(10)


def rows_by_rows(a, b):
    return lax.dot_general(a, b, (((1,), (1,)), ((), ())), preferred_element_type=jnp.float32)


def plain(a, b):
    return lax.dot_general(a, b, (((1,), (0,)), ((), ())), preferred_element_type=jnp.float32)


def columns_by_rows(a, b):
    return lax.dot_general(a, b, (((0,), (0,)), ((), ())), preferred_element_type=jnp.float32)


def heads_of(ref, start, low_lanes, high_lanes):
    first = ref[:, pl.ds(start, 128)]
    middle = ref[:, pl.ds(pl.multiple_of(start + 128, 128), 128)]
    last = ref[:, pl.ds(pl.multiple_of(start + 256, 128), 128)]
    return (
        jnp.concatenate([first, middle * low_lanes], 1),
        jnp.concatenate([middle * high_lanes, last], 1),
    )


def store_pair(ref, index, even, odd):
    start = index
    kind = ref.dtype
    ref[:, pl.ds(start, 128)] = even[:, :128].astype(kind)
    ref[:, pl.ds(pl.multiple_of(start + 128, 128), 128)] = (even[:, 128:] + odd[:, :128]).astype(kind)
    ref[:, pl.ds(pl.multiple_of(start + 256, 128), 128)] = odd[:, 128:].astype(kind)


def attention_kernel(
    pairs,
    q,
    k,
    v,
    g,
    rest,
    dot,
    dq,
    dk,
    dv,
    qn,
    gn,
    dotn,
    ko,
    vo,
    dqs,
    dks,
    dvs,
    mss,
    msr,
    own_ms,
    ws,
    wr,
    fo,
    pring,
    dring,
    acck,
    accv,
    q2,
    g2,
    send,
    recv,
):
    rows = q.shape[0]
    me = lax.axis_index("ctx")
    total = lax.axis_size("ctx")
    core = lax.rem(me, 2)
    ahead_chip = lax.rem(me + 2, total)
    behind_chip = lax.rem(me + total - 2, total)
    other = me + 1 - 2 * core
    core_zero = core == 0
    c0 = jnp.where(core_zero, 1.0, 0.0).astype(jnp.float32)
    c1 = 1.0 - c0
    has_behind = me >= 2

    def qk_cols(pair):
        return pl.ds(pl.multiple_of(pair * PAIR_QK, 128), PAIR_QK)

    def v_cols(pair):
        return pl.ds(pl.multiple_of(pair * PAIR_V, 128), PAIR_V)

    def message(kind, pair):
        src, dst, target = {
            M_Q: lambda: (q.at[:, qk_cols(pair)], qn.at[:, qk_cols(pair)], behind_chip),
            M_G: lambda: (g.at[:, v_cols(pair)], gn.at[:, v_cols(pair)], behind_chip),
            M_K: lambda: (k.at[:, qk_cols(pair)], ko.at[:, qk_cols(pair)], other),
            M_V: lambda: (v.at[:, v_cols(pair)], vo.at[:, v_cols(pair)], other),
            M_DQ: lambda: (dqs.at[:, qk_cols(pair)], dq.at[:, qk_cols(pair)], ahead_chip),
            M_MS: lambda: (mss.at[pair], msr.at[pair], ahead_chip),
            M_W: lambda: (ws.at[pair], wr.at[pair], behind_chip),
            M_DK: lambda: (dks.at[:, qk_cols(pair)], dk.at[:, qk_cols(pair)], other),
            M_DV: lambda: (dvs.at[:, v_cols(pair)], dv.at[:, v_cols(pair)], other),
            M_DOT: lambda: (dot, dotn, behind_chip),
        }[kind]()
        return pltpu.make_async_remote_copy(
            src_ref=src,
            dst_ref=dst,
            send_sem=send.at[kind, pair],
            recv_sem=recv.at[kind, pair],
            device_id={"ctx": target},
            device_id_type=MESH,
        )

    barrier = pltpu.get_barrier_semaphore()
    for partner in (behind_chip, ahead_chip, other):
        pl.semaphore_signal(barrier, inc=1, device_id={"ctx": partner}, device_id_type=MESH)
    pl.semaphore_wait(barrier, 3)

    message(M_DOT, 0).start()
    for pair in range(min(AHEAD, pairs)):
        for kind in (M_Q, M_G, M_K, M_V):
            message(kind, pair).start()

    lane = lax.broadcasted_iota(jnp.int32, (1, 128), 1)
    low_lanes = jnp.where(lane < 64, 1.0, 0.0).astype(jnp.bfloat16)
    high_lanes = jnp.where(lane < 64, 0.0, 1.0).astype(jnp.bfloat16)
    is_low = lane < 64

    def pick_second(pair):
        @pl.when(core_zero)
        def _():
            q2[...] = qn[:, qk_cols(pair)]
            g2[...] = gn[:, v_cols(pair)]

        @pl.when(jnp.logical_not(core_zero))
        def _():
            q2[...] = q[:, qk_cols(pair)]
            g2[...] = g[:, v_cols(pair)]

    def v_head(ref, pair, head):
        return ref[:, pl.ds(pl.multiple_of(pair * PAIR_V + head * V_DIM, 128), V_DIM)]

    def first_phase(pair):
        for kind in (M_Q, M_G, M_K, M_V):
            message(kind, pair).wait_recv()

        @pl.when(pair == 0)
        def _():
            message(M_DOT, 0).wait_recv()

        @pl.when(pair + AHEAD < pairs)
        def _():
            for kind in (M_Q, M_G, M_K, M_V):
                message(kind, pair + AHEAD).start()

        pick_second(pair)
        slot = lax.rem(pair, 3)
        start = pl.multiple_of(pair * PAIR_QK, 128)
        k_own = heads_of(k, start, low_lanes, high_lanes)
        k_oth = heads_of(ko, start, low_lanes, high_lanes)
        q_own = heads_of(q, start, low_lanes, high_lanes)
        q_new = heads_of(qn, start, low_lanes, high_lanes)
        q_sec = heads_of(q2, 0, low_lanes, high_lanes)
        key_pos = lax.broadcasted_iota(jnp.int32, (rows, rows), 0)
        query_pos = lax.broadcasted_iota(jnp.int32, (rows, rows), 1)
        allowed = key_pos <= query_pos
        dot_new = dotn[pair]
        dot_own = dot[pair]
        dot_sec = c0 * dot_new + c1 * dot_own
        tops, sums, tops_own, sums_own, dq_heads = [], [], [], [], []
        for head in range(2):
            s1 = rows_by_rows(k_own[head], q_new[head]) * SCALE
            s2 = rows_by_rows(k_oth[head], q_sec[head]) * SCALE
            s3 = rows_by_rows(k_own[head], q_own[head]) * SCALE
            s3 = jnp.where(allowed, s3, -1e30)
            m1 = jnp.max(s1, 0, keepdims=True)
            m2 = jnp.max(s2, 0, keepdims=True)
            m3 = jnp.max(s3, 0, keepdims=True)
            top_new = jnp.maximum(m1, jnp.where(core_zero, m2, LOW))
            top_own = jnp.maximum(m3, jnp.where(core_zero, LOW, m2))
            top_sec = jnp.where(core_zero, top_new, top_own)
            p1 = jnp.exp(s1 - top_new)
            p2 = jnp.exp(s2 - top_sec)
            p3 = jnp.exp(s3 - top_own)
            z1 = jnp.sum(p1, 0, keepdims=True)
            z2 = jnp.sum(p2, 0, keepdims=True)
            z3 = jnp.sum(p3, 0, keepdims=True)
            tops.append(top_new)
            sums.append(z1 + c0 * z2)
            tops_own.append(top_own)
            sums_own.append(z3 + c1 * z2)
            g1 = rows_by_rows(v_head(v, pair, head), v_head(gn, pair, head))
            g2_ = rows_by_rows(v_head(vo, pair, head), g2[:, head * V_DIM : (head + 1) * V_DIM])
            g3 = rows_by_rows(v_head(v, pair, head), v_head(g, pair, head))
            d1 = (p1 * (g1 - dot_new[head : head + 1])).astype(jnp.bfloat16)
            d2 = (p2 * (g2_ - dot_sec[head : head + 1])).astype(jnp.bfloat16)
            d3 = (p3 * (g3 - dot_own[head : head + 1])).astype(jnp.bfloat16)
            for task, (p_, d_) in enumerate(((p1, d1), (p2, d2), (p3, d3))):
                pring[slot, head * 3 + task] = p_.astype(jnp.bfloat16)
                dring[slot, head * 3 + task] = d_
            dq_heads.append(columns_by_rows(d1, k_own[head]) + c0 * columns_by_rows(d2, k_oth[head]))
        zero = jnp.zeros((4, rows), jnp.float32)
        mss[pair] = jnp.concatenate(tops + sums + [zero], 0)
        own_ms[pair] = jnp.concatenate(tops_own + sums_own + [zero], 0)
        message(M_MS, pair).start()
        store_pair(dqs, start, *dq_heads)
        message(M_DQ, pair).start()

    def second_phase(pair):
        message(M_MS, pair).wait_recv()
        theirs = msr[pair]
        ours = own_ms[pair]
        away = rest[pair]
        top_far = jnp.where(has_behind, theirs[0:2], LOW)
        top = jnp.maximum(jnp.maximum(ours[0:2], away), top_far)
        whole = (
            ours[2:4] * jnp.exp(ours[0:2] - top)
            + jnp.exp(away - top)
            + theirs[2:4] * jnp.exp(top_far - top)
        )
        total_lse = top + jnp.log(whole)
        zero = jnp.zeros((6, rows), jnp.float32)
        ws[pair] = jnp.concatenate([jnp.exp(top_far - total_lse), zero], 0)
        fo[pair] = jnp.concatenate([jnp.exp(ours[0:2] - total_lse), zero], 0)
        message(M_W, pair).start()

    def third_phase(pair):
        message(M_W, pair).wait_recv()
        message(M_DQ, pair).wait_recv()
        pick_second(pair)
        slot = lax.rem(pair, 3)
        start = pl.multiple_of(pair * PAIR_QK, 128)
        k_own = heads_of(k, start, low_lanes, high_lanes)
        k_oth = heads_of(ko, start, low_lanes, high_lanes)
        q_own = heads_of(q, start, low_lanes, high_lanes)
        q_new = heads_of(qn, start, low_lanes, high_lanes)
        q_sec = heads_of(q2, 0, low_lanes, high_lanes)
        new_weight = wr[pair]
        own_weight = fo[pair]
        far_weight = ws[pair]
        sec_weight = c0 * new_weight + c1 * own_weight
        eye = lax.broadcasted_iota(jnp.int32, (rows, rows), 0) == lax.broadcasted_iota(
            jnp.int32, (rows, rows), 1
        )
        dq_heads, dk_heads, dko_heads, columns = [], [], [], []
        acc = lax.rem(pair, 2)
        for head in range(2):
            weights = [w[head : head + 1] for w in (new_weight, sec_weight, own_weight)]
            probs = [
                (pring[slot, head * 3 + t].astype(jnp.float32) * weights[t]).astype(jnp.bfloat16)
                for t in range(3)
            ]
            grads = [
                (dring[slot, head * 3 + t].astype(jnp.float32) * (weights[t] * SCALE)).astype(
                    jnp.bfloat16
                )
                for t in range(3)
            ]
            accv[acc, :, head * V_DIM : (head + 1) * V_DIM] = plain(
                probs[0], v_head(gn, pair, head)
            ) + plain(probs[2], v_head(g, pair, head))
            dvs[:, pl.ds(pl.multiple_of(pair * PAIR_V + head * V_DIM, 128), V_DIM)] = plain(
                probs[1], g2[:, head * V_DIM : (head + 1) * V_DIM]
            ).astype(jnp.bfloat16)
            dk_heads.append(plain(grads[0], q_new[head]) + plain(grads[2], q_own[head]))
            dko_heads.append(plain(grads[1], q_sec[head]))
            dq_heads.append(
                columns_by_rows(grads[2], k_own[head])
                + c1 * columns_by_rows(grads[1], k_oth[head])
            )
            columns.append(
                jnp.sum(jnp.where(eye, far_weight[head : head + 1] * SCALE, 0.0), 1, keepdims=True)
            )
        store_pair(dks, start, *dko_heads)
        message(M_DV, pair).start()
        message(M_DK, pair).start()
        store_pair(acck.at[acc], 0, *dk_heads)
        first = pl.ds(start, 128)
        middle = pl.ds(pl.multiple_of(start + 128, 128), 128)
        last = pl.ds(pl.multiple_of(start + 256, 128), 128)
        even, odd = dq_heads
        dq[:, first] = (even[:, :128] + columns[0] * dq[:, first].astype(jnp.float32)).astype(dq.dtype)
        dq[:, middle] = (
            even[:, 128:]
            + odd[:, :128]
            + jnp.where(is_low, columns[0], columns[1]) * dq[:, middle].astype(jnp.float32)
        ).astype(dq.dtype)
        dq[:, last] = (odd[:, 128:] + columns[1] * dq[:, last].astype(jnp.float32)).astype(dq.dtype)

    def fourth_phase(pair):
        message(M_DK, pair).wait_recv()
        message(M_DV, pair).wait_recv()
        acc = lax.rem(pair, 2)
        dk[:, qk_cols(pair)] = (acck[acc] + dk[:, qk_cols(pair)].astype(jnp.float32)).astype(dk.dtype)
        dv[:, v_cols(pair)] = (accv[acc] + dv[:, v_cols(pair)].astype(jnp.float32)).astype(dv.dtype)

    def step(at, carry):
        for lag, phase in enumerate((first_phase, second_phase, third_phase, fourth_phase)):
            @pl.when((at >= lag) & (at < pairs + lag))
            def _(lag=lag, phase=phase):
                phase(at - lag)

        return carry

    lax.fori_loop(0, pairs + 3, step, 0)

    message(M_DOT, 0).wait_send()

    def drain(pair, carry):
        for kind in (M_Q, M_G, M_K, M_V, M_DQ, M_MS, M_W, M_DK, M_DV):
            message(kind, pair).wait_send()
        return carry

    lax.fori_loop(0, pairs, drain, 0)


def attention_part(queries, key_states, value_states, out_grad, lse_rest, out_dot):
    rows, qk = queries.shape[1:]
    vv = value_states.shape[2]
    pairs = qk // PAIR_QK
    half = jnp.bfloat16
    vmem = pl.BlockSpec(memory_space=pltpu.VMEM)
    small = pltpu.VMEM((pairs, 8, rows), jnp.float32)
    wide = pltpu.VMEM((rows, qk), half)
    narrow = pltpu.VMEM((rows, vv), half)
    outs = pl.pallas_call(
        functools.partial(attention_kernel, pairs),
        out_shape=[
            jax.ShapeDtypeStruct((rows, qk), half),
            jax.ShapeDtypeStruct((rows, qk), half),
            jax.ShapeDtypeStruct((rows, vv), half),
        ],
        in_specs=[vmem] * 6,
        out_specs=[vmem] * 3,
        scratch_shapes=[
            wide,
            narrow,
            pltpu.VMEM((pairs, 2, rows), jnp.float32),
            wide,
            narrow,
            wide,
            wide,
            narrow,
            small,
            small,
            small,
            small,
            small,
            small,
            pltpu.VMEM((3, 6, rows, rows), half),
            pltpu.VMEM((3, 6, rows, rows), half),
            pltpu.VMEM((2, rows, PAIR_QK), jnp.float32),
            pltpu.VMEM((2, rows, PAIR_V), jnp.float32),
            pltpu.VMEM((rows, PAIR_QK), half),
            pltpu.VMEM((rows, PAIR_V), half),
            pltpu.SemaphoreType.DMA((10, pairs)),
            pltpu.SemaphoreType.DMA((10, pairs)),
        ],
        compiler_params=pltpu.CompilerParams(
            collective_id=0, has_side_effects=True, vmem_limit_bytes=58 * 2**20
        ),
        name="window_grads",
    )(
        queries[0],
        key_states[0],
        value_states[0],
        out_grad[0],
        lse_rest[0].reshape(pairs, 2, rows),
        out_dot[0].reshape(pairs, 2, rows),
    )
    return [out[None] for out in outs]


def passed_along(x, axis, by):
    length = lax.axis_size(axis)
    return lax.ppermute(x, axis, [(i, (i + by) % length) for i in range(length)])


def expert_part(moe_acts, moe_grads, counts, replica_list):
    acts = moe_acts[0]
    grads = moe_grads[0]
    group = lax.axis_index("grp")
    groups = lax.axis_size("grp")
    replicas = replica_list.shape[1]
    own = acts.shape[0] - replicas
    acts_in = [acts[slot] for slot in range(own)]
    grads_in = [grads[slot] for slot in range(own)]
    live = [counts[group, slot] for slot in range(own)]
    expert = [jnp.int32(slot) for slot in range(own)]
    for replica in range(replicas):
        source = (group - 1 - replica) % groups
        acts_in.append(passed_along(acts[own + replica], "grp", replica + 1))
        grads_in.append(passed_along(grads[own + replica], "grp", replica + 1))
        live.append(counts[source, own + replica])
        expert.append(replica_list[source, replica])
    rows_all = lax.all_gather(jnp.stack(grads_in), "ctx", axis=1, tiled=True)
    row_ids = lax.iota(jnp.int32, rows_all.shape[1])
    keep = row_ids[None, :] < jnp.stack(live)[:, None]
    chosen = jnp.stack(expert)[:, None] == lax.iota(jnp.int32, own)[None, :]
    parts = []
    left = jnp.concatenate(acts_in, 1)
    for k in range(own):
        masked = jnp.where((keep & chosen[:, k : k + 1])[:, :, None], rows_all, jnp.zeros_like(rows_all))
        parts.append(
            jnp.dot(left, masked.reshape(-1, masked.shape[2]), preferred_element_type=jnp.float32)
        )
    return jnp.stack(parts)[None]


def local(queries, key_states, value_states, out_grad, lse_rest, out_dot, moe_acts, moe_grads, counts, replica_list):
    grads = attention_part(queries, key_states, value_states, out_grad, lse_rest, out_dot)
    expert_grad = expert_part(moe_acts, moe_grads, counts, replica_list)
    return (*grads, expert_grad)


def solution(mesh):
    return jax.shard_map(
        local,
        mesh=mesh,
        in_specs=(
            P("grp", "ctx", None),
            P("grp", "ctx", None),
            P("grp", "ctx", None),
            P("grp", "ctx", None),
            P("grp", None, "ctx"),
            P("grp", None, "ctx"),
            P("grp", None, "ctx", None),
            P("grp", None, "ctx", None),
            P(),
            P(),
        ),
        out_specs=(
            P("grp", "ctx", None),
            P("grp", "ctx", None),
            P("grp", "ctx", None),
            P("grp", None, "ctx", None),
        ),
        check_vma=False,
    )
```

```python
import functools

import jax
import jax.numpy as jnp
from jax import lax
from jax.experimental import pallas as pl
from jax.experimental.pallas import tpu as pltpu
from jax.sharding import PartitionSpec as P

QK_DIM = 192
V_DIM = 128
PAIR_QK = 2 * QK_DIM
PAIR_V = 2 * V_DIM
AHEAD = 1
SCALE = QK_DIM**-0.5
LOW = -1e38
MESH = pl.DeviceIdType.MESH

M_Q, M_G, M_K, M_V, M_DQ, M_MS, M_W, M_DK, M_DV, M_DOT = range(10)

E_ACTS, E_ROWS, E_HIGH, E_SPREAD, E_LEVEL, E_AROUND, E_OTHER = range(7)


def first_sems(replicas, owners, columns):
    sizes = {
        E_ACTS: replicas,
        E_ROWS: replicas,
        E_HIGH: 1,
        E_SPREAD: 2 * (owners - 1),
        E_LEVEL: 1,
        E_AROUND: 2 * (columns - 1),
        E_OTHER: 2 * columns,
    }
    starts, total = {}, 0
    for kind, size in sizes.items():
        starts[kind] = total
        total += size
    return starts, total


def rows_by_rows(a, b):
    return lax.dot_general(a, b, (((1,), (1,)), ((), ())), preferred_element_type=jnp.float32)


def plain(a, b):
    return lax.dot_general(a, b, (((1,), (0,)), ((), ())), preferred_element_type=jnp.float32)


def columns_by_rows(a, b):
    return lax.dot_general(a, b, (((0,), (0,)), ((), ())), preferred_element_type=jnp.float32)


def heads_of(ref, start, low_lanes, high_lanes):
    first = ref[:, pl.ds(start, 128)]
    middle = ref[:, pl.ds(pl.multiple_of(start + 128, 128), 128)]
    last = ref[:, pl.ds(pl.multiple_of(start + 256, 128), 128)]
    return (
        jnp.concatenate([first, middle * low_lanes], 1),
        jnp.concatenate([middle * high_lanes, last], 1),
    )


def store_pair(ref, index, even, odd):
    start = index
    kind = ref.dtype
    ref[:, pl.ds(start, 128)] = even[:, :128].astype(kind)
    ref[:, pl.ds(pl.multiple_of(start + 128, 128), 128)] = (even[:, 128:] + odd[:, :128]).astype(kind)
    ref[:, pl.ds(pl.multiple_of(start + 256, 128), 128)] = odd[:, 128:].astype(kind)


def attention_kernel(
    pairs,
    q,
    k,
    v,
    g,
    rest,
    dot,
    acts,
    high,
    pieces,
    lanes,
    dq,
    dk,
    dv,
    expert,
    qn,
    gn,
    dotn,
    ko,
    vo,
    dqs,
    dks,
    dvs,
    mss,
    msr,
    own_ms,
    ws,
    wr,
    fo,
    pring,
    dring,
    acck,
    accv,
    q2,
    g2,
    left,
    right,
    made,
    send,
    recv,
    esend,
    erecv,
    own_sem,
    out_sem,
):
    rows = q.shape[0]
    me = lax.axis_index("ctx")
    total = lax.axis_size("ctx")
    core = lax.rem(me, 2)
    ahead_chip = lax.rem(me + 2, total)
    behind_chip = lax.rem(me + total - 2, total)
    other = me + 1 - 2 * core
    core_zero = core == 0
    c0 = jnp.where(core_zero, 1.0, 0.0).astype(jnp.float32)
    c1 = 1.0 - c0
    has_behind = me >= 2

    def qk_cols(pair):
        return pl.ds(pl.multiple_of(pair * PAIR_QK, 128), PAIR_QK)

    def v_cols(pair):
        return pl.ds(pl.multiple_of(pair * PAIR_V, 128), PAIR_V)

    def message(kind, pair):
        src, dst, target = {
            M_Q: lambda: (q.at[:, qk_cols(pair)], qn.at[:, qk_cols(pair)], behind_chip),
            M_G: lambda: (g.at[:, v_cols(pair)], gn.at[:, v_cols(pair)], behind_chip),
            M_K: lambda: (k.at[:, qk_cols(pair)], ko.at[:, qk_cols(pair)], other),
            M_V: lambda: (v.at[:, v_cols(pair)], vo.at[:, v_cols(pair)], other),
            M_DQ: lambda: (dqs.at[:, qk_cols(pair)], dq.at[:, qk_cols(pair)], ahead_chip),
            M_MS: lambda: (mss.at[pair], msr.at[pair], ahead_chip),
            M_W: lambda: (ws.at[pair], wr.at[pair], behind_chip),
            M_DK: lambda: (dks.at[:, qk_cols(pair)], dk.at[:, qk_cols(pair)], other),
            M_DV: lambda: (dvs.at[:, v_cols(pair)], dv.at[:, v_cols(pair)], other),
            M_DOT: lambda: (dot, dotn, behind_chip),
        }[kind]()
        return pltpu.make_async_remote_copy(
            src_ref=src,
            dst_ref=dst,
            send_sem=send.at[kind, pair],
            recv_sem=recv.at[kind, pair],
            device_id={"ctx": target},
            device_id_type=MESH,
        )

    group = lax.axis_index("grp")
    groups = lax.axis_size("grp")
    slots = acts.shape[0]
    replicas = groups - 1
    own_slots = slots - replicas
    half_rows = left.shape[1] // (2 * slots)
    piece = pieces.shape[1]
    columns = total // 4
    owners = groups // 2
    upper = (me >= total // 2).astype(jnp.int32)
    level = me + 2 - 4 * (lax.rem(me, 4) // 2)
    twin = group + 1 - 2 * lax.rem(group, 2)
    starts, _ = first_sems(replicas, owners, columns)

    def unit(device):
        return right.at[
            pl.ds(slots * (device >= total // 2).astype(jnp.int32), slots),
            pl.ds(pl.multiple_of(lax.rem(device, total // 2) * piece, piece), piece),
        ]

    def block(index):
        return left.at[:, pl.ds(pl.multiple_of(index * half_rows, 128), half_rows)]

    def expert_message(kind, at, src, dst, target):
        sem = starts[kind] + at
        return pltpu.make_async_remote_copy(
            src_ref=src,
            dst_ref=dst,
            send_sem=esend.at[sem],
            recv_sem=erecv.at[sem],
            device_id=target,
            device_id_type=MESH,
        )

    def in_group(device):
        return {"ctx": device, "grp": group}

    def owner(index):
        return {"ctx": me, "grp": index}

    def expert_messages(kind):
        if kind == E_ACTS:
            return [
                expert_message(
                    kind,
                    r,
                    acts.at[own_slots + r, :, pl.ds(0, half_rows)],
                    block(own_slots + r),
                    owner(lax.rem(group + r + 1, groups)),
                )
                for r in range(replicas)
            ]
        if kind == E_ROWS:
            return [
                expert_message(
                    kind,
                    r,
                    pieces.at[own_slots + r],
                    right.at[
                        slots * upper + own_slots + r,
                        pl.ds(pl.multiple_of(lax.rem(me, total // 2) * piece, piece), piece),
                    ],
                    owner(lax.rem(group + r + 1, groups)),
                )
                for r in range(replicas)
            ]
        if kind == E_HIGH:
            place = lax.rem(twin - group + groups, groups)
            return [expert_message(kind, 0, high, block(slots + 1 + place), owner(twin))]
        if kind == E_SPREAD:
            place = lax.rem(group - twin + groups, groups)
            found = []
            for m in range(1, owners):
                to = owner(lax.rem(group + 2 * m, groups))
                found.append(
                    expert_message(kind, 2 * m - 2, high, block(slots + 1 + 2 * m), to)
                )
                found.append(
                    expert_message(
                        kind,
                        2 * m - 1,
                        block(slots + 1 + place),
                        block(slots + 1 + lax.rem(place + 2 * m, groups)),
                        to,
                    )
                )
            return found
        if kind == E_LEVEL:
            return [expert_message(kind, 0, unit(me), unit(me), in_group(level))]
        if kind == E_AROUND:
            return [
                expert_message(
                    kind,
                    2 * m - 2 + which,
                    unit(device),
                    unit(device),
                    in_group(lax.rem(me + 4 * m, total)),
                )
                for m in range(1, columns)
                for which, device in enumerate((me, level))
            ]
        return [
            expert_message(kind, m, unit(2 * m + core), unit(2 * m + core), in_group(other))
            for m in range(2 * columns)
        ]

    def own_copies():
        found = [
            pltpu.make_async_copy(
                acts.at[slot, :, pl.ds(0, half_rows)], block(slot), own_sem.at[slot]
            )
            for slot in range(own_slots)
        ]
        found.append(pltpu.make_async_copy(high, block(slots + 1), own_sem.at[own_slots]))
        place = pl.ds(pl.multiple_of(lax.rem(me, total // 2) * piece, piece), piece)
        for slot in range(own_slots):
            found.append(
                pltpu.make_async_copy(
                    pieces.at[slot],
                    right.at[slots * upper + slot, place],
                    own_sem.at[own_slots + 1 + slot],
                )
            )
        return found

    def begin(*kinds):
        for kind in kinds:
            for each in expert_messages(kind):
                each.start()

    def arrived(*kinds):
        for kind in kinds:
            for each in expert_messages(kind):
                each.wait_recv()

    def left_behind(*kinds):
        for kind in kinds:
            for each in expert_messages(kind):
                each.wait_send()

    width = made.shape[2]
    parts = right.shape[2] // width

    def made_copy(index):
        slot = lax.rem(index, 2)
        cols = pl.ds(pl.multiple_of(lax.rem(index, parts) * width, 128), width)
        return pltpu.make_async_copy(
            made.at[slot], expert.at[lax.div(index, parts), :, cols], out_sem.at[slot]
        )

    def expert_step(index):
        @pl.when(index >= 2)
        def _():
            made_copy(index - 2).wait()

        mask = lanes[lax.div(index, parts)]
        cols = pl.ds(pl.multiple_of(lax.rem(index, parts) * width, 128), width)
        result = None
        for low, count in ((0, slots), (slots + 1, slots - 1)):
            here = slice(low * half_rows, (low + count) * half_rows)
            a = left[:, here] * mask[:, here]
            b = right[low : low + count, :, cols].reshape(count * half_rows, width)
            product = plain(a, b)
            result = product if result is None else result + product
        made[lax.rem(index, 2)] = result
        made_copy(index).start()

    barrier = pltpu.get_barrier_semaphore()
    partners = [in_group(partner) for partner in (behind_chip, ahead_chip, other, level)]
    partners += [in_group(lax.rem(me + 4 * m, total)) for m in range(1, columns)]
    partners += [owner(lax.rem(group + m, groups)) for m in range(1, groups)]
    for partner in partners:
        pl.semaphore_signal(barrier, inc=1, device_id=partner, device_id_type=MESH)
    pl.semaphore_wait(barrier, len(partners))

    message(M_DOT, 0).start()
    for pair in range(min(AHEAD, pairs)):
        for kind in (M_Q, M_G, M_K, M_V):
            message(kind, pair).start()

    lane = lax.broadcasted_iota(jnp.int32, (1, 128), 1)
    low_lanes = jnp.where(lane < 64, 1.0, 0.0).astype(jnp.bfloat16)
    high_lanes = jnp.where(lane < 64, 0.0, 1.0).astype(jnp.bfloat16)
    is_low = lane < 64

    def pick_second(pair):
        @pl.when(core_zero)
        def _():
            q2[...] = qn[:, qk_cols(pair)]
            g2[...] = gn[:, v_cols(pair)]

        @pl.when(jnp.logical_not(core_zero))
        def _():
            q2[...] = q[:, qk_cols(pair)]
            g2[...] = g[:, v_cols(pair)]

    def v_head(ref, pair, head):
        return ref[:, pl.ds(pl.multiple_of(pair * PAIR_V + head * V_DIM, 128), V_DIM)]

    def first_phase(pair):
        for kind in (M_Q, M_G, M_K, M_V):
            message(kind, pair).wait_recv()

        @pl.when(pair == 0)
        def _():
            message(M_DOT, 0).wait_recv()

        @pl.when(pair + AHEAD < pairs)
        def _():
            for kind in (M_Q, M_G, M_K, M_V):
                message(kind, pair + AHEAD).start()

        pick_second(pair)
        slot = lax.rem(pair, 3)
        start = pl.multiple_of(pair * PAIR_QK, 128)
        k_own = heads_of(k, start, low_lanes, high_lanes)
        k_oth = heads_of(ko, start, low_lanes, high_lanes)
        q_own = heads_of(q, start, low_lanes, high_lanes)
        q_new = heads_of(qn, start, low_lanes, high_lanes)
        q_sec = heads_of(q2, 0, low_lanes, high_lanes)
        key_pos = lax.broadcasted_iota(jnp.int32, (rows, rows), 0)
        query_pos = lax.broadcasted_iota(jnp.int32, (rows, rows), 1)
        allowed = key_pos <= query_pos
        dot_new = dotn[pair]
        dot_own = dot[pair]
        dot_sec = c0 * dot_new + c1 * dot_own
        tops, sums, tops_own, sums_own, dq_heads = [], [], [], [], []
        for head in range(2):
            s1 = rows_by_rows(k_own[head], q_new[head]) * SCALE
            s2 = rows_by_rows(k_oth[head], q_sec[head]) * SCALE
            s3 = rows_by_rows(k_own[head], q_own[head]) * SCALE
            s3 = jnp.where(allowed, s3, -1e30)
            m1 = jnp.max(s1, 0, keepdims=True)
            m2 = jnp.max(s2, 0, keepdims=True)
            m3 = jnp.max(s3, 0, keepdims=True)
            top_new = jnp.maximum(m1, jnp.where(core_zero, m2, LOW))
            top_own = jnp.maximum(m3, jnp.where(core_zero, LOW, m2))
            top_sec = jnp.where(core_zero, top_new, top_own)
            p1 = jnp.exp(s1 - top_new)
            p2 = jnp.exp(s2 - top_sec)
            p3 = jnp.exp(s3 - top_own)
            z1 = jnp.sum(p1, 0, keepdims=True)
            z2 = jnp.sum(p2, 0, keepdims=True)
            z3 = jnp.sum(p3, 0, keepdims=True)
            tops.append(top_new)
            sums.append(z1 + c0 * z2)
            tops_own.append(top_own)
            sums_own.append(z3 + c1 * z2)
            g1 = rows_by_rows(v_head(v, pair, head), v_head(gn, pair, head))
            g2_ = rows_by_rows(v_head(vo, pair, head), g2[:, head * V_DIM : (head + 1) * V_DIM])
            g3 = rows_by_rows(v_head(v, pair, head), v_head(g, pair, head))
            d1 = (p1 * (g1 - dot_new[head : head + 1])).astype(jnp.bfloat16)
            d2 = (p2 * (g2_ - dot_sec[head : head + 1])).astype(jnp.bfloat16)
            d3 = (p3 * (g3 - dot_own[head : head + 1])).astype(jnp.bfloat16)
            for task, (p_, d_) in enumerate(((p1, d1), (p2, d2), (p3, d3))):
                pring[slot, head * 3 + task] = p_.astype(jnp.bfloat16)
                dring[slot, head * 3 + task] = d_
            dq_heads.append(columns_by_rows(d1, k_own[head]) + c0 * columns_by_rows(d2, k_oth[head]))
        zero = jnp.zeros((4, rows), jnp.float32)
        mss[pair] = jnp.concatenate(tops + sums + [zero], 0)
        own_ms[pair] = jnp.concatenate(tops_own + sums_own + [zero], 0)
        message(M_MS, pair).start()
        store_pair(dqs, start, *dq_heads)
        message(M_DQ, pair).start()

    def second_phase(pair):
        message(M_MS, pair).wait_recv()
        theirs = msr[pair]
        ours = own_ms[pair]
        away = rest[pair]
        top_far = jnp.where(has_behind, theirs[0:2], LOW)
        top = jnp.maximum(jnp.maximum(ours[0:2], away), top_far)
        whole = (
            ours[2:4] * jnp.exp(ours[0:2] - top)
            + jnp.exp(away - top)
            + theirs[2:4] * jnp.exp(top_far - top)
        )
        total_lse = top + jnp.log(whole)
        zero = jnp.zeros((6, rows), jnp.float32)
        ws[pair] = jnp.concatenate([jnp.exp(top_far - total_lse), zero], 0)
        fo[pair] = jnp.concatenate([jnp.exp(ours[0:2] - total_lse), zero], 0)
        message(M_W, pair).start()

    def third_phase(pair):
        message(M_W, pair).wait_recv()
        message(M_DQ, pair).wait_recv()
        pick_second(pair)
        slot = lax.rem(pair, 3)
        start = pl.multiple_of(pair * PAIR_QK, 128)
        k_own = heads_of(k, start, low_lanes, high_lanes)
        k_oth = heads_of(ko, start, low_lanes, high_lanes)
        q_own = heads_of(q, start, low_lanes, high_lanes)
        q_new = heads_of(qn, start, low_lanes, high_lanes)
        q_sec = heads_of(q2, 0, low_lanes, high_lanes)
        new_weight = wr[pair]
        own_weight = fo[pair]
        far_weight = ws[pair]
        sec_weight = c0 * new_weight + c1 * own_weight
        eye = lax.broadcasted_iota(jnp.int32, (rows, rows), 0) == lax.broadcasted_iota(
            jnp.int32, (rows, rows), 1
        )
        dq_heads, dk_heads, dko_heads, columns = [], [], [], []
        acc = lax.rem(pair, 2)
        for head in range(2):
            weights = [w[head : head + 1] for w in (new_weight, sec_weight, own_weight)]
            probs = [
                (pring[slot, head * 3 + t].astype(jnp.float32) * weights[t]).astype(jnp.bfloat16)
                for t in range(3)
            ]
            grads = [
                (dring[slot, head * 3 + t].astype(jnp.float32) * (weights[t] * SCALE)).astype(
                    jnp.bfloat16
                )
                for t in range(3)
            ]
            accv[acc, :, head * V_DIM : (head + 1) * V_DIM] = plain(
                probs[0], v_head(gn, pair, head)
            ) + plain(probs[2], v_head(g, pair, head))
            dvs[:, pl.ds(pl.multiple_of(pair * PAIR_V + head * V_DIM, 128), V_DIM)] = plain(
                probs[1], g2[:, head * V_DIM : (head + 1) * V_DIM]
            ).astype(jnp.bfloat16)
            dk_heads.append(plain(grads[0], q_new[head]) + plain(grads[2], q_own[head]))
            dko_heads.append(plain(grads[1], q_sec[head]))
            dq_heads.append(
                columns_by_rows(grads[2], k_own[head])
                + c1 * columns_by_rows(grads[1], k_oth[head])
            )
            columns.append(
                jnp.sum(jnp.where(eye, far_weight[head : head + 1] * SCALE, 0.0), 1, keepdims=True)
            )
        store_pair(dks, start, *dko_heads)
        message(M_DV, pair).start()
        message(M_DK, pair).start()
        store_pair(acck.at[acc], 0, *dk_heads)
        first = pl.ds(start, 128)
        middle = pl.ds(pl.multiple_of(start + 128, 128), 128)
        last = pl.ds(pl.multiple_of(start + 256, 128), 128)
        even, odd = dq_heads
        dq[:, first] = (even[:, :128] + columns[0] * dq[:, first].astype(jnp.float32)).astype(dq.dtype)
        dq[:, middle] = (
            even[:, 128:]
            + odd[:, :128]
            + jnp.where(is_low, columns[0], columns[1]) * dq[:, middle].astype(jnp.float32)
        ).astype(dq.dtype)
        dq[:, last] = (odd[:, 128:] + columns[1] * dq[:, last].astype(jnp.float32)).astype(dq.dtype)

    def fourth_phase(pair):
        message(M_DK, pair).wait_recv()
        message(M_DV, pair).wait_recv()
        acc = lax.rem(pair, 2)
        dk[:, qk_cols(pair)] = (acck[acc] + dk[:, qk_cols(pair)].astype(jnp.float32)).astype(dk.dtype)
        dv[:, v_cols(pair)] = (accv[acc] + dv[:, v_cols(pair)].astype(jnp.float32)).astype(dv.dtype)

    def step(at, carry):
        for lag, phase in enumerate((first_phase, second_phase, third_phase, fourth_phase)):
            @pl.when((at >= lag) & (at < pairs + lag))
            def _(lag=lag, phase=phase):
                phase(at - lag)

        return carry

    def first_stage():
        for each in own_copies():
            each.start()
        begin(E_ROWS, E_HIGH)

    def second_stage():
        begin(E_ACTS)

    def third_stage():
        for each in own_copies():
            each.wait()
        arrived(E_ROWS, E_HIGH)
        begin(E_LEVEL, E_SPREAD)

    def fourth_stage():
        arrived(E_LEVEL)
        begin(E_AROUND)

    def fifth_stage():
        arrived(E_AROUND)
        begin(E_OTHER)

    def sixth_stage():
        arrived(E_OTHER, E_ACTS, E_SPREAD)

    stages = {1: first_stage, 2: second_stage, 3: third_stage, 5: fourth_stage, 8: fifth_stage, 9: sixth_stage}
    products = own_slots * parts
    product_at = 10

    def step_with_experts(at, carry):
        step(at, carry)
        for when, stage in stages.items():
            pl.when(at == when)(stage)

        @pl.when((at >= product_at) & (at < product_at + products))
        def _():
            expert_step(at - product_at)

        return carry

    lax.fori_loop(0, max(pairs + 3, product_at + products), step_with_experts, 0)
    for index in range(products - 2, products):
        made_copy(index).wait()
    left_behind(E_ACTS, E_ROWS, E_HIGH, E_SPREAD, E_LEVEL, E_AROUND, E_OTHER)

    message(M_DOT, 0).wait_send()

    def drain(pair, carry):
        for kind in (M_Q, M_G, M_K, M_V, M_DQ, M_MS, M_W, M_DK, M_DV):
            message(kind, pair).wait_send()
        return carry

    lax.fori_loop(0, pairs, drain, 0)


def gradients(queries, key_states, value_states, out_grad, lse_rest, out_dot, acts, high, pieces, lanes):
    rows, qk = queries.shape
    vv = value_states.shape[1]
    pairs = qk // PAIR_QK
    slots, features, cap = acts.shape
    hidden = pieces.shape[2]
    experts = lanes.shape[0]
    groups = lax.axis_size("grp")
    columns = lax.axis_size("ctx") // 4
    width = min(hidden, 256)
    _, sems = first_sems(groups - 1, groups // 2, columns)
    half = jnp.bfloat16
    vmem = pl.BlockSpec(memory_space=pltpu.VMEM)
    anywhere = pl.BlockSpec(memory_space=pl.ANY)
    small = pltpu.VMEM((pairs, 8, rows), jnp.float32)
    wide = pltpu.VMEM((rows, qk), half)
    narrow = pltpu.VMEM((rows, vv), half)
    return pl.pallas_call(
        functools.partial(attention_kernel, pairs),
        out_shape=[
            jax.ShapeDtypeStruct((rows, qk), half),
            jax.ShapeDtypeStruct((rows, qk), half),
            jax.ShapeDtypeStruct((rows, vv), half),
            jax.ShapeDtypeStruct((experts, features, hidden), jnp.float32),
        ],
        in_specs=[vmem] * 6 + [anywhere] * 3 + [vmem],
        out_specs=[vmem] * 3 + [anywhere],
        scratch_shapes=[
            wide,
            narrow,
            pltpu.VMEM((pairs, 2, rows), jnp.float32),
            wide,
            narrow,
            wide,
            wide,
            narrow,
            small,
            small,
            small,
            small,
            small,
            small,
            pltpu.VMEM((3, 6, rows, rows), half),
            pltpu.VMEM((3, 6, rows, rows), half),
            pltpu.VMEM((2, rows, PAIR_QK), jnp.float32),
            pltpu.VMEM((2, rows, PAIR_V), jnp.float32),
            pltpu.VMEM((rows, PAIR_QK), half),
            pltpu.VMEM((rows, PAIR_V), half),
            pltpu.VMEM((features, slots * cap), half),
            pltpu.VMEM((2 * slots, cap // 2, hidden), half),
            pltpu.VMEM((2, features, width), jnp.float32),
            pltpu.SemaphoreType.DMA((10, pairs)),
            pltpu.SemaphoreType.DMA((10, pairs)),
            pltpu.SemaphoreType.DMA((sems,)),
            pltpu.SemaphoreType.DMA((sems,)),
            pltpu.SemaphoreType.DMA((2 * experts + 1,)),
            pltpu.SemaphoreType.DMA((2,)),
        ],
        compiler_params=pltpu.CompilerParams(
            collective_id=0, has_side_effects=True, vmem_limit_bytes=60 * 2**20
        ),
        name="window_grads",
    )(
        queries,
        key_states,
        value_states,
        out_grad,
        lse_rest.reshape(pairs, 2, rows),
        out_dot.reshape(pairs, 2, rows),
        acts,
        high,
        pieces,
        lanes,
    )


def expert_inputs(acts, grads, counts, replica_list):
    group = lax.axis_index("grp")
    groups = lax.axis_size("grp")
    slots, _, cap = acts.shape
    replicas = replica_list.shape[1]
    own = slots - replicas
    half_rows = cap // 2
    full = jnp.argmax(counts[group])
    high = lax.dynamic_slice(acts, (full, 0, half_rows), (1, acts.shape[1], half_rows))[0]
    full_piece = lax.dynamic_slice_in_dim(grads, full, 1, 0)
    upper = lax.axis_index("ctx") >= lax.axis_size("ctx") // 2
    pieces = jnp.where(upper, jnp.broadcast_to(full_piece, grads.shape), grads)
    block = lax.iota(jnp.int32, slots)
    behind = jnp.maximum(block - own + 1, 0)
    source = (group - behind) % groups
    slot_id = lax.iota(jnp.int32, slots)
    mine = (source[:, None] == lax.iota(jnp.int32, groups)[None, :]).astype(jnp.int32)
    my_counts = jnp.sum(mine[:, :, None] * counts[None], 1)
    my_lists = jnp.sum(mine[:, :, None] * replica_list[None], 1)
    live = jnp.sum(jnp.where(block[:, None] == slot_id[None, :], my_counts, 0), 1)
    listed = jnp.sum(
        jnp.where((block[:, None] - own) == lax.iota(jnp.int32, replicas)[None, :], my_lists, 0), 1
    )
    expert = jnp.where(block < own, block, listed)
    back = jnp.maximum(block - 1, 0)
    src = (group - back) % groups
    theirs = (src[:, None] == lax.iota(jnp.int32, groups)[None, :]).astype(jnp.int32)
    their_counts = jnp.sum(theirs[:, :, None] * counts[None], 1)
    their_full = jnp.argmax(their_counts, 1)
    meant = jnp.where(back == 0, their_full < own, their_full == own + back - 1)
    their_lists = jnp.sum(theirs[:, :, None] * replica_list[None], 1)
    their_expert = jnp.sum(
        jnp.where((their_full[:, None] - own) == lax.iota(jnp.int32, replicas)[None, :], their_lists, 0), 1
    )
    high_expert = jnp.where(back == 0, their_full, their_expert)
    high_live = jnp.where(meant & (block >= 1), half_rows, 0)
    all_live = jnp.concatenate([jnp.minimum(live, half_rows), high_live])
    all_expert = jnp.concatenate([expert, high_expert])
    wanted = all_expert[None] == lax.iota(jnp.int32, own)[:, None]
    keep = lax.iota(jnp.int32, half_rows)[None, None] < jnp.where(wanted, all_live[None], 0)[:, :, None]
    lanes = keep.astype(jnp.bfloat16).reshape(own, 1, 2 * slots * half_rows)
    return high, pieces, lanes


def local(queries, key_states, value_states, out_grad, lse_rest, out_dot, moe_acts, moe_grads, counts, replica_list):
    high, pieces, lanes = expert_inputs(moe_acts[0], moe_grads[0], counts, replica_list)
    found = gradients(
        queries[0],
        key_states[0],
        value_states[0],
        out_grad[0],
        lse_rest[0],
        out_dot[0],
        moe_acts[0],
        high,
        pieces,
        lanes,
    )
    return tuple(each[None] for each in found)


def solution(mesh):
    return jax.shard_map(
        local,
        mesh=mesh,
        in_specs=(
            P("grp", "ctx", None),
            P("grp", "ctx", None),
            P("grp", "ctx", None),
            P("grp", "ctx", None),
            P("grp", None, "ctx"),
            P("grp", None, "ctx"),
            P("grp", None, "ctx", None),
            P("grp", None, "ctx", None),
            P(),
            P(),
        ),
        out_specs=(
            P("grp", "ctx", None),
            P("grp", "ctx", None),
            P("grp", "ctx", None),
            P("grp", None, "ctx", None),
        ),
        check_vma=False,
    )
```

```python
import functools

import jax
import jax.numpy as jnp
from jax import lax
from jax.experimental import pallas as pl
from jax.experimental.pallas import tpu as pltpu
from jax.sharding import PartitionSpec as P

QK_DIM = 192
V_DIM = 128
PAIR_QK = 2 * QK_DIM
PAIR_V = 2 * V_DIM
SCALE = QK_DIM**-0.5
LOW = -1e38
MESH = pl.DeviceIdType.MESH

M_Q, M_G, M_K, M_V, M_DQ, M_MS, M_W, M_DK, M_DV, M_DOT = range(10)
M_Q_VIA, M_G_VIA, M_DQ_VIA, M_Q_ON, M_G_ON, M_DQ_ON = range(10, 16)
KINDS = 16

E_ACTS, E_ROWS, E_HIGH, E_SPREAD, E_LEVEL, E_AROUND, E_OTHER = range(7)


def first_sems(replicas, owners, columns):
    sizes = {
        E_ACTS: replicas,
        E_ROWS: replicas,
        E_HIGH: 1,
        E_SPREAD: 2 * (owners - 1),
        E_LEVEL: 1,
        E_AROUND: 2 * (columns - 1),
        E_OTHER: 2 * columns,
    }
    starts, total = {}, 0
    for kind, size in sizes.items():
        starts[kind] = total
        total += size
    return starts, total


def rows_by_rows(a, b):
    return lax.dot_general(a, b, (((1,), (1,)), ((), ())), preferred_element_type=jnp.float32)


def plain(a, b):
    return lax.dot_general(a, b, (((1,), (0,)), ((), ())), preferred_element_type=jnp.float32)


def columns_by_rows(a, b):
    return lax.dot_general(a, b, (((0,), (0,)), ((), ())), preferred_element_type=jnp.float32)


def heads_of(ref, start, low_lanes, high_lanes):
    first = ref[:, pl.ds(start, 128)]
    middle = ref[:, pl.ds(pl.multiple_of(start + 128, 128), 128)]
    last = ref[:, pl.ds(pl.multiple_of(start + 256, 128), 128)]
    return (
        jnp.concatenate([first, middle * low_lanes], 1),
        jnp.concatenate([middle * high_lanes, last], 1),
    )


def store_pair(ref, index, even, odd):
    start = index
    kind = ref.dtype
    ref[:, pl.ds(start, 128)] = even[:, :128].astype(kind)
    ref[:, pl.ds(pl.multiple_of(start + 128, 128), 128)] = (even[:, 128:] + odd[:, :128]).astype(kind)
    ref[:, pl.ds(pl.multiple_of(start + 256, 128), 128)] = odd[:, 128:].astype(kind)


def attention_kernel(
    pairs,
    q,
    k,
    v,
    g,
    rest,
    dot,
    acts,
    high,
    pieces,
    lanes,
    dq,
    dk,
    dv,
    expert,
    q_via,
    g_via,
    dq_via,
    qn,
    gn,
    dotn,
    ko,
    vo,
    dqs,
    dks,
    dvs,
    mss,
    msr,
    own_ms,
    ws,
    wr,
    fo,
    pring,
    dring,
    acck,
    accv,
    q2,
    g2,
    left,
    right,
    made,
    send,
    recv,
    esend,
    erecv,
    own_sem,
    out_sem,
):
    rows = q.shape[0]
    me = lax.axis_index("ctx")
    total = lax.axis_size("ctx")
    core = lax.rem(me, 2)
    ahead_chip = lax.rem(me + 2, total)
    behind_chip = lax.rem(me + total - 2, total)
    other = me + 1 - 2 * core
    core_zero = core == 0
    c0 = jnp.where(core_zero, 1.0, 0.0).astype(jnp.float32)
    c1 = 1.0 - c0
    has_behind = me >= 2
    has_ahead = me < total - 2
    column = lax.div(me, 4)
    low_level = lax.rem(me, 4) < 2
    level = me + 2 - 4 * lax.div(lax.rem(me, 4), 2)
    last_column = total // 4 - 1

    def q_detour(boundary, pair):
        return (lax.rem(pair, 4) <= boundary) & (pair >= 2)

    def dq_detour(boundary, pair):
        return lax.rem(pair, 4) < 3 - boundary

    def sends_q_via(pair):
        return low_level & (column >= 1) & q_detour(column - 1, pair)

    def passes_q_on(pair):
        return jnp.logical_not(low_level) & (column >= 1) & q_detour(column - 1, pair)

    def sends_dq_via(pair):
        return jnp.logical_not(low_level) & (column < last_column) & dq_detour(column, pair)

    def passes_dq_on(pair):
        return low_level & (column < last_column) & dq_detour(column, pair)

    def qk_cols(pair):
        return pl.ds(pl.multiple_of(pair * PAIR_QK, 128), PAIR_QK)

    def v_cols(pair):
        return pl.ds(pl.multiple_of(pair * PAIR_V, 128), PAIR_V)

    def message(kind, pair):
        src, dst, target = {
            M_Q: lambda: (q.at[:, qk_cols(pair)], qn.at[:, qk_cols(pair)], behind_chip),
            M_G: lambda: (g.at[:, v_cols(pair)], gn.at[:, v_cols(pair)], behind_chip),
            M_K: lambda: (k.at[:, qk_cols(pair)], ko.at[:, qk_cols(pair)], other),
            M_V: lambda: (v.at[:, v_cols(pair)], vo.at[:, v_cols(pair)], other),
            M_DQ: lambda: (dqs.at[:, qk_cols(pair)], dq.at[:, qk_cols(pair)], ahead_chip),
            M_MS: lambda: (mss.at[pair], msr.at[pair], ahead_chip),
            M_W: lambda: (ws.at[pair], wr.at[pair], behind_chip),
            M_DK: lambda: (dks.at[:, qk_cols(pair)], dk.at[:, qk_cols(pair)], other),
            M_DV: lambda: (dvs.at[:, v_cols(pair)], dv.at[:, v_cols(pair)], other),
            M_DOT: lambda: (dot, dotn, behind_chip),
            M_Q_VIA: lambda: (q.at[:, qk_cols(pair)], q_via.at[:, qk_cols(pair)], level),
            M_G_VIA: lambda: (g.at[:, v_cols(pair)], g_via.at[:, v_cols(pair)], level),
            M_DQ_VIA: lambda: (dqs.at[:, qk_cols(pair)], dq_via.at[:, qk_cols(pair)], level),
            M_Q_ON: lambda: (
                q_via.at[:, qk_cols(pair)],
                qn.at[:, qk_cols(pair)],
                lax.rem(me + total - 4, total),
            ),
            M_G_ON: lambda: (
                g_via.at[:, v_cols(pair)],
                gn.at[:, v_cols(pair)],
                lax.rem(me + total - 4, total),
            ),
            M_DQ_ON: lambda: (
                dq_via.at[:, qk_cols(pair)],
                dq.at[:, qk_cols(pair)],
                lax.rem(me + 4, total),
            ),
        }[kind]()
        lands_as = {M_Q_ON: M_Q, M_G_ON: M_G, M_DQ_ON: M_DQ}.get(kind, kind)
        return pltpu.make_async_remote_copy(
            src_ref=src,
            dst_ref=dst,
            send_sem=send.at[kind, pair],
            recv_sem=recv.at[lands_as, pair],
            device_id={"ctx": target},
            device_id_type=MESH,
        )

    group = lax.axis_index("grp")
    groups = lax.axis_size("grp")
    slots = acts.shape[0]
    replicas = groups - 1
    own_slots = slots - replicas
    half_rows = left.shape[1] // (2 * slots)
    piece = pieces.shape[1]
    columns = total // 4
    owners = groups // 2
    upper = (me >= total // 2).astype(jnp.int32)
    twin = group + 1 - 2 * lax.rem(group, 2)
    starts, _ = first_sems(replicas, owners, columns)

    def unit(device):
        return right.at[
            pl.ds(slots * (device >= total // 2).astype(jnp.int32), slots),
            pl.ds(pl.multiple_of(lax.rem(device, total // 2) * piece, piece), piece),
        ]

    def block(index):
        return left.at[:, pl.ds(pl.multiple_of(index * half_rows, 128), half_rows)]

    def expert_message(kind, at, src, dst, target):
        sem = starts[kind] + at
        return pltpu.make_async_remote_copy(
            src_ref=src,
            dst_ref=dst,
            send_sem=esend.at[sem],
            recv_sem=erecv.at[sem],
            device_id=target,
            device_id_type=MESH,
        )

    def in_group(device):
        return {"ctx": device, "grp": group}

    def owner(index):
        return {"ctx": me, "grp": index}

    def expert_messages(kind):
        if kind == E_ACTS:
            return [
                expert_message(
                    kind,
                    r,
                    acts.at[own_slots + r, :, pl.ds(0, half_rows)],
                    block(own_slots + r),
                    owner(lax.rem(group + r + 1, groups)),
                )
                for r in range(replicas)
            ]
        if kind == E_ROWS:
            return [
                expert_message(
                    kind,
                    r,
                    pieces.at[own_slots + r],
                    right.at[
                        slots * upper + own_slots + r,
                        pl.ds(pl.multiple_of(lax.rem(me, total // 2) * piece, piece), piece),
                    ],
                    owner(lax.rem(group + r + 1, groups)),
                )
                for r in range(replicas)
            ]
        if kind == E_HIGH:
            place = lax.rem(twin - group + groups, groups)
            return [expert_message(kind, 0, high, block(slots + 1 + place), owner(twin))]
        if kind == E_SPREAD:
            place = lax.rem(group - twin + groups, groups)
            found = []
            for m in range(1, owners):
                to = owner(lax.rem(group + 2 * m, groups))
                found.append(
                    expert_message(kind, 2 * m - 2, high, block(slots + 1 + 2 * m), to)
                )
                found.append(
                    expert_message(
                        kind,
                        2 * m - 1,
                        block(slots + 1 + place),
                        block(slots + 1 + lax.rem(place + 2 * m, groups)),
                        to,
                    )
                )
            return found
        if kind == E_LEVEL:
            return [expert_message(kind, 0, unit(me), unit(me), in_group(level))]
        if kind == E_AROUND:
            return [
                expert_message(
                    kind,
                    2 * m - 2 + which,
                    unit(device),
                    unit(device),
                    in_group(lax.rem(me + 4 * m, total)),
                )
                for m in range(1, columns)
                for which, device in enumerate((me, level))
            ]
        return [
            expert_message(kind, m, unit(2 * m + core), unit(2 * m + core), in_group(other))
            for m in range(2 * columns)
        ]

    def own_copies():
        found = [
            pltpu.make_async_copy(
                acts.at[slot, :, pl.ds(0, half_rows)], block(slot), own_sem.at[slot]
            )
            for slot in range(own_slots)
        ]
        found.append(pltpu.make_async_copy(high, block(slots + 1), own_sem.at[own_slots]))
        place = pl.ds(pl.multiple_of(lax.rem(me, total // 2) * piece, piece), piece)
        for slot in range(own_slots):
            found.append(
                pltpu.make_async_copy(
                    pieces.at[slot],
                    right.at[slots * upper + slot, place],
                    own_sem.at[own_slots + 1 + slot],
                )
            )
        return found

    def begin(*kinds):
        for kind in kinds:
            for each in expert_messages(kind):
                each.start()

    def arrived(*kinds):
        for kind in kinds:
            for each in expert_messages(kind):
                each.wait_recv()

    def left_behind(*kinds):
        for kind in kinds:
            for each in expert_messages(kind):
                each.wait_send()

    width = made.shape[2]
    parts = right.shape[2] // width

    def made_copy(index):
        slot = lax.rem(index, 2)
        cols = pl.ds(pl.multiple_of(lax.rem(index, parts) * width, 128), width)
        return pltpu.make_async_copy(
            made.at[slot], expert.at[lax.div(index, parts), :, cols], out_sem.at[slot]
        )

    def expert_step(index):
        @pl.when(index >= 2)
        def _():
            made_copy(index - 2).wait()

        mask = lanes[lax.div(index, parts)]
        cols = pl.ds(pl.multiple_of(lax.rem(index, parts) * width, 128), width)
        result = None
        for low, count in ((0, slots), (slots + 1, slots - 1)):
            here = slice(low * half_rows, (low + count) * half_rows)
            a = left[:, here] * mask[:, here]
            b = right[low : low + count, :, cols].reshape(count * half_rows, width)
            product = plain(a, b)
            result = product if result is None else result + product
        made[lax.rem(index, 2)] = result
        made_copy(index).start()

    barrier = pltpu.get_barrier_semaphore()
    partners = [in_group(partner) for partner in (behind_chip, ahead_chip, other, level)]
    partners += [in_group(lax.rem(me + 4 * m, total)) for m in range(1, columns)]
    partners += [owner(lax.rem(group + m, groups)) for m in range(1, groups)]
    for partner in partners:
        pl.semaphore_signal(barrier, inc=1, device_id=partner, device_id_type=MESH)
    pl.semaphore_wait(barrier, len(partners))

    @pl.when(jnp.logical_not(has_ahead))
    def _():
        qn[...] = jnp.zeros_like(qn)
        gn[...] = jnp.zeros_like(gn)
        dotn[...] = jnp.zeros_like(dotn)
        wr[...] = jnp.zeros_like(wr)

    @pl.when(jnp.logical_not(has_behind))
    def _():
        msr[...] = jnp.zeros_like(msr)
        dq[...] = jnp.zeros_like(dq)

    def send_chunk(pair):
        message(M_K, pair).start()
        message(M_V, pair).start()
        via = sends_q_via(pair)

        @pl.when(has_behind & jnp.logical_not(via))
        def _():
            message(M_Q, pair).start()
            message(M_G, pair).start()

        @pl.when(via)
        def _():
            message(M_Q_VIA, pair).start()
            message(M_G_VIA, pair).start()

    def pass_q_on(pair):
        @pl.when((pair < pairs) & passes_q_on(pair))
        def _():
            message(M_Q_VIA, pair).wait_recv()
            message(M_Q_ON, pair).start()
            message(M_G_VIA, pair).wait_recv()
            message(M_G_ON, pair).start()

    def pass_dq_on(pair):
        @pl.when(passes_dq_on(pair))
        def _():
            message(M_DQ_VIA, pair).wait_recv()
            message(M_DQ_ON, pair).start()

    @pl.when(has_behind)
    def _():
        message(M_DOT, 0).start()

    send_chunk(0)

    lane = lax.broadcasted_iota(jnp.int32, (1, 128), 1)
    low_lanes = jnp.where(lane < 64, 1.0, 0.0).astype(jnp.bfloat16)
    high_lanes = jnp.where(lane < 64, 0.0, 1.0).astype(jnp.bfloat16)
    is_low = lane < 64

    def pick_second(pair):
        @pl.when(core_zero)
        def _():
            q2[...] = qn[:, qk_cols(pair)]
            g2[...] = gn[:, v_cols(pair)]

        @pl.when(jnp.logical_not(core_zero))
        def _():
            q2[...] = q[:, qk_cols(pair)]
            g2[...] = g[:, v_cols(pair)]

    def v_head(ref, pair, head):
        return ref[:, pl.ds(pl.multiple_of(pair * PAIR_V + head * V_DIM, 128), V_DIM)]

    def first_phase(pair):
        message(M_K, pair).wait_recv()
        message(M_V, pair).wait_recv()

        @pl.when(has_ahead)
        def _():
            message(M_Q, pair).wait_recv()
            message(M_G, pair).wait_recv()

        @pl.when((pair == 0) & has_ahead)
        def _():
            message(M_DOT, 0).wait_recv()

        for extra, early in ((2 * pair + 1, True), (2 * pair + 2, True), (pair + 3, False)):
            pl.when((extra < pairs) & ((pair < 2) == early))(functools.partial(send_chunk, extra))

        pick_second(pair)
        slot = lax.rem(pair, 3)
        start = pl.multiple_of(pair * PAIR_QK, 128)
        k_own = heads_of(k, start, low_lanes, high_lanes)
        k_oth = heads_of(ko, start, low_lanes, high_lanes)
        q_own = heads_of(q, start, low_lanes, high_lanes)
        q_new = heads_of(qn, start, low_lanes, high_lanes)
        q_sec = heads_of(q2, 0, low_lanes, high_lanes)
        key_pos = lax.broadcasted_iota(jnp.int32, (rows, rows), 0)
        query_pos = lax.broadcasted_iota(jnp.int32, (rows, rows), 1)
        allowed = key_pos <= query_pos
        dot_new = dotn[pair]
        dot_own = dot[pair]
        dot_sec = c0 * dot_new + c1 * dot_own
        tops, sums, tops_own, sums_own, dq_heads = [], [], [], [], []
        for head in range(2):
            s1 = rows_by_rows(k_own[head], q_new[head]) * SCALE
            s2 = rows_by_rows(k_oth[head], q_sec[head]) * SCALE
            s3 = rows_by_rows(k_own[head], q_own[head]) * SCALE
            s3 = jnp.where(allowed, s3, -1e30)
            m1 = jnp.max(s1, 0, keepdims=True)
            m2 = jnp.max(s2, 0, keepdims=True)
            m3 = jnp.max(s3, 0, keepdims=True)
            top_new = jnp.maximum(m1, jnp.where(core_zero, m2, LOW))
            top_own = jnp.maximum(m3, jnp.where(core_zero, LOW, m2))
            top_sec = jnp.where(core_zero, top_new, top_own)
            p1 = jnp.exp(s1 - top_new)
            p2 = jnp.exp(s2 - top_sec)
            p3 = jnp.exp(s3 - top_own)
            z1 = jnp.sum(p1, 0, keepdims=True)
            z2 = jnp.sum(p2, 0, keepdims=True)
            z3 = jnp.sum(p3, 0, keepdims=True)
            tops.append(top_new)
            sums.append(z1 + c0 * z2)
            tops_own.append(top_own)
            sums_own.append(z3 + c1 * z2)
            g1 = rows_by_rows(v_head(v, pair, head), v_head(gn, pair, head))
            g2_ = rows_by_rows(v_head(vo, pair, head), g2[:, head * V_DIM : (head + 1) * V_DIM])
            g3 = rows_by_rows(v_head(v, pair, head), v_head(g, pair, head))
            d1 = (p1 * (g1 - dot_new[head : head + 1])).astype(jnp.bfloat16)
            d2 = (p2 * (g2_ - dot_sec[head : head + 1])).astype(jnp.bfloat16)
            d3 = (p3 * (g3 - dot_own[head : head + 1])).astype(jnp.bfloat16)
            for task, (p_, d_) in enumerate(((p1, d1), (p2, d2), (p3, d3))):
                pring[slot, head * 3 + task] = p_.astype(jnp.bfloat16)
                dring[slot, head * 3 + task] = d_
            dq_heads.append(columns_by_rows(d1, k_own[head]) + c0 * columns_by_rows(d2, k_oth[head]))
        zero = jnp.zeros((4, rows), jnp.float32)
        mss[pair] = jnp.concatenate(tops + sums + [zero], 0)
        own_ms[pair] = jnp.concatenate(tops_own + sums_own + [zero], 0)
        store_pair(dqs, start, *dq_heads)
        via = sends_dq_via(pair)

        @pl.when(has_ahead)
        def _():
            message(M_MS, pair).start()

        @pl.when(has_ahead & jnp.logical_not(via))
        def _():
            message(M_DQ, pair).start()

        @pl.when(via)
        def _():
            message(M_DQ_VIA, pair).start()

        @pl.when(pair == 1)
        def _():
            pass_q_on(1)
            pass_q_on(2)

        @pl.when(pair == 2)
        def _():
            pass_q_on(3)
            pass_q_on(4)

        @pl.when(pair >= 3)
        def _():
            pass_q_on(pair + 2)

    def second_phase(pair):
        pass_dq_on(pair)

        @pl.when(has_behind)
        def _():
            message(M_MS, pair).wait_recv()

        theirs = msr[pair]
        ours = own_ms[pair]
        away = rest[pair]
        top_far = jnp.where(has_behind, theirs[0:2], LOW)
        top = jnp.maximum(jnp.maximum(ours[0:2], away), top_far)
        whole = (
            ours[2:4] * jnp.exp(ours[0:2] - top)
            + jnp.exp(away - top)
            + theirs[2:4] * jnp.exp(top_far - top)
        )
        total_lse = top + jnp.log(whole)
        zero = jnp.zeros((6, rows), jnp.float32)
        ws[pair] = jnp.concatenate([jnp.exp(top_far - total_lse), zero], 0)
        fo[pair] = jnp.concatenate([jnp.exp(ours[0:2] - total_lse), zero], 0)

        @pl.when(has_behind)
        def _():
            message(M_W, pair).start()

    def third_phase(pair):
        @pl.when(has_ahead)
        def _():
            message(M_W, pair).wait_recv()

        @pl.when(has_behind)
        def _():
            message(M_DQ, pair).wait_recv()

        pick_second(pair)
        slot = lax.rem(pair, 3)
        start = pl.multiple_of(pair * PAIR_QK, 128)
        k_own = heads_of(k, start, low_lanes, high_lanes)
        k_oth = heads_of(ko, start, low_lanes, high_lanes)
        q_own = heads_of(q, start, low_lanes, high_lanes)
        q_new = heads_of(qn, start, low_lanes, high_lanes)
        q_sec = heads_of(q2, 0, low_lanes, high_lanes)
        new_weight = wr[pair]
        own_weight = fo[pair]
        far_weight = ws[pair]
        sec_weight = c0 * new_weight + c1 * own_weight
        eye = lax.broadcasted_iota(jnp.int32, (rows, rows), 0) == lax.broadcasted_iota(
            jnp.int32, (rows, rows), 1
        )
        dq_heads, dk_heads, dko_heads, columns = [], [], [], []
        acc = lax.rem(pair, 2)
        for head in range(2):
            weights = [w[head : head + 1] for w in (new_weight, sec_weight, own_weight)]
            probs = [
                (pring[slot, head * 3 + t].astype(jnp.float32) * weights[t]).astype(jnp.bfloat16)
                for t in range(3)
            ]
            grads = [
                (dring[slot, head * 3 + t].astype(jnp.float32) * (weights[t] * SCALE)).astype(
                    jnp.bfloat16
                )
                for t in range(3)
            ]
            accv[acc, :, head * V_DIM : (head + 1) * V_DIM] = plain(
                probs[0], v_head(gn, pair, head)
            ) + plain(probs[2], v_head(g, pair, head))
            dvs[:, pl.ds(pl.multiple_of(pair * PAIR_V + head * V_DIM, 128), V_DIM)] = plain(
                probs[1], g2[:, head * V_DIM : (head + 1) * V_DIM]
            ).astype(jnp.bfloat16)
            dk_heads.append(plain(grads[0], q_new[head]) + plain(grads[2], q_own[head]))
            dko_heads.append(plain(grads[1], q_sec[head]))
            dq_heads.append(
                columns_by_rows(grads[2], k_own[head])
                + c1 * columns_by_rows(grads[1], k_oth[head])
            )
            columns.append(
                jnp.sum(jnp.where(eye, far_weight[head : head + 1] * SCALE, 0.0), 1, keepdims=True)
            )
        store_pair(dks, start, *dko_heads)
        message(M_DV, pair).start()
        message(M_DK, pair).start()
        store_pair(acck.at[acc], 0, *dk_heads)
        first = pl.ds(start, 128)
        middle = pl.ds(pl.multiple_of(start + 128, 128), 128)
        last = pl.ds(pl.multiple_of(start + 256, 128), 128)
        even, odd = dq_heads
        dq[:, first] = (even[:, :128] + columns[0] * dq[:, first].astype(jnp.float32)).astype(dq.dtype)
        dq[:, middle] = (
            even[:, 128:]
            + odd[:, :128]
            + jnp.where(is_low, columns[0], columns[1]) * dq[:, middle].astype(jnp.float32)
        ).astype(dq.dtype)
        dq[:, last] = (odd[:, 128:] + columns[1] * dq[:, last].astype(jnp.float32)).astype(dq.dtype)

    def fourth_phase(pair):
        message(M_DK, pair).wait_recv()
        message(M_DV, pair).wait_recv()
        acc = lax.rem(pair, 2)
        dk[:, qk_cols(pair)] = (acck[acc] + dk[:, qk_cols(pair)].astype(jnp.float32)).astype(dk.dtype)
        dv[:, v_cols(pair)] = (accv[acc] + dv[:, v_cols(pair)].astype(jnp.float32)).astype(dv.dtype)

    def step(at, carry):
        for lag, phase in enumerate((first_phase, second_phase, third_phase, fourth_phase)):
            @pl.when((at >= lag) & (at < pairs + lag))
            def _(lag=lag, phase=phase):
                phase(at - lag)

        return carry

    def first_stage():
        for each in own_copies():
            each.start()
        begin(E_ROWS, E_HIGH)

    def second_stage():
        begin(E_ACTS)

    def third_stage():
        for each in own_copies():
            each.wait()
        arrived(E_ROWS, E_HIGH)
        begin(E_LEVEL, E_SPREAD)

    def fourth_stage():
        arrived(E_LEVEL)
        begin(E_AROUND)

    def fifth_stage():
        arrived(E_AROUND)
        begin(E_OTHER)

    def sixth_stage():
        arrived(E_OTHER, E_ACTS, E_SPREAD)

    stages = {1: first_stage, 2: second_stage, 3: third_stage, 5: fourth_stage, 8: fifth_stage, 9: sixth_stage}
    products = own_slots * parts
    product_at = 10

    def step_with_experts(at, carry):
        step(at, carry)
        for when, stage in stages.items():
            pl.when(at == when)(stage)

        @pl.when((at >= product_at) & (at < product_at + products))
        def _():
            expert_step(at - product_at)

        return carry

    lax.fori_loop(0, max(pairs + 3, product_at + products), step_with_experts, 0)
    for index in range(products - 2, products):
        made_copy(index).wait()
    left_behind(E_ACTS, E_ROWS, E_HIGH, E_SPREAD, E_LEVEL, E_AROUND, E_OTHER)

    @pl.when(has_behind)
    def _():
        message(M_DOT, 0).wait_send()

    def drain(pair, carry):
        def settle(condition, *kinds):
            @pl.when(condition)
            def _():
                for kind in kinds:
                    message(kind, pair).wait_send()

        settle(pair >= 0, M_K, M_V, M_DK, M_DV)
        settle(has_behind, M_W)
        settle(has_ahead, M_MS)
        settle(has_behind & jnp.logical_not(sends_q_via(pair)), M_Q, M_G)
        settle(sends_q_via(pair), M_Q_VIA, M_G_VIA)
        settle(passes_q_on(pair), M_Q_ON, M_G_ON)
        settle(has_ahead & jnp.logical_not(sends_dq_via(pair)), M_DQ)
        settle(sends_dq_via(pair), M_DQ_VIA)
        settle(passes_dq_on(pair), M_DQ_ON)
        return carry

    lax.fori_loop(0, pairs, drain, 0)


def gradients(queries, key_states, value_states, out_grad, lse_rest, out_dot, acts, high, pieces, lanes):
    rows, qk = queries.shape
    vv = value_states.shape[1]
    pairs = qk // PAIR_QK
    slots, features, cap = acts.shape
    hidden = pieces.shape[2]
    experts = lanes.shape[0]
    groups = lax.axis_size("grp")
    columns = lax.axis_size("ctx") // 4
    width = min(hidden, 256)
    _, sems = first_sems(groups - 1, groups // 2, columns)
    half = jnp.bfloat16
    vmem = pl.BlockSpec(memory_space=pltpu.VMEM)
    anywhere = pl.BlockSpec(memory_space=pl.ANY)
    small = pltpu.VMEM((pairs, 8, rows), jnp.float32)
    wide = pltpu.VMEM((rows, qk), half)
    narrow = pltpu.VMEM((rows, vv), half)
    return pl.pallas_call(
        functools.partial(attention_kernel, pairs),
        out_shape=[
            jax.ShapeDtypeStruct((rows, qk), half),
            jax.ShapeDtypeStruct((rows, qk), half),
            jax.ShapeDtypeStruct((rows, vv), half),
            jax.ShapeDtypeStruct((experts, features, hidden), jnp.float32),
            jax.ShapeDtypeStruct((rows, qk), half),
            jax.ShapeDtypeStruct((rows, vv), half),
            jax.ShapeDtypeStruct((rows, qk), half),
        ],
        in_specs=[vmem] * 6 + [anywhere] * 3 + [vmem],
        out_specs=[vmem] * 3 + [anywhere] * 4,
        scratch_shapes=[
            wide,
            narrow,
            pltpu.VMEM((pairs, 2, rows), jnp.float32),
            wide,
            narrow,
            wide,
            wide,
            narrow,
            small,
            small,
            small,
            small,
            small,
            small,
            pltpu.VMEM((3, 6, rows, rows), half),
            pltpu.VMEM((3, 6, rows, rows), half),
            pltpu.VMEM((2, rows, PAIR_QK), jnp.float32),
            pltpu.VMEM((2, rows, PAIR_V), jnp.float32),
            pltpu.VMEM((rows, PAIR_QK), half),
            pltpu.VMEM((rows, PAIR_V), half),
            pltpu.VMEM((features, slots * cap), half),
            pltpu.VMEM((2 * slots, cap // 2, hidden), half),
            pltpu.VMEM((2, features, width), jnp.float32),
            pltpu.SemaphoreType.DMA((KINDS, pairs)),
            pltpu.SemaphoreType.DMA((KINDS, pairs)),
            pltpu.SemaphoreType.DMA((sems,)),
            pltpu.SemaphoreType.DMA((sems,)),
            pltpu.SemaphoreType.DMA((2 * experts + 1,)),
            pltpu.SemaphoreType.DMA((2,)),
        ],
        compiler_params=pltpu.CompilerParams(
            collective_id=0, has_side_effects=True, vmem_limit_bytes=60 * 2**20
        ),
        name="window_grads",
    )(
        queries,
        key_states,
        value_states,
        out_grad,
        lse_rest.reshape(pairs, 2, rows),
        out_dot.reshape(pairs, 2, rows),
        acts,
        high,
        pieces,
        lanes,
    )[:4]


def expert_inputs(acts, grads, counts, replica_list):
    group = lax.axis_index("grp")
    groups = lax.axis_size("grp")
    slots, _, cap = acts.shape
    replicas = replica_list.shape[1]
    own = slots - replicas
    half_rows = cap // 2
    full = jnp.argmax(counts[group])
    high = lax.dynamic_slice(acts, (full, 0, half_rows), (1, acts.shape[1], half_rows))[0]
    full_piece = lax.dynamic_slice_in_dim(grads, full, 1, 0)
    upper = lax.axis_index("ctx") >= lax.axis_size("ctx") // 2
    pieces = jnp.where(upper, jnp.broadcast_to(full_piece, grads.shape), grads)
    block = lax.iota(jnp.int32, slots)
    behind = jnp.maximum(block - own + 1, 0)
    source = (group - behind) % groups
    slot_id = lax.iota(jnp.int32, slots)
    mine = (source[:, None] == lax.iota(jnp.int32, groups)[None, :]).astype(jnp.int32)
    my_counts = jnp.sum(mine[:, :, None] * counts[None], 1)
    my_lists = jnp.sum(mine[:, :, None] * replica_list[None], 1)
    live = jnp.sum(jnp.where(block[:, None] == slot_id[None, :], my_counts, 0), 1)
    listed = jnp.sum(
        jnp.where((block[:, None] - own) == lax.iota(jnp.int32, replicas)[None, :], my_lists, 0), 1
    )
    expert = jnp.where(block < own, block, listed)
    back = jnp.maximum(block - 1, 0)
    src = (group - back) % groups
    theirs = (src[:, None] == lax.iota(jnp.int32, groups)[None, :]).astype(jnp.int32)
    their_counts = jnp.sum(theirs[:, :, None] * counts[None], 1)
    their_full = jnp.argmax(their_counts, 1)
    meant = jnp.where(back == 0, their_full < own, their_full == own + back - 1)
    their_lists = jnp.sum(theirs[:, :, None] * replica_list[None], 1)
    their_expert = jnp.sum(
        jnp.where((their_full[:, None] - own) == lax.iota(jnp.int32, replicas)[None, :], their_lists, 0), 1
    )
    high_expert = jnp.where(back == 0, their_full, their_expert)
    high_live = jnp.where(meant & (block >= 1), half_rows, 0)
    all_live = jnp.concatenate([jnp.minimum(live, half_rows), high_live])
    all_expert = jnp.concatenate([expert, high_expert])
    wanted = all_expert[None] == lax.iota(jnp.int32, own)[:, None]
    keep = lax.iota(jnp.int32, half_rows)[None, None] < jnp.where(wanted, all_live[None], 0)[:, :, None]
    lanes = keep.astype(jnp.bfloat16).reshape(own, 1, 2 * slots * half_rows)
    return high, pieces, lanes


def local(queries, key_states, value_states, out_grad, lse_rest, out_dot, moe_acts, moe_grads, counts, replica_list):
    high, pieces, lanes = expert_inputs(moe_acts[0], moe_grads[0], counts, replica_list)
    found = gradients(
        queries[0],
        key_states[0],
        value_states[0],
        out_grad[0],
        lse_rest[0],
        out_dot[0],
        moe_acts[0],
        high,
        pieces,
        lanes,
    )
    return tuple(each[None] for each in found)


def solution(mesh):
    return jax.shard_map(
        local,
        mesh=mesh,
        in_specs=(
            P("grp", "ctx", None),
            P("grp", "ctx", None),
            P("grp", "ctx", None),
            P("grp", "ctx", None),
            P("grp", None, "ctx"),
            P("grp", None, "ctx"),
            P("grp", None, "ctx", None),
            P("grp", None, "ctx", None),
            P(),
            P(),
        ),
        out_specs=(
            P("grp", "ctx", None),
            P("grp", "ctx", None),
            P("grp", "ctx", None),
            P("grp", None, "ctx", None),
        ),
        check_vma=False,
    )
```

```python
import functools

import jax
import jax.numpy as jnp
from jax import lax
from jax.experimental import pallas as pl
from jax.experimental.pallas import tpu as pltpu
from jax.sharding import PartitionSpec as P

QK_DIM = 192
V_DIM = 128
PAIR_QK = 2 * QK_DIM
PAIR_V = 2 * V_DIM
SCALE = QK_DIM**-0.5
LOW = -1e38
MESH = pl.DeviceIdType.MESH

M_Q, M_G, M_K, M_V, M_DQ, M_MS, M_W, M_DK, M_DV, M_DOT = range(10)
M_Q_VIA, M_G_VIA, M_DQ_VIA, M_Q_ON, M_G_ON, M_DQ_ON = range(10, 16)
KINDS = 16
LIMIT_MIB = 48

E_ACTS, E_ROWS, E_HIGH, E_SPREAD, E_LEVEL, E_AROUND, E_OTHER = range(7)


def first_sems(replicas, owners, columns):
    sizes = {
        E_ACTS: replicas,
        E_ROWS: replicas,
        E_HIGH: 1,
        E_SPREAD: 2 * (owners - 1),
        E_LEVEL: 1,
        E_AROUND: 2 * (columns - 1),
        E_OTHER: 2 * columns,
    }
    starts, total = {}, 0
    for kind, size in sizes.items():
        starts[kind] = total
        total += size
    return starts, total


def rows_by_rows(a, b):
    return lax.dot_general(a, b, (((1,), (1,)), ((), ())), preferred_element_type=jnp.float32)


def plain(a, b):
    return lax.dot_general(a, b, (((1,), (0,)), ((), ())), preferred_element_type=jnp.float32)


def columns_by_rows(a, b):
    return lax.dot_general(a, b, (((0,), (0,)), ((), ())), preferred_element_type=jnp.float32)


def heads_of(ref, start, low_lanes, high_lanes):
    first = ref[:, pl.ds(start, 128)]
    middle = ref[:, pl.ds(pl.multiple_of(start + 128, 128), 128)]
    last = ref[:, pl.ds(pl.multiple_of(start + 256, 128), 128)]
    return (
        jnp.concatenate([first, middle * low_lanes], 1),
        jnp.concatenate([middle * high_lanes, last], 1),
    )


def store_pair(ref, index, even, odd):
    start = index
    kind = ref.dtype
    ref[:, pl.ds(start, 128)] = even[:, :128].astype(kind)
    ref[:, pl.ds(pl.multiple_of(start + 128, 128), 128)] = (even[:, 128:] + odd[:, :128]).astype(kind)
    ref[:, pl.ds(pl.multiple_of(start + 256, 128), 128)] = odd[:, 128:].astype(kind)


def attention_kernel(
    pairs,
    q_in,
    k_in,
    v_in,
    g_in,
    rest_rows,
    dot_rows,
    acts_in,
    grads_in,
    counts,
    lists,
    dq,
    dk,
    dv,
    expert,
    q_via,
    g_via,
    dq_via,
    qn,
    gn,
    dotn,
    ko,
    vo,
    dqs,
    dks,
    dvs,
    mss,
    msr,
    own_ms,
    ws,
    wr,
    fo,
    pring,
    dring,
    acck,
    accv,
    q2,
    g2,
    left,
    right,
    rest,
    dot,
    high,
    pieces,
    lanes,
    q,
    k,
    v,
    g,
    acts,
    grads,
    in_sem,
    send,
    recv,
    esend,
    erecv,
    own_sem,
):
    rows = q.shape[0]
    loads = [
        pltpu.make_async_copy(source, held, in_sem.at[at])
        for at, (source, held) in enumerate(
            ((k_in, k), (v_in, v), (q_in, q), (g_in, g), (acts_in, acts), (grads_in, grads))
        )
    ]
    for load in loads:
        load.start()
    me = lax.axis_index("ctx")
    total = lax.axis_size("ctx")
    core = lax.rem(me, 2)
    ahead_chip = lax.rem(me + 2, total)
    behind_chip = lax.rem(me + total - 2, total)
    other = me + 1 - 2 * core
    core_zero = core == 0
    c0 = jnp.where(core_zero, 1.0, 0.0).astype(jnp.float32)
    c1 = 1.0 - c0
    has_behind = me >= 2
    has_ahead = me < total - 2
    column = lax.div(me, 4)
    low_level = lax.rem(me, 4) < 2
    level = me + 2 - 4 * lax.div(lax.rem(me, 4), 2)
    last_column = total // 4 - 1

    def q_detour(boundary, pair):
        return (lax.rem(pair, 4) <= boundary) & (pair >= 2)

    def dq_detour(boundary, pair):
        return lax.rem(pair, 4) < 3 - boundary

    def sends_q_via(pair):
        return low_level & (column >= 1) & q_detour(column - 1, pair)

    def passes_q_on(pair):
        return jnp.logical_not(low_level) & (column >= 1) & q_detour(column - 1, pair)

    def sends_dq_via(pair):
        return jnp.logical_not(low_level) & (column < last_column) & dq_detour(column, pair)

    def passes_dq_on(pair):
        return low_level & (column < last_column) & dq_detour(column, pair)

    def qk_cols(pair):
        return pl.ds(pl.multiple_of(pair * PAIR_QK, 128), PAIR_QK)

    def v_cols(pair):
        return pl.ds(pl.multiple_of(pair * PAIR_V, 128), PAIR_V)

    def message(kind, pair):
        src, dst, target = {
            M_Q: lambda: (q_in.at[:, qk_cols(pair)], qn.at[:, qk_cols(pair)], behind_chip),
            M_G: lambda: (g_in.at[:, v_cols(pair)], gn.at[:, v_cols(pair)], behind_chip),
            M_K: lambda: (k_in.at[:, qk_cols(pair)], ko.at[:, qk_cols(pair)], other),
            M_V: lambda: (v_in.at[:, v_cols(pair)], vo.at[:, v_cols(pair)], other),
            M_DQ: lambda: (dqs.at[:, qk_cols(pair)], dq.at[:, qk_cols(pair)], ahead_chip),
            M_MS: lambda: (mss.at[pair], msr.at[pair], ahead_chip),
            M_W: lambda: (ws.at[pair], wr.at[pair], behind_chip),
            M_DK: lambda: (dks.at[:, qk_cols(pair)], dk.at[:, qk_cols(pair)], other),
            M_DV: lambda: (dvs.at[:, v_cols(pair)], dv.at[:, v_cols(pair)], other),
            M_DOT: lambda: (dot, dotn, behind_chip),
            M_Q_VIA: lambda: (q_in.at[:, qk_cols(pair)], q_via.at[:, qk_cols(pair)], level),
            M_G_VIA: lambda: (g_in.at[:, v_cols(pair)], g_via.at[:, v_cols(pair)], level),
            M_DQ_VIA: lambda: (dqs.at[:, qk_cols(pair)], dq_via.at[:, qk_cols(pair)], level),
            M_Q_ON: lambda: (
                q_via.at[:, qk_cols(pair)],
                qn.at[:, qk_cols(pair)],
                lax.rem(me + total - 4, total),
            ),
            M_G_ON: lambda: (
                g_via.at[:, v_cols(pair)],
                gn.at[:, v_cols(pair)],
                lax.rem(me + total - 4, total),
            ),
            M_DQ_ON: lambda: (
                dq_via.at[:, qk_cols(pair)],
                dq.at[:, qk_cols(pair)],
                lax.rem(me + 4, total),
            ),
        }[kind]()
        lands_as = {M_Q_ON: M_Q, M_G_ON: M_G, M_DQ_ON: M_DQ}.get(kind, kind)
        return pltpu.make_async_remote_copy(
            src_ref=src,
            dst_ref=dst,
            send_sem=send.at[kind, pair],
            recv_sem=recv.at[lands_as, pair],
            device_id={"ctx": target},
            device_id_type=MESH,
        )

    group = lax.axis_index("grp")
    groups = lax.axis_size("grp")
    slots = acts.shape[0]
    replicas = groups - 1
    own_slots = slots - replicas
    half_rows = left.shape[1] // (2 * slots)
    piece = pieces.shape[1]
    columns = total // 4
    owners = groups // 2
    upper = (me >= total // 2).astype(jnp.int32)
    twin = group + 1 - 2 * lax.rem(group, 2)
    starts, _ = first_sems(replicas, owners, columns)

    def unit(device):
        return right.at[
            pl.ds(slots * (device >= total // 2).astype(jnp.int32), slots),
            pl.ds(pl.multiple_of(lax.rem(device, total // 2) * piece, piece), piece),
        ]

    def block(index):
        return left.at[:, pl.ds(pl.multiple_of(index * half_rows, 128), half_rows)]

    def expert_message(kind, at, src, dst, target):
        sem = starts[kind] + at
        return pltpu.make_async_remote_copy(
            src_ref=src,
            dst_ref=dst,
            send_sem=esend.at[sem],
            recv_sem=erecv.at[sem],
            device_id=target,
            device_id_type=MESH,
        )

    def in_group(device):
        return {"ctx": device, "grp": group}

    def owner(index):
        return {"ctx": me, "grp": index}

    def expert_messages(kind):
        if kind == E_ACTS:
            return [
                expert_message(
                    kind,
                    r,
                    acts.at[own_slots + r, :, pl.ds(0, half_rows)],
                    block(own_slots + r),
                    owner(lax.rem(group + r + 1, groups)),
                )
                for r in range(replicas)
            ]
        if kind == E_ROWS:
            return [
                expert_message(
                    kind,
                    r,
                    pieces.at[own_slots + r],
                    right.at[
                        slots * upper + own_slots + r,
                        pl.ds(pl.multiple_of(lax.rem(me, total // 2) * piece, piece), piece),
                    ],
                    owner(lax.rem(group + r + 1, groups)),
                )
                for r in range(replicas)
            ]
        if kind == E_HIGH:
            place = lax.rem(twin - group + groups, groups)
            return [expert_message(kind, 0, high, block(slots + 1 + place), owner(twin))]
        if kind == E_SPREAD:
            place = lax.rem(group - twin + groups, groups)
            found = []
            for m in range(1, owners):
                to = owner(lax.rem(group + 2 * m, groups))
                found.append(
                    expert_message(kind, 2 * m - 2, high, block(slots + 1 + 2 * m), to)
                )
                found.append(
                    expert_message(
                        kind,
                        2 * m - 1,
                        block(slots + 1 + place),
                        block(slots + 1 + lax.rem(place + 2 * m, groups)),
                        to,
                    )
                )
            return found
        if kind == E_LEVEL:
            return [expert_message(kind, 0, unit(me), unit(me), in_group(level))]
        if kind == E_AROUND:
            return [
                expert_message(
                    kind,
                    2 * m - 2 + which,
                    unit(device),
                    unit(device),
                    in_group(lax.rem(me + 4 * m, total)),
                )
                for m in range(1, columns)
                for which, device in enumerate((me, level))
            ]
        return [
            expert_message(kind, m, unit(2 * m + core), unit(2 * m + core), in_group(other))
            for m in range(2 * columns)
        ]

    def own_copies():
        found = [
            pltpu.make_async_copy(
                acts.at[slot, :, pl.ds(0, half_rows)], block(slot), own_sem.at[slot]
            )
            for slot in range(own_slots)
        ]
        found.append(pltpu.make_async_copy(high, block(slots + 1), own_sem.at[own_slots]))
        place = pl.ds(pl.multiple_of(lax.rem(me, total // 2) * piece, piece), piece)
        for slot in range(own_slots):
            found.append(
                pltpu.make_async_copy(
                    pieces.at[slot],
                    right.at[slots * upper + slot, place],
                    own_sem.at[own_slots + 1 + slot],
                )
            )
        return found

    def begin(*kinds):
        for kind in kinds:
            for each in expert_messages(kind):
                each.start()

    def arrived(*kinds):
        for kind in kinds:
            for each in expert_messages(kind):
                each.wait_recv()

    def left_behind(*kinds):
        for kind in kinds:
            for each in expert_messages(kind):
                each.wait_send()

    width = min(expert.shape[2], 256)
    parts = expert.shape[2] // width

    def expert_step(index):
        mask = lanes[lax.div(index, parts)][0:1].astype(left.dtype)
        cols = pl.ds(pl.multiple_of(lax.rem(index, parts) * width, 128), width)
        result = None
        for low, count in ((0, slots), (slots + 1, slots - 1)):
            here = slice(low * half_rows, (low + count) * half_rows)
            a = left[:, here] * mask[:, here]
            b = right[low : low + count, :, cols].reshape(count * half_rows, width)
            product = plain(a, b)
            result = product if result is None else result + product
        expert[lax.div(index, parts), :, cols] = result

    barrier = pltpu.get_barrier_semaphore()
    partners = [in_group(partner) for partner in (behind_chip, ahead_chip, other, level)]
    partners += [in_group(lax.rem(me + 4 * m, total)) for m in range(1, columns)]
    partners += [owner(lax.rem(group + m, groups)) for m in range(1, groups)]
    for partner in partners:
        pl.semaphore_signal(barrier, inc=1, device_id=partner, device_id_type=MESH)
    pl.semaphore_wait(barrier, len(partners))

    @pl.when(jnp.logical_not(has_ahead))
    def _():
        qn[...] = jnp.zeros_like(qn)
        gn[...] = jnp.zeros_like(gn)
        dotn[...] = jnp.zeros_like(dotn)
        wr[...] = jnp.zeros_like(wr)

    @pl.when(jnp.logical_not(has_behind))
    def _():
        msr[...] = jnp.zeros_like(msr)
        dq[...] = jnp.zeros_like(dq)

    def send_chunk(pair):
        message(M_K, pair).start()
        message(M_V, pair).start()
        via = sends_q_via(pair)

        @pl.when(has_behind & jnp.logical_not(via))
        def _():
            message(M_Q, pair).start()
            message(M_G, pair).start()

        @pl.when(via)
        def _():
            message(M_Q_VIA, pair).start()
            message(M_G_VIA, pair).start()

    def pass_q_on(pair):
        @pl.when((pair < pairs) & passes_q_on(pair))
        def _():
            message(M_Q_VIA, pair).wait_recv()
            message(M_Q_ON, pair).start()
            message(M_G_VIA, pair).wait_recv()
            message(M_G_ON, pair).start()

    def pass_dq_on(pair):
        @pl.when(passes_dq_on(pair))
        def _():
            message(M_DQ_VIA, pair).wait_recv()
            message(M_DQ_ON, pair).start()

    send_chunk(0)
    for pair in range(pairs):
        rest[pair] = rest_rows[2 * pair : 2 * pair + 2]
        dot[pair] = dot_rows[2 * pair : 2 * pair + 2]

    @pl.when(has_behind)
    def _():
        message(M_DOT, 0).start()

    cap = acts.shape[2]
    full = [jnp.where(counts[group, slot] == cap, 1.0, 0.0) for slot in range(slots)]
    row_ids = lax.broadcasted_iota(jnp.int32, (1, half_rows), 1)

    def mark(expert_id, index, value):
        lanes[expert_id, 0:1, index * half_rows : (index + 1) * half_rows] = value

    for k_ in range(own_slots):
        for slot in range(own_slots):
            live = row_ids < counts[group, slot]
            mark(k_, slot, jnp.where(live, 1.0, 0.0) if slot == k_ else jnp.zeros(row_ids.shape))
        mark(k_, slots, jnp.zeros(row_ids.shape))
        mark(k_, slots + 1, jnp.zeros(row_ids.shape) + full[k_])
        for r in range(replicas):
            source = lax.rem(group + groups - 1 - r, groups)
            held = counts[source, own_slots + r]
            wanted = jnp.where(lists[source, r] == k_, 1.0, 0.0)
            mark(k_, own_slots + r, jnp.where(row_ids < held, wanted, 0.0))
            whole = jnp.where(held == cap, wanted, 0.0)
            mark(k_, slots + 2 + r, jnp.zeros(row_ids.shape) + whole)

    lane = lax.broadcasted_iota(jnp.int32, (1, 128), 1)
    low_lanes = jnp.where(lane < 64, 1.0, 0.0).astype(jnp.bfloat16)
    high_lanes = jnp.where(lane < 64, 0.0, 1.0).astype(jnp.bfloat16)
    is_low = lane < 64

    def pick_second(pair):
        @pl.when(core_zero)
        def _():
            q2[...] = qn[:, qk_cols(pair)]
            g2[...] = gn[:, v_cols(pair)]

        @pl.when(jnp.logical_not(core_zero))
        def _():
            q2[...] = q[:, qk_cols(pair)]
            g2[...] = g[:, v_cols(pair)]

    def v_head(ref, pair, head):
        return ref[:, pl.ds(pl.multiple_of(pair * PAIR_V + head * V_DIM, 128), V_DIM)]

    def first_phase(pair):
        message(M_K, pair).wait_recv()
        message(M_V, pair).wait_recv()

        @pl.when(has_ahead)
        def _():
            message(M_Q, pair).wait_recv()
            message(M_G, pair).wait_recv()

        @pl.when((pair == 0) & has_ahead)
        def _():
            message(M_DOT, 0).wait_recv()

        @pl.when(pair == 0)
        def _():
            for load in loads[:4]:
                load.wait()

        for extra, early in ((2 * pair + 1, True), (2 * pair + 2, True), (pair + 3, False)):
            pl.when((extra < pairs) & ((pair < 2) == early))(functools.partial(send_chunk, extra))

        pick_second(pair)
        slot = lax.rem(pair, 3)
        start = pl.multiple_of(pair * PAIR_QK, 128)
        k_own = heads_of(k, start, low_lanes, high_lanes)
        k_oth = heads_of(ko, start, low_lanes, high_lanes)
        q_own = heads_of(q, start, low_lanes, high_lanes)
        q_new = heads_of(qn, start, low_lanes, high_lanes)
        q_sec = heads_of(q2, 0, low_lanes, high_lanes)
        key_pos = lax.broadcasted_iota(jnp.int32, (rows, rows), 0)
        query_pos = lax.broadcasted_iota(jnp.int32, (rows, rows), 1)
        allowed = key_pos <= query_pos
        dot_new = dotn[pair]
        dot_own = dot[pair]
        dot_sec = c0 * dot_new + c1 * dot_own
        tops, sums, tops_own, sums_own, dq_heads = [], [], [], [], []
        for head in range(2):
            s1 = rows_by_rows(k_own[head], q_new[head]) * SCALE
            s2 = rows_by_rows(k_oth[head], q_sec[head]) * SCALE
            s3 = rows_by_rows(k_own[head], q_own[head]) * SCALE
            s3 = jnp.where(allowed, s3, -1e30)
            m1 = jnp.max(s1, 0, keepdims=True)
            m2 = jnp.max(s2, 0, keepdims=True)
            m3 = jnp.max(s3, 0, keepdims=True)
            top_new = jnp.maximum(m1, jnp.where(core_zero, m2, LOW))
            top_own = jnp.maximum(m3, jnp.where(core_zero, LOW, m2))
            top_sec = jnp.where(core_zero, top_new, top_own)
            p1 = jnp.exp(s1 - top_new)
            p2 = jnp.exp(s2 - top_sec)
            p3 = jnp.exp(s3 - top_own)
            z1 = jnp.sum(p1, 0, keepdims=True)
            z2 = jnp.sum(p2, 0, keepdims=True)
            z3 = jnp.sum(p3, 0, keepdims=True)
            tops.append(top_new)
            sums.append(z1 + c0 * z2)
            tops_own.append(top_own)
            sums_own.append(z3 + c1 * z2)
            g1 = rows_by_rows(v_head(v, pair, head), v_head(gn, pair, head))
            g2_ = rows_by_rows(v_head(vo, pair, head), g2[:, head * V_DIM : (head + 1) * V_DIM])
            g3 = rows_by_rows(v_head(v, pair, head), v_head(g, pair, head))
            d1 = (p1 * (g1 - dot_new[head : head + 1])).astype(jnp.bfloat16)
            d2 = (p2 * (g2_ - dot_sec[head : head + 1])).astype(jnp.bfloat16)
            d3 = (p3 * (g3 - dot_own[head : head + 1])).astype(jnp.bfloat16)
            for task, (p_, d_) in enumerate(((p1, d1), (p2, d2), (p3, d3))):
                pring[slot, head * 3 + task] = p_.astype(jnp.bfloat16)
                dring[slot, head * 3 + task] = d_
            dq_heads.append(columns_by_rows(d1, k_own[head]) + c0 * columns_by_rows(d2, k_oth[head]))
        zero = jnp.zeros((4, rows), jnp.float32)
        mss[pair] = jnp.concatenate(tops + sums + [zero], 0)
        own_ms[pair] = jnp.concatenate(tops_own + sums_own + [zero], 0)
        store_pair(dqs, start, *dq_heads)
        via = sends_dq_via(pair)

        @pl.when(has_ahead)
        def _():
            message(M_MS, pair).start()

        @pl.when(has_ahead & jnp.logical_not(via))
        def _():
            message(M_DQ, pair).start()

        @pl.when(via)
        def _():
            message(M_DQ_VIA, pair).start()

        @pl.when(pair == 1)
        def _():
            pass_q_on(1)
            pass_q_on(2)

        @pl.when(pair == 2)
        def _():
            pass_q_on(3)
            pass_q_on(4)

        @pl.when(pair >= 3)
        def _():
            pass_q_on(pair + 2)

    def second_phase(pair):
        pass_dq_on(pair)

        @pl.when(has_behind)
        def _():
            message(M_MS, pair).wait_recv()

        theirs = msr[pair]
        ours = own_ms[pair]
        away = rest[pair]
        top_far = jnp.where(has_behind, theirs[0:2], LOW)
        top = jnp.maximum(jnp.maximum(ours[0:2], away), top_far)
        whole = (
            ours[2:4] * jnp.exp(ours[0:2] - top)
            + jnp.exp(away - top)
            + theirs[2:4] * jnp.exp(top_far - top)
        )
        total_lse = top + jnp.log(whole)
        zero = jnp.zeros((6, rows), jnp.float32)
        ws[pair] = jnp.concatenate([jnp.exp(top_far - total_lse), zero], 0)
        fo[pair] = jnp.concatenate([jnp.exp(ours[0:2] - total_lse), zero], 0)

        @pl.when(has_behind)
        def _():
            message(M_W, pair).start()

    def third_phase(pair):
        @pl.when(has_ahead)
        def _():
            message(M_W, pair).wait_recv()

        @pl.when(has_behind)
        def _():
            message(M_DQ, pair).wait_recv()

        pick_second(pair)
        slot = lax.rem(pair, 3)
        start = pl.multiple_of(pair * PAIR_QK, 128)
        k_own = heads_of(k, start, low_lanes, high_lanes)
        k_oth = heads_of(ko, start, low_lanes, high_lanes)
        q_own = heads_of(q, start, low_lanes, high_lanes)
        q_new = heads_of(qn, start, low_lanes, high_lanes)
        q_sec = heads_of(q2, 0, low_lanes, high_lanes)
        new_weight = wr[pair]
        own_weight = fo[pair]
        far_weight = ws[pair]
        sec_weight = c0 * new_weight + c1 * own_weight
        eye = lax.broadcasted_iota(jnp.int32, (rows, rows), 0) == lax.broadcasted_iota(
            jnp.int32, (rows, rows), 1
        )
        dq_heads, dk_heads, dko_heads, columns = [], [], [], []
        acc = lax.rem(pair, 2)
        for head in range(2):
            weights = [w[head : head + 1] for w in (new_weight, sec_weight, own_weight)]
            probs = [
                (pring[slot, head * 3 + t].astype(jnp.float32) * weights[t]).astype(jnp.bfloat16)
                for t in range(3)
            ]
            grads = [
                (dring[slot, head * 3 + t].astype(jnp.float32) * (weights[t] * SCALE)).astype(
                    jnp.bfloat16
                )
                for t in range(3)
            ]
            accv[acc, :, head * V_DIM : (head + 1) * V_DIM] = plain(
                probs[0], v_head(gn, pair, head)
            ) + plain(probs[2], v_head(g, pair, head))
            dvs[:, pl.ds(pl.multiple_of(pair * PAIR_V + head * V_DIM, 128), V_DIM)] = plain(
                probs[1], g2[:, head * V_DIM : (head + 1) * V_DIM]
            ).astype(jnp.bfloat16)
            dk_heads.append(plain(grads[0], q_new[head]) + plain(grads[2], q_own[head]))
            dko_heads.append(plain(grads[1], q_sec[head]))
            dq_heads.append(
                columns_by_rows(grads[2], k_own[head])
                + c1 * columns_by_rows(grads[1], k_oth[head])
            )
            columns.append(
                jnp.sum(jnp.where(eye, far_weight[head : head + 1] * SCALE, 0.0), 1, keepdims=True)
            )
        store_pair(dks, start, *dko_heads)
        message(M_DV, pair).start()
        message(M_DK, pair).start()
        store_pair(acck.at[acc], 0, *dk_heads)
        first = pl.ds(start, 128)
        middle = pl.ds(pl.multiple_of(start + 128, 128), 128)
        last = pl.ds(pl.multiple_of(start + 256, 128), 128)
        even, odd = dq_heads
        dq[:, first] = (even[:, :128] + columns[0] * dq[:, first].astype(jnp.float32)).astype(dq.dtype)
        dq[:, middle] = (
            even[:, 128:]
            + odd[:, :128]
            + jnp.where(is_low, columns[0], columns[1]) * dq[:, middle].astype(jnp.float32)
        ).astype(dq.dtype)
        dq[:, last] = (odd[:, 128:] + columns[1] * dq[:, last].astype(jnp.float32)).astype(dq.dtype)

    def fourth_phase(pair):
        message(M_DK, pair).wait_recv()
        message(M_DV, pair).wait_recv()
        acc = lax.rem(pair, 2)
        dk[:, qk_cols(pair)] = (acck[acc] + dk[:, qk_cols(pair)].astype(jnp.float32)).astype(dk.dtype)
        dv[:, v_cols(pair)] = (accv[acc] + dv[:, v_cols(pair)].astype(jnp.float32)).astype(dv.dtype)

    def step(at, carry):
        for lag, phase in enumerate((first_phase, second_phase, third_phase, fourth_phase)):
            @pl.when((at >= lag) & (at < pairs + lag))
            def _(lag=lag, phase=phase):
                phase(at - lag)

        return carry

    def first_stage():
        for load in loads[4:]:
            load.wait()
        full_high, full_piece = 0.0, 0.0
        for slot in range(slots):
            full_high = full_high + full[slot] * acts[slot, :, half_rows:].astype(jnp.float32)
            full_piece = full_piece + full[slot] * grads[slot].astype(jnp.float32)
        high[...] = full_high.astype(high.dtype)
        is_upper = jnp.where(upper == 1, 1.0, 0.0)
        for slot in range(slots):
            mixed = is_upper * full_piece + (1.0 - is_upper) * grads[slot].astype(jnp.float32)
            pieces[slot] = mixed.astype(pieces.dtype)
        for each in own_copies():
            each.start()
        begin(E_ROWS, E_HIGH)

    def second_stage():
        begin(E_ACTS)

    def third_stage():
        for each in own_copies():
            each.wait()
        arrived(E_ROWS, E_HIGH)
        begin(E_LEVEL, E_SPREAD)

    def fourth_stage():
        arrived(E_LEVEL)
        begin(E_AROUND)

    def fifth_stage():
        arrived(E_AROUND)
        begin(E_OTHER)

    def sixth_stage():
        arrived(E_OTHER, E_ACTS, E_SPREAD)

    stages = {1: first_stage, 2: second_stage, 3: third_stage, 5: fourth_stage, 8: fifth_stage, 9: sixth_stage}
    products = own_slots * parts
    product_at = 10

    def step_with_experts(at, carry):
        step(at, carry)
        for when, stage in stages.items():
            pl.when(at == when)(stage)

        @pl.when((at >= product_at) & (at < product_at + products))
        def _():
            expert_step(at - product_at)

        return carry

    lax.fori_loop(0, max(pairs + 3, product_at + products), step_with_experts, 0)
    left_behind(E_ACTS, E_ROWS, E_HIGH, E_SPREAD, E_LEVEL, E_AROUND, E_OTHER)

    @pl.when(has_behind)
    def _():
        message(M_DOT, 0).wait_send()

    def drain(pair, carry):
        def settle(condition, *kinds):
            @pl.when(condition)
            def _():
                for kind in kinds:
                    message(kind, pair).wait_send()

        settle(pair >= 0, M_K, M_V, M_DK, M_DV)
        settle(has_behind, M_W)
        settle(has_ahead, M_MS)
        settle(has_behind & jnp.logical_not(sends_q_via(pair)), M_Q, M_G)
        settle(sends_q_via(pair), M_Q_VIA, M_G_VIA)
        settle(passes_q_on(pair), M_Q_ON, M_G_ON)
        settle(has_ahead & jnp.logical_not(sends_dq_via(pair)), M_DQ)
        settle(sends_dq_via(pair), M_DQ_VIA)
        settle(passes_dq_on(pair), M_DQ_ON)
        return carry

    lax.fori_loop(0, pairs, drain, 0)


def gradients(queries, key_states, value_states, out_grad, lse_rest, out_dot, acts, grads, counts, lists):
    rows, qk = queries.shape
    vv = value_states.shape[1]
    pairs = qk // PAIR_QK
    slots, features, cap = acts.shape
    hidden = grads.shape[2]
    experts = slots - lists.shape[1]
    groups = lax.axis_size("grp")
    columns = lax.axis_size("ctx") // 4
    _, sems = first_sems(groups - 1, groups // 2, columns)
    half = jnp.bfloat16
    vmem = pl.BlockSpec(memory_space=pltpu.VMEM)
    anywhere = pl.BlockSpec(memory_space=pl.ANY)
    small = pltpu.VMEM((pairs, 8, rows), jnp.float32)
    wide = pltpu.VMEM((rows, qk), half)
    narrow = pltpu.VMEM((rows, vv), half)
    return pl.pallas_call(
        functools.partial(attention_kernel, pairs),
        out_shape=[
            pltpu.VMEM((rows, qk), half),
            pltpu.VMEM((rows, qk), half),
            pltpu.VMEM((rows, vv), half),
            pltpu.VMEM((experts, features, hidden), jnp.float32),
            jax.ShapeDtypeStruct((rows, qk), half),
            jax.ShapeDtypeStruct((rows, vv), half),
            jax.ShapeDtypeStruct((rows, qk), half),
        ],
        in_specs=[anywhere] * 4 + [vmem] * 2 + [anywhere] * 2 + [pl.BlockSpec(memory_space=pltpu.SMEM)] * 2,
        out_specs=[vmem] * 4 + [anywhere] * 3,
        scratch_shapes=[
            wide,
            narrow,
            pltpu.VMEM((pairs, 2, rows), jnp.float32),
            wide,
            narrow,
            wide,
            wide,
            narrow,
            small,
            small,
            small,
            small,
            small,
            small,
            pltpu.VMEM((3, 6, rows, rows), half),
            pltpu.VMEM((3, 6, rows, rows), half),
            pltpu.VMEM((2, rows, PAIR_QK), jnp.float32),
            pltpu.VMEM((2, rows, PAIR_V), jnp.float32),
            pltpu.VMEM((rows, PAIR_QK), half),
            pltpu.VMEM((rows, PAIR_V), half),
            pltpu.VMEM((features, slots * cap), half),
            pltpu.VMEM((2 * slots, cap // 2, hidden), half),
            pltpu.VMEM((pairs, 2, rows), jnp.float32),
            pltpu.VMEM((pairs, 2, rows), jnp.float32),
            pltpu.VMEM((features, cap // 2), half),
            pltpu.VMEM(grads.shape, half),
            pltpu.VMEM((experts, 8, slots * cap), jnp.float32),
            wide,
            wide,
            narrow,
            narrow,
            pltpu.VMEM(acts.shape, half),
            pltpu.VMEM(grads.shape, half),
            pltpu.SemaphoreType.DMA((6,)),
            pltpu.SemaphoreType.DMA((KINDS, pairs)),
            pltpu.SemaphoreType.DMA((KINDS, pairs)),
            pltpu.SemaphoreType.DMA((sems,)),
            pltpu.SemaphoreType.DMA((sems,)),
            pltpu.SemaphoreType.DMA((2 * experts + 1,)),
        ],
        compiler_params=pltpu.CompilerParams(
            collective_id=0, has_side_effects=True, vmem_limit_bytes=LIMIT_MIB * 2**20
        ),
        name="window_grads",
    )(
        queries,
        key_states,
        value_states,
        out_grad,
        lse_rest,
        out_dot,
        acts,
        grads,
        counts,
        lists,
    )[:4]


def local(queries, key_states, value_states, out_grad, lse_rest, out_dot, moe_acts, moe_grads, counts, replica_list):
    found = gradients(
        queries[0],
        key_states[0],
        value_states[0],
        out_grad[0],
        lse_rest[0],
        out_dot[0],
        moe_acts[0],
        moe_grads[0],
        counts,
        replica_list,
    )
    return tuple(each[None] for each in found)


def solution(mesh):
    return jax.shard_map(
        local,
        mesh=mesh,
        in_specs=(
            P("grp", "ctx", None),
            P("grp", "ctx", None),
            P("grp", "ctx", None),
            P("grp", "ctx", None),
            P("grp", None, "ctx"),
            P("grp", None, "ctx"),
            P("grp", None, "ctx", None),
            P("grp", None, "ctx", None),
            P(),
            P(),
        ),
        out_specs=(
            P("grp", "ctx", None),
            P("grp", "ctx", None),
            P("grp", "ctx", None),
            P("grp", None, "ctx", None),
        ),
        check_vma=False,
    )
```

```python
import functools

import jax
import jax.numpy as jnp
from jax import lax
from jax.experimental import pallas as pl
from jax.experimental.pallas import tpu as pltpu
from jax.sharding import PartitionSpec as P

QK_DIM = 192
V_DIM = 128
PAIR_QK = 2 * QK_DIM
PAIR_V = 2 * V_DIM
SCALE = QK_DIM**-0.5
LOW = -1e38
MESH = pl.DeviceIdType.MESH

M_Q, M_G, M_K, M_V, M_DQ, M_MS, M_W, M_DK, M_DV, M_DOT = range(10)
M_Q_VIA, M_G_VIA, M_DQ_VIA, M_Q_ON, M_G_ON, M_DQ_ON = range(10, 16)
KINDS = 16
LIMIT_MIB = 48

E_ACTS, E_ROWS, E_HIGH, E_SPREAD, E_LEVEL, E_AROUND, E_OTHER = range(7)


def first_sems(slots, replicas, owners, columns):
    sizes = {
        E_ACTS: replicas,
        E_ROWS: replicas,
        E_HIGH: 1,
        E_SPREAD: 2 * (owners - 1),
        E_LEVEL: slots,
        E_AROUND: 2 * (columns - 1),
        E_OTHER: 2 * columns,
    }
    starts, total = {}, 0
    for kind, size in sizes.items():
        starts[kind] = total
        total += size
    return starts, total


def rows_by_rows(a, b):
    return lax.dot_general(a, b, (((1,), (1,)), ((), ())), preferred_element_type=jnp.float32)


def plain(a, b):
    return lax.dot_general(a, b, (((1,), (0,)), ((), ())), preferred_element_type=jnp.float32)


def columns_by_rows(a, b):
    return lax.dot_general(a, b, (((0,), (0,)), ((), ())), preferred_element_type=jnp.float32)


def heads_of(ref, start, low_lanes, high_lanes):
    first = ref[:, pl.ds(start, 128)]
    middle = ref[:, pl.ds(pl.multiple_of(start + 128, 128), 128)]
    last = ref[:, pl.ds(pl.multiple_of(start + 256, 128), 128)]
    return (
        jnp.concatenate([first, middle * low_lanes], 1),
        jnp.concatenate([middle * high_lanes, last], 1),
    )


def store_pair(ref, index, even, odd):
    start = index
    kind = ref.dtype
    ref[:, pl.ds(start, 128)] = even[:, :128].astype(kind)
    ref[:, pl.ds(pl.multiple_of(start + 128, 128), 128)] = (even[:, 128:] + odd[:, :128]).astype(kind)
    ref[:, pl.ds(pl.multiple_of(start + 256, 128), 128)] = odd[:, 128:].astype(kind)


def attention_kernel(
    pairs,
    q_in,
    k_in,
    v_in,
    g_in,
    rest_rows,
    dot_rows,
    acts_in,
    grads_in,
    counts,
    lists,
    dq,
    dk,
    dv,
    expert,
    q_via,
    g_via,
    dq_via,
    qn,
    gn,
    dotn,
    ko,
    vo,
    dqs,
    dks,
    dvs,
    mss,
    msr,
    own_ms,
    ws,
    wr,
    fo,
    pring,
    dring,
    acck,
    accv,
    q2,
    g2,
    left,
    right,
    rest,
    dot,
    high,
    pieces,
    lanes,
    q,
    k,
    v,
    g,
    acts,
    grads,
    in_sem,
    send,
    recv,
    esend,
    erecv,
    own_sem,
):
    rows = q.shape[0]
    loads = [
        pltpu.make_async_copy(source, held, in_sem.at[at])
        for at, (source, held) in enumerate(
            ((k_in, k), (v_in, v), (q_in, q), (g_in, g), (acts_in, acts), (grads_in, grads))
        )
    ]
    for load in loads:
        load.start()
    me = lax.axis_index("ctx")
    total = lax.axis_size("ctx")
    core = lax.rem(me, 2)
    ahead_chip = lax.rem(me + 2, total)
    behind_chip = lax.rem(me + total - 2, total)
    other = me + 1 - 2 * core
    core_zero = core == 0
    c0 = jnp.where(core_zero, 1.0, 0.0).astype(jnp.float32)
    c1 = 1.0 - c0
    has_behind = me >= 2
    has_ahead = me < total - 2
    column = lax.div(me, 4)
    low_level = lax.rem(me, 4) < 2
    level = me + 2 - 4 * lax.div(lax.rem(me, 4), 2)
    last_column = total // 4 - 1

    def q_detour(boundary, pair):
        return (lax.rem(pair, 4) <= boundary) & (pair >= 2)

    def dq_detour(boundary, pair):
        return lax.rem(pair, 4) < 3 - boundary

    def sends_q_via(pair):
        return low_level & (column >= 1) & q_detour(column - 1, pair)

    def passes_q_on(pair):
        return jnp.logical_not(low_level) & (column >= 1) & q_detour(column - 1, pair)

    def sends_dq_via(pair):
        return jnp.logical_not(low_level) & (column < last_column) & dq_detour(column, pair)

    def passes_dq_on(pair):
        return low_level & (column < last_column) & dq_detour(column, pair)

    def qk_cols(pair):
        return pl.ds(pl.multiple_of(pair * PAIR_QK, 128), PAIR_QK)

    def v_cols(pair):
        return pl.ds(pl.multiple_of(pair * PAIR_V, 128), PAIR_V)

    def message(kind, pair):
        src, dst, target = {
            M_Q: lambda: (q_in.at[:, qk_cols(pair)], qn.at[:, qk_cols(pair)], behind_chip),
            M_G: lambda: (g_in.at[:, v_cols(pair)], gn.at[:, v_cols(pair)], behind_chip),
            M_K: lambda: (k_in.at[:, qk_cols(pair)], ko.at[:, qk_cols(pair)], other),
            M_V: lambda: (v_in.at[:, v_cols(pair)], vo.at[:, v_cols(pair)], other),
            M_DQ: lambda: (dqs.at[:, qk_cols(pair)], dq.at[:, qk_cols(pair)], ahead_chip),
            M_MS: lambda: (mss.at[pair], msr.at[pair], ahead_chip),
            M_W: lambda: (ws.at[pair], wr.at[pair], behind_chip),
            M_DK: lambda: (dks.at[:, qk_cols(pair)], dk.at[:, qk_cols(pair)], other),
            M_DV: lambda: (dvs.at[:, v_cols(pair)], dv.at[:, v_cols(pair)], other),
            M_DOT: lambda: (dot, dotn, behind_chip),
            M_Q_VIA: lambda: (q_in.at[:, qk_cols(pair)], q_via.at[:, qk_cols(pair)], level),
            M_G_VIA: lambda: (g_in.at[:, v_cols(pair)], g_via.at[:, v_cols(pair)], level),
            M_DQ_VIA: lambda: (dqs.at[:, qk_cols(pair)], dq_via.at[:, qk_cols(pair)], level),
            M_Q_ON: lambda: (
                q_via.at[:, qk_cols(pair)],
                qn.at[:, qk_cols(pair)],
                lax.rem(me + total - 4, total),
            ),
            M_G_ON: lambda: (
                g_via.at[:, v_cols(pair)],
                gn.at[:, v_cols(pair)],
                lax.rem(me + total - 4, total),
            ),
            M_DQ_ON: lambda: (
                dq_via.at[:, qk_cols(pair)],
                dq.at[:, qk_cols(pair)],
                lax.rem(me + 4, total),
            ),
        }[kind]()
        lands_as = {M_Q_ON: M_Q, M_G_ON: M_G, M_DQ_ON: M_DQ}.get(kind, kind)
        return pltpu.make_async_remote_copy(
            src_ref=src,
            dst_ref=dst,
            send_sem=send.at[kind, pair],
            recv_sem=recv.at[lands_as, pair],
            device_id={"ctx": target},
            device_id_type=MESH,
        )

    group = lax.axis_index("grp")
    groups = lax.axis_size("grp")
    slots = acts.shape[0]
    replicas = groups - 1
    own_slots = slots - replicas
    half_rows = left.shape[1] // (2 * slots)
    piece = pieces.shape[1]
    columns = total // 4
    owners = groups // 2
    upper = (me >= total // 2).astype(jnp.int32)
    twin = group + 1 - 2 * lax.rem(group, 2)
    starts, _ = first_sems(slots, replicas, owners, columns)

    def unit(device):
        return right.at[
            pl.ds(slots * (device >= total // 2).astype(jnp.int32), slots),
            pl.ds(pl.multiple_of(lax.rem(device, total // 2) * piece, piece), piece),
        ]

    def piece_at(device, index):
        return right.at[
            slots * (device >= total // 2).astype(jnp.int32) + index,
            pl.ds(pl.multiple_of(lax.rem(device, total // 2) * piece, piece), piece),
        ]

    def block(index):
        return left.at[:, pl.ds(pl.multiple_of(index * half_rows, 128), half_rows)]

    def expert_message(kind, at, src, dst, target):
        sem = starts[kind] + at
        return pltpu.make_async_remote_copy(
            src_ref=src,
            dst_ref=dst,
            send_sem=esend.at[sem],
            recv_sem=erecv.at[sem],
            device_id=target,
            device_id_type=MESH,
        )

    def in_group(device):
        return {"ctx": device, "grp": group}

    def owner(index):
        return {"ctx": me, "grp": index}

    def expert_messages(kind):
        if kind == E_ACTS:
            return [
                expert_message(
                    kind,
                    r,
                    acts.at[own_slots + r, :, pl.ds(0, half_rows)],
                    block(own_slots + r),
                    owner(lax.rem(group + r + 1, groups)),
                )
                for r in range(replicas)
            ]
        if kind == E_ROWS:
            return [
                expert_message(
                    kind,
                    r,
                    pieces.at[own_slots + r],
                    piece_at(me, own_slots + r),
                    {"ctx": me if r % 2 else level, "grp": lax.rem(group + r + 1, groups)},
                )
                for r in range(replicas)
            ]
        if kind == E_HIGH:
            place = lax.rem(twin - group + groups, groups)
            return [expert_message(kind, 0, high, block(slots + 1 + place), owner(twin))]
        if kind == E_SPREAD:
            place = lax.rem(group - twin + groups, groups)
            found = []
            for m in range(1, owners):
                to = owner(lax.rem(group + 2 * m, groups))
                found.append(
                    expert_message(kind, 2 * m - 2, high, block(slots + 1 + 2 * m), to)
                )
                found.append(
                    expert_message(
                        kind,
                        2 * m - 1,
                        block(slots + 1 + place),
                        block(slots + 1 + lax.rem(place + 2 * m, groups)),
                        to,
                    )
                )
            return found
        if kind == E_LEVEL:
            found = []
            for index in range(slots):
                away = index >= own_slots and (index - own_slots) % 2 == 0
                held = piece_at(level if away else me, index)
                found.append(expert_message(kind, index, held, held, in_group(level)))
            return found
        if kind == E_AROUND:
            return [
                expert_message(
                    kind,
                    2 * m - 2 + which,
                    unit(device),
                    unit(device),
                    in_group(lax.rem(me + 4 * m, total)),
                )
                for m in range(1, columns)
                for which, device in enumerate((me, level))
            ]
        return [
            expert_message(kind, m, unit(2 * m + core), unit(2 * m + core), in_group(other))
            for m in range(2 * columns)
        ]

    def own_copies():
        found = [
            pltpu.make_async_copy(
                acts.at[slot, :, pl.ds(0, half_rows)], block(slot), own_sem.at[slot]
            )
            for slot in range(own_slots)
        ]
        found.append(pltpu.make_async_copy(high, block(slots + 1), own_sem.at[own_slots]))
        place = pl.ds(pl.multiple_of(lax.rem(me, total // 2) * piece, piece), piece)
        for slot in range(own_slots):
            found.append(
                pltpu.make_async_copy(
                    pieces.at[slot],
                    right.at[slots * upper + slot, place],
                    own_sem.at[own_slots + 1 + slot],
                )
            )
        return found

    def begin(*kinds):
        for kind in kinds:
            for each in expert_messages(kind):
                each.start()

    def arrived(*kinds):
        for kind in kinds:
            for each in expert_messages(kind):
                each.wait_recv()

    def left_behind(*kinds):
        for kind in kinds:
            for each in expert_messages(kind):
                each.wait_send()

    width = min(expert.shape[2], 256)
    parts = expert.shape[2] // width

    def expert_step(index):
        mask = lanes[lax.div(index, parts)][0:1].astype(left.dtype)
        cols = pl.ds(pl.multiple_of(lax.rem(index, parts) * width, 128), width)
        result = None
        for low, count in ((0, slots), (slots + 1, slots - 1)):
            here = slice(low * half_rows, (low + count) * half_rows)
            a = left[:, here] * mask[:, here]
            b = right[low : low + count, :, cols].reshape(count * half_rows, width)
            product = plain(a, b)
            result = product if result is None else result + product
        expert[lax.div(index, parts), :, cols] = result

    barrier = pltpu.get_barrier_semaphore()
    partners = [in_group(partner) for partner in (behind_chip, ahead_chip, other, level)]
    partners += [in_group(lax.rem(me + 4 * m, total)) for m in range(1, columns)]
    partners += [owner(lax.rem(group + m, groups)) for m in range(1, groups)]
    partners += [{"ctx": level, "grp": lax.rem(group + m, groups)} for m in range(1, groups, 2)]
    for partner in partners:
        pl.semaphore_signal(barrier, inc=1, device_id=partner, device_id_type=MESH)
    pl.semaphore_wait(barrier, len(partners))

    @pl.when(jnp.logical_not(has_ahead))
    def _():
        qn[...] = jnp.zeros_like(qn)
        gn[...] = jnp.zeros_like(gn)
        dotn[...] = jnp.zeros_like(dotn)
        wr[...] = jnp.zeros_like(wr)

    @pl.when(jnp.logical_not(has_behind))
    def _():
        msr[...] = jnp.zeros_like(msr)
        dq[...] = jnp.zeros_like(dq)

    def send_chunk(pair):
        message(M_K, pair).start()
        message(M_V, pair).start()
        via = sends_q_via(pair)

        @pl.when(has_behind & jnp.logical_not(via))
        def _():
            message(M_Q, pair).start()
            message(M_G, pair).start()

        @pl.when(via)
        def _():
            message(M_Q_VIA, pair).start()
            message(M_G_VIA, pair).start()

    def pass_q_on(pair):
        @pl.when((pair < pairs) & passes_q_on(pair))
        def _():
            message(M_Q_VIA, pair).wait_recv()
            message(M_Q_ON, pair).start()
            message(M_G_VIA, pair).wait_recv()
            message(M_G_ON, pair).start()

    def pass_dq_on(pair):
        @pl.when(passes_dq_on(pair))
        def _():
            message(M_DQ_VIA, pair).wait_recv()
            message(M_DQ_ON, pair).start()

    send_chunk(0)
    for pair in range(pairs):
        rest[pair] = rest_rows[2 * pair : 2 * pair + 2]
        dot[pair] = dot_rows[2 * pair : 2 * pair + 2]

    @pl.when(has_behind)
    def _():
        message(M_DOT, 0).start()

    cap = acts.shape[2]
    full = [jnp.where(counts[group, slot] == cap, 1.0, 0.0) for slot in range(slots)]
    row_ids = lax.broadcasted_iota(jnp.int32, (1, half_rows), 1)

    def mark(expert_id, index, value):
        lanes[expert_id, 0:1, index * half_rows : (index + 1) * half_rows] = value

    for k_ in range(own_slots):
        for slot in range(own_slots):
            live = row_ids < counts[group, slot]
            mark(k_, slot, jnp.where(live, 1.0, 0.0) if slot == k_ else jnp.zeros(row_ids.shape))
        mark(k_, slots, jnp.zeros(row_ids.shape))
        mark(k_, slots + 1, jnp.zeros(row_ids.shape) + full[k_])
        for r in range(replicas):
            source = lax.rem(group + groups - 1 - r, groups)
            held = counts[source, own_slots + r]
            wanted = jnp.where(lists[source, r] == k_, 1.0, 0.0)
            mark(k_, own_slots + r, jnp.where(row_ids < held, wanted, 0.0))
            whole = jnp.where(held == cap, wanted, 0.0)
            mark(k_, slots + 2 + r, jnp.zeros(row_ids.shape) + whole)

    lane = lax.broadcasted_iota(jnp.int32, (1, 128), 1)
    low_lanes = jnp.where(lane < 64, 1.0, 0.0).astype(jnp.bfloat16)
    high_lanes = jnp.where(lane < 64, 0.0, 1.0).astype(jnp.bfloat16)
    is_low = lane < 64

    def pick_second(pair):
        @pl.when(core_zero)
        def _():
            q2[...] = qn[:, qk_cols(pair)]
            g2[...] = gn[:, v_cols(pair)]

        @pl.when(jnp.logical_not(core_zero))
        def _():
            q2[...] = q[:, qk_cols(pair)]
            g2[...] = g[:, v_cols(pair)]

    def v_head(ref, pair, head):
        return ref[:, pl.ds(pl.multiple_of(pair * PAIR_V + head * V_DIM, 128), V_DIM)]

    def first_phase(pair):
        @pl.when(pair == 0)
        def _():
            for load in loads[:4]:
                load.wait()

        slot = lax.rem(pair, 3)
        start = pl.multiple_of(pair * PAIR_QK, 128)
        k_own = heads_of(k, start, low_lanes, high_lanes)
        q_own = heads_of(q, start, low_lanes, high_lanes)
        key_pos = lax.broadcasted_iota(jnp.int32, (rows, rows), 0)
        query_pos = lax.broadcasted_iota(jnp.int32, (rows, rows), 1)
        allowed = key_pos <= query_pos
        dot_own = dot[pair]

        def keep(head, task, prob, grad):
            pring[slot, head * 3 + task] = prob.astype(jnp.bfloat16)
            dring[slot, head * 3 + task] = grad.astype(jnp.bfloat16)

        tops_own, sums_own = [], []
        for head in range(2):
            s3 = rows_by_rows(k_own[head], q_own[head]) * SCALE
            s3 = jnp.where(allowed, s3, -1e30)
            m3 = jnp.max(s3, 0, keepdims=True)
            p3 = jnp.exp(s3 - m3)
            g3 = rows_by_rows(v_head(v, pair, head), v_head(g, pair, head))
            keep(head, 2, p3, p3 * (g3 - dot_own[head : head + 1]))
            tops_own.append(m3)
            sums_own.append(jnp.sum(p3, 0, keepdims=True))

        message(M_K, pair).wait_recv()
        message(M_V, pair).wait_recv()

        @pl.when(has_ahead)
        def _():
            message(M_Q, pair).wait_recv()
            message(M_G, pair).wait_recv()

        @pl.when((pair == 0) & has_ahead)
        def _():
            message(M_DOT, 0).wait_recv()

        pl.when(pair == 0)(lambda: send_chunk(1))
        pl.when(pair + 2 < pairs)(lambda: send_chunk(pair + 2))

        pick_second(pair)
        k_oth = heads_of(ko, start, low_lanes, high_lanes)
        q_new = heads_of(qn, start, low_lanes, high_lanes)
        q_sec = heads_of(q2, 0, low_lanes, high_lanes)
        dot_new = dotn[pair]
        dot_sec = c0 * dot_new + c1 * dot_own
        lses, tops_sec, sums_sec, dq_heads = [], [], [], []
        for head in range(2):
            s1 = rows_by_rows(k_own[head], q_new[head]) * SCALE
            s2 = rows_by_rows(k_oth[head], q_sec[head]) * SCALE
            m1 = jnp.max(s1, 0, keepdims=True)
            m2 = jnp.max(s2, 0, keepdims=True)
            top_new = jnp.maximum(m1, jnp.where(core_zero, m2, LOW))
            top_sec = jnp.where(core_zero, top_new, m2)
            p1 = jnp.exp(s1 - top_new)
            p2 = jnp.exp(s2 - top_sec)
            z1 = jnp.sum(p1, 0, keepdims=True)
            z2 = jnp.sum(p2, 0, keepdims=True)
            sum_new = z1 + c0 * z2
            lses.append(top_new + jnp.log(sum_new))
            inverse = 1.0 / sum_new
            p1 = p1 * inverse
            p2 = p2 * jnp.where(core_zero, inverse, 1.0)
            tops_sec.append(jnp.where(core_zero, LOW, m2))
            sums_sec.append(z2)
            g1 = rows_by_rows(v_head(v, pair, head), v_head(gn, pair, head))
            g2_ = rows_by_rows(v_head(vo, pair, head), g2[:, head * V_DIM : (head + 1) * V_DIM])
            d1 = (p1 * (g1 - dot_new[head : head + 1])).astype(jnp.bfloat16)
            d2 = (p2 * (g2_ - dot_sec[head : head + 1])).astype(jnp.bfloat16)
            keep(head, 0, p1, d1)
            keep(head, 1, p2, d2)
            dq_heads.append(columns_by_rows(d1, k_own[head]) + c0 * columns_by_rows(d2, k_oth[head]))
        mss[pair] = jnp.concatenate(lses, 0)
        own_ms[pair] = jnp.concatenate(tops_own + sums_own + tops_sec + sums_sec, 0)
        store_pair(dqs, start, *dq_heads)
        via = sends_dq_via(pair)

        @pl.when(has_ahead)
        def _():
            message(M_MS, pair).start()

        @pl.when(has_ahead & jnp.logical_not(via))
        def _():
            message(M_DQ, pair).start()

        @pl.when(via)
        def _():
            message(M_DQ_VIA, pair).start()

        pl.when(pair >= 1)(lambda: pass_q_on(pair + 1))

    def second_phase(pair):
        pass_dq_on(pair)

        @pl.when(has_behind)
        def _():
            message(M_MS, pair).wait_recv()

        theirs = msr[pair]
        ours = own_ms[pair]
        away = rest[pair]
        top_far = jnp.where(has_behind, theirs, LOW)
        top = jnp.maximum(jnp.maximum(ours[0:2], ours[4:6]), jnp.maximum(away, top_far))
        whole = (
            ours[2:4] * jnp.exp(ours[0:2] - top)
            + ours[6:8] * jnp.exp(ours[4:6] - top)
            + jnp.exp(away - top)
            + jnp.exp(top_far - top)
        )
        total_lse = top + jnp.log(whole)
        ws[pair] = jnp.exp(top_far - total_lse)
        zero = jnp.zeros((4, rows), jnp.float32)
        fo[pair] = jnp.concatenate(
            [jnp.exp(ours[0:2] - total_lse), jnp.exp(ours[4:6] - total_lse), zero], 0
        )

        @pl.when(has_behind)
        def _():
            message(M_W, pair).start()

    def third_phase(pair):
        slot = lax.rem(pair, 3)
        start = pl.multiple_of(pair * PAIR_QK, 128)
        k_own = heads_of(k, start, low_lanes, high_lanes)
        q_own = heads_of(q, start, low_lanes, high_lanes)
        own_weight = fo[pair]
        far_weight = ws[pair]
        eye = lax.broadcasted_iota(jnp.int32, (rows, rows), 0) == lax.broadcasted_iota(
            jnp.int32, (rows, rows), 1
        )
        acc = lax.rem(pair, 2)

        def scaled(head, task, weight):
            prob = pring[slot, head * 3 + task].astype(jnp.float32) * weight
            grad = dring[slot, head * 3 + task].astype(jnp.float32) * (weight * SCALE)
            return prob.astype(jnp.bfloat16), grad.astype(jnp.bfloat16)

        dq_own, dk_own, columns = [], [], []
        for head in range(2):
            prob, grad = scaled(head, 2, own_weight[head : head + 1])
            accv[acc, :, head * V_DIM : (head + 1) * V_DIM] = plain(prob, v_head(g, pair, head))
            dk_own.append(plain(grad, q_own[head]))
            dq_own.append(columns_by_rows(grad, k_own[head]))
            columns.append(
                jnp.sum(jnp.where(eye, far_weight[head : head + 1] * SCALE, 0.0), 1, keepdims=True)
            )
        store_pair(acck.at[acc], 0, *dk_own)

        @pl.when(has_ahead)
        def _():
            message(M_W, pair).wait_recv()

        pick_second(pair)
        k_oth = heads_of(ko, start, low_lanes, high_lanes)
        q_new = heads_of(qn, start, low_lanes, high_lanes)
        q_sec = heads_of(q2, 0, low_lanes, high_lanes)
        new_weight = wr[pair]
        sec_weight = c0 * new_weight + c1 * own_weight[2:4]
        dq_heads, dk_heads, dko_heads = [], [], []
        for head in range(2):
            prob, grad = scaled(head, 1, sec_weight[head : head + 1])
            dvs[:, pl.ds(pl.multiple_of(pair * PAIR_V + head * V_DIM, 128), V_DIM)] = plain(
                prob, g2[:, head * V_DIM : (head + 1) * V_DIM]
            ).astype(jnp.bfloat16)
            dko_heads.append(plain(grad, q_sec[head]))
            dq_heads.append(dq_own[head] + c1 * columns_by_rows(grad, k_oth[head]))
        store_pair(dks, start, *dko_heads)
        message(M_DV, pair).start()
        message(M_DK, pair).start()
        for head in range(2):
            prob, grad = scaled(head, 0, new_weight[head : head + 1])
            accv[acc, :, head * V_DIM : (head + 1) * V_DIM] += plain(prob, v_head(gn, pair, head))
            dk_heads.append(plain(grad, q_new[head]))
        even, odd = dk_heads
        acck[acc, :, :128] += even[:, :128]
        acck[acc, :, 128:256] += even[:, 128:] + odd[:, :128]
        acck[acc, :, 256:] += odd[:, 128:]

        @pl.when(has_behind)
        def _():
            message(M_DQ, pair).wait_recv()

        first = pl.ds(start, 128)
        middle = pl.ds(pl.multiple_of(start + 128, 128), 128)
        last = pl.ds(pl.multiple_of(start + 256, 128), 128)
        even, odd = dq_heads
        dq[:, first] = (even[:, :128] + columns[0] * dq[:, first].astype(jnp.float32)).astype(dq.dtype)
        dq[:, middle] = (
            even[:, 128:]
            + odd[:, :128]
            + jnp.where(is_low, columns[0], columns[1]) * dq[:, middle].astype(jnp.float32)
        ).astype(dq.dtype)
        dq[:, last] = (odd[:, 128:] + columns[1] * dq[:, last].astype(jnp.float32)).astype(dq.dtype)

    def fourth_phase(pair):
        message(M_DK, pair).wait_recv()
        message(M_DV, pair).wait_recv()
        acc = lax.rem(pair, 2)
        dk[:, qk_cols(pair)] = (acck[acc] + dk[:, qk_cols(pair)].astype(jnp.float32)).astype(dk.dtype)
        dv[:, v_cols(pair)] = (accv[acc] + dv[:, v_cols(pair)].astype(jnp.float32)).astype(dv.dtype)

    def step(at, carry):
        for lag, phase in enumerate((first_phase, second_phase, third_phase, fourth_phase)):
            @pl.when((at >= lag) & (at < pairs + lag))
            def _(lag=lag, phase=phase):
                phase(at - lag)

        return carry

    def first_stage():
        for load in loads[4:]:
            load.wait()
        full_high, full_piece = 0.0, 0.0
        for slot in range(slots):
            full_high = full_high + full[slot] * acts[slot, :, half_rows:].astype(jnp.float32)
            full_piece = full_piece + full[slot] * grads[slot].astype(jnp.float32)
        high[...] = full_high.astype(high.dtype)
        is_upper = jnp.where(upper == 1, 1.0, 0.0)
        for slot in range(slots):
            mixed = is_upper * full_piece + (1.0 - is_upper) * grads[slot].astype(jnp.float32)
            pieces[slot] = mixed.astype(pieces.dtype)
        for each in own_copies():
            each.start()
        begin(E_ROWS, E_HIGH)

    def second_stage():
        for each in own_copies():
            each.wait()
        arrived(E_ROWS, E_HIGH)
        begin(E_LEVEL, E_SPREAD)

    def third_stage():
        arrived(E_LEVEL)

    def fourth_stage():
        arrived(E_AROUND)
        begin(E_OTHER)

    def fifth_stage():
        arrived(E_OTHER, E_ACTS, E_SPREAD)

    stages = {0: first_stage, 2: second_stage, 3: third_stage, 10: fourth_stage, 11: fifth_stage}
    spread_out = [(1 + at, each) for at, each in enumerate(expert_messages(E_ACTS))]
    spread_out += [(3 + at, each) for at, each in enumerate(expert_messages(E_AROUND))]
    products = own_slots * parts
    product_at, at_once = 11, 2

    def step_with_experts(at, carry):
        step(at, carry)
        for when, stage in stages.items():
            pl.when(at == when)(stage)

        for when, each in spread_out:
            pl.when(at == when)(each.start)

        @pl.when((at >= product_at) & (at < product_at + products // at_once))
        def _():
            for part in range(at_once):
                expert_step((at - product_at) * at_once + part)

        return carry

    lax.fori_loop(0, max(pairs + 3, product_at + products // at_once), step_with_experts, 0)
    left_behind(E_ACTS, E_ROWS, E_HIGH, E_SPREAD, E_LEVEL, E_AROUND, E_OTHER)

    @pl.when(has_behind)
    def _():
        message(M_DOT, 0).wait_send()

    def drain(pair, carry):
        def settle(condition, *kinds):
            @pl.when(condition)
            def _():
                for kind in kinds:
                    message(kind, pair).wait_send()

        settle(pair >= 0, M_K, M_V, M_DK, M_DV)
        settle(has_behind, M_W)
        settle(has_ahead, M_MS)
        settle(has_behind & jnp.logical_not(sends_q_via(pair)), M_Q, M_G)
        settle(sends_q_via(pair), M_Q_VIA, M_G_VIA)
        settle(passes_q_on(pair), M_Q_ON, M_G_ON)
        settle(has_ahead & jnp.logical_not(sends_dq_via(pair)), M_DQ)
        settle(sends_dq_via(pair), M_DQ_VIA)
        settle(passes_dq_on(pair), M_DQ_ON)
        return carry

    lax.fori_loop(0, pairs, drain, 0)


def gradients(queries, key_states, value_states, out_grad, lse_rest, out_dot, acts, grads, counts, lists):
    rows, qk = queries.shape
    vv = value_states.shape[1]
    pairs = qk // PAIR_QK
    slots, features, cap = acts.shape
    hidden = grads.shape[2]
    experts = slots - lists.shape[1]
    groups = lax.axis_size("grp")
    columns = lax.axis_size("ctx") // 4
    _, sems = first_sems(slots, groups - 1, groups // 2, columns)
    half = jnp.bfloat16
    vmem = pl.BlockSpec(memory_space=pltpu.VMEM)
    anywhere = pl.BlockSpec(memory_space=pl.ANY)
    small = pltpu.VMEM((pairs, 8, rows), jnp.float32)
    two_rows = pltpu.VMEM((pairs, 2, rows), jnp.float32)
    wide = pltpu.VMEM((rows, qk), half)
    narrow = pltpu.VMEM((rows, vv), half)
    return pl.pallas_call(
        functools.partial(attention_kernel, pairs),
        out_shape=[
            pltpu.VMEM((rows, qk), half),
            pltpu.VMEM((rows, qk), half),
            pltpu.VMEM((rows, vv), half),
            pltpu.VMEM((experts, features, hidden), jnp.float32),
            jax.ShapeDtypeStruct((rows, qk), half),
            jax.ShapeDtypeStruct((rows, vv), half),
            jax.ShapeDtypeStruct((rows, qk), half),
        ],
        in_specs=[anywhere] * 4 + [vmem] * 2 + [anywhere] * 2 + [pl.BlockSpec(memory_space=pltpu.SMEM)] * 2,
        out_specs=[vmem] * 4 + [anywhere] * 3,
        scratch_shapes=[
            wide,
            narrow,
            pltpu.VMEM((pairs, 2, rows), jnp.float32),
            wide,
            narrow,
            wide,
            wide,
            narrow,
            two_rows,
            two_rows,
            small,
            two_rows,
            two_rows,
            small,
            pltpu.VMEM((3, 6, rows, rows), half),
            pltpu.VMEM((3, 6, rows, rows), half),
            pltpu.VMEM((2, rows, PAIR_QK), jnp.float32),
            pltpu.VMEM((2, rows, PAIR_V), jnp.float32),
            pltpu.VMEM((rows, PAIR_QK), half),
            pltpu.VMEM((rows, PAIR_V), half),
            pltpu.VMEM((features, slots * cap), half),
            pltpu.VMEM((2 * slots, cap // 2, hidden), half),
            pltpu.VMEM((pairs, 2, rows), jnp.float32),
            pltpu.VMEM((pairs, 2, rows), jnp.float32),
            pltpu.VMEM((features, cap // 2), half),
            pltpu.VMEM(grads.shape, half),
            pltpu.VMEM((experts, 8, slots * cap), jnp.float32),
            wide,
            wide,
            narrow,
            narrow,
            pltpu.VMEM(acts.shape, half),
            pltpu.VMEM(grads.shape, half),
            pltpu.SemaphoreType.DMA((6,)),
            pltpu.SemaphoreType.DMA((KINDS, pairs)),
            pltpu.SemaphoreType.DMA((KINDS, pairs)),
            pltpu.SemaphoreType.DMA((sems,)),
            pltpu.SemaphoreType.DMA((sems,)),
            pltpu.SemaphoreType.DMA((2 * experts + 1,)),
        ],
        compiler_params=pltpu.CompilerParams(
            collective_id=0, has_side_effects=True, vmem_limit_bytes=LIMIT_MIB * 2**20
        ),
        name="window_grads",
    )(
        queries,
        key_states,
        value_states,
        out_grad,
        lse_rest,
        out_dot,
        acts,
        grads,
        counts,
        lists,
    )[:4]


def out_kernel(count, *refs):
    copies = [
        pltpu.make_async_copy(refs[at], refs[count + at].at[0], refs[2 * count].at[at])
        for at in range(count)
    ]
    for copy in copies:
        copy.start()
    for copy in copies:
        copy.wait()


def written_out(found):
    anywhere = pl.BlockSpec(memory_space=pl.ANY)
    count = len(found)
    return pl.pallas_call(
        functools.partial(out_kernel, count),
        out_shape=[jax.ShapeDtypeStruct((1, *each.shape), each.dtype) for each in found],
        in_specs=[pl.BlockSpec(memory_space=pltpu.VMEM)] * count,
        out_specs=[anywhere] * count,
        scratch_shapes=[pltpu.SemaphoreType.DMA((count,))],
        compiler_params=pltpu.CompilerParams(vmem_limit_bytes=24 * 2**20),
        name="written_out",
    )(*found)


def local(queries, key_states, value_states, out_grad, lse_rest, out_dot, moe_acts, moe_grads, counts, replica_list):
    found = gradients(
        queries[0],
        key_states[0],
        value_states[0],
        out_grad[0],
        lse_rest[0],
        out_dot[0],
        moe_acts[0],
        moe_grads[0],
        counts,
        replica_list,
    )
    return tuple(written_out(found))


def solution(mesh):
    return jax.shard_map(
        local,
        mesh=mesh,
        in_specs=(
            P("grp", "ctx", None),
            P("grp", "ctx", None),
            P("grp", "ctx", None),
            P("grp", "ctx", None),
            P("grp", None, "ctx"),
            P("grp", None, "ctx"),
            P("grp", None, "ctx", None),
            P("grp", None, "ctx", None),
            P(),
            P(),
        ),
        out_specs=(
            P("grp", "ctx", None),
            P("grp", "ctx", None),
            P("grp", "ctx", None),
            P("grp", None, "ctx", None),
        ),
        check_vma=False,
    )
```

```python
import functools

import jax
import jax.numpy as jnp
from jax import lax
from jax.experimental import pallas as pl
from jax.experimental.pallas import tpu as pltpu
from jax.sharding import PartitionSpec as P

QK_DIM = 192
V_DIM = 128
PAIR_QK = 2 * QK_DIM
PAIR_V = 2 * V_DIM
SCALE = QK_DIM**-0.5
LOW = -1e38
MESH = pl.DeviceIdType.MESH

M_Q, M_G, M_K, M_V, M_DQ, M_MS, M_W, M_DK, M_DV, M_DOT = range(10)
M_Q_VIA, M_G_VIA, M_DQ_VIA, M_Q_ON, M_G_ON, M_DQ_ON = range(10, 16)
KINDS = 16
LIMIT_MIB = 48
DRAIN_LAG = 5

E_ACTS, E_ROWS, E_HIGH, E_SPREAD, E_LEVEL, E_AROUND, E_OTHER = range(7)


def first_sems(slots, replicas, owners, columns):
    sizes = {
        E_ACTS: replicas,
        E_ROWS: replicas,
        E_HIGH: 1,
        E_SPREAD: 2 * (owners - 1),
        E_LEVEL: slots,
        E_AROUND: 2 * (columns - 1),
        E_OTHER: 2 * columns,
    }
    starts, total = {}, 0
    for kind, size in sizes.items():
        starts[kind] = total
        total += size
    return starts, total


def rows_by_rows(a, b):
    return lax.dot_general(a, b, (((1,), (1,)), ((), ())), preferred_element_type=jnp.float32)


def plain(a, b):
    return lax.dot_general(a, b, (((1,), (0,)), ((), ())), preferred_element_type=jnp.float32)


def columns_by_rows(a, b):
    return lax.dot_general(a, b, (((0,), (0,)), ((), ())), preferred_element_type=jnp.float32)


def heads_of(ref, start, low_lanes, high_lanes):
    first = ref[:, pl.ds(start, 128)]
    middle = ref[:, pl.ds(pl.multiple_of(start + 128, 128), 128)]
    last = ref[:, pl.ds(pl.multiple_of(start + 256, 128), 128)]
    return (
        jnp.concatenate([first, middle * low_lanes], 1),
        jnp.concatenate([middle * high_lanes, last], 1),
    )


def store_pair(ref, index, even, odd):
    start = index
    kind = ref.dtype
    ref[:, pl.ds(start, 128)] = even[:, :128].astype(kind)
    ref[:, pl.ds(pl.multiple_of(start + 128, 128), 128)] = (even[:, 128:] + odd[:, :128]).astype(kind)
    ref[:, pl.ds(pl.multiple_of(start + 256, 128), 128)] = odd[:, 128:].astype(kind)


def attention_kernel(
    pairs,
    q_in,
    k_in,
    v_in,
    g_in,
    rest_rows,
    dot_rows,
    acts_in,
    grads_in,
    counts,
    lists,
    dq,
    dk,
    dv,
    expert,
    q_via,
    g_via,
    dq_via,
    qn,
    gn,
    dotn,
    ko,
    vo,
    dqs,
    dks,
    dvs,
    mss,
    msr,
    own_ms,
    ws,
    wr,
    fo,
    pring,
    dring,
    acck,
    accv,
    q2,
    g2,
    left,
    right,
    rest,
    dot,
    high,
    pieces,
    lanes,
    q,
    k,
    v,
    g,
    acts,
    grads,
    in_sem,
    send,
    recv,
    esend,
    erecv,
    own_sem,
):
    rows = q.shape[0]
    loads = [
        pltpu.make_async_copy(source, held, in_sem.at[at])
        for at, (source, held) in enumerate(
            ((k_in, k), (v_in, v), (q_in, q), (g_in, g), (acts_in, acts), (grads_in, grads))
        )
    ]
    for load in loads:
        load.start()
    me = lax.axis_index("ctx")
    total = lax.axis_size("ctx")
    core = lax.rem(me, 2)
    ahead_chip = lax.rem(me + 2, total)
    behind_chip = lax.rem(me + total - 2, total)
    other = me + 1 - 2 * core
    core_zero = core == 0
    c0 = jnp.where(core_zero, 1.0, 0.0).astype(jnp.float32)
    c1 = 1.0 - c0
    has_behind = me >= 2
    has_ahead = me < total - 2
    column = lax.div(me, 4)
    low_level = lax.rem(me, 4) < 2
    level = me + 2 - 4 * lax.div(lax.rem(me, 4), 2)
    last_column = total // 4 - 1

    def q_detour(boundary, pair):
        return (lax.rem(pair, 4) <= boundary) & (pair >= 2)

    def dq_detour(boundary, pair):
        return lax.rem(pair, 4) < 3 - boundary

    def sends_q_via(pair):
        return low_level & (column >= 1) & q_detour(column - 1, pair)

    def passes_q_on(pair):
        return jnp.logical_not(low_level) & (column >= 1) & q_detour(column - 1, pair)

    def sends_dq_via(pair):
        return jnp.logical_not(low_level) & (column < last_column) & dq_detour(column, pair)

    def passes_dq_on(pair):
        return low_level & (column < last_column) & dq_detour(column, pair)

    def qk_cols(pair):
        return pl.ds(pl.multiple_of(pair * PAIR_QK, 128), PAIR_QK)

    def v_cols(pair):
        return pl.ds(pl.multiple_of(pair * PAIR_V, 128), PAIR_V)

    def message(kind, pair):
        src, dst, target = {
            M_Q: lambda: (q_in.at[:, qk_cols(pair)], qn.at[:, qk_cols(pair)], behind_chip),
            M_G: lambda: (g_in.at[:, v_cols(pair)], gn.at[:, v_cols(pair)], behind_chip),
            M_K: lambda: (k_in.at[:, qk_cols(pair)], ko.at[:, qk_cols(pair)], other),
            M_V: lambda: (v_in.at[:, v_cols(pair)], vo.at[:, v_cols(pair)], other),
            M_DQ: lambda: (dqs.at[:, qk_cols(pair)], dq.at[:, qk_cols(pair)], ahead_chip),
            M_MS: lambda: (mss.at[pair], msr.at[pair], ahead_chip),
            M_W: lambda: (ws.at[pair], wr.at[pair], behind_chip),
            M_DK: lambda: (dks.at[:, qk_cols(pair)], dk.at[:, qk_cols(pair)], other),
            M_DV: lambda: (dvs.at[:, v_cols(pair)], dv.at[:, v_cols(pair)], other),
            M_DOT: lambda: (dot, dotn, behind_chip),
            M_Q_VIA: lambda: (q_in.at[:, qk_cols(pair)], q_via.at[:, qk_cols(pair)], level),
            M_G_VIA: lambda: (g_in.at[:, v_cols(pair)], g_via.at[:, v_cols(pair)], level),
            M_DQ_VIA: lambda: (dqs.at[:, qk_cols(pair)], dq_via.at[:, qk_cols(pair)], level),
            M_Q_ON: lambda: (
                q_via.at[:, qk_cols(pair)],
                qn.at[:, qk_cols(pair)],
                lax.rem(me + total - 4, total),
            ),
            M_G_ON: lambda: (
                g_via.at[:, v_cols(pair)],
                gn.at[:, v_cols(pair)],
                lax.rem(me + total - 4, total),
            ),
            M_DQ_ON: lambda: (
                dq_via.at[:, qk_cols(pair)],
                dq.at[:, qk_cols(pair)],
                lax.rem(me + 4, total),
            ),
        }[kind]()
        lands_as = {M_Q_ON: M_Q, M_G_ON: M_G, M_DQ_ON: M_DQ}.get(kind, kind)
        return pltpu.make_async_remote_copy(
            src_ref=src,
            dst_ref=dst,
            send_sem=send.at[kind, pair],
            recv_sem=recv.at[lands_as, pair],
            device_id={"ctx": target},
            device_id_type=MESH,
        )

    group = lax.axis_index("grp")
    groups = lax.axis_size("grp")
    slots = acts.shape[0]
    replicas = groups - 1
    own_slots = slots - replicas
    half_rows = left.shape[1] // (2 * slots)
    piece = pieces.shape[1]
    columns = total // 4
    owners = groups // 2
    upper = (me >= total // 2).astype(jnp.int32)
    twin = group + 1 - 2 * lax.rem(group, 2)
    starts, _ = first_sems(slots, replicas, owners, columns)

    def unit(device):
        return right.at[
            pl.ds(slots * (device >= total // 2).astype(jnp.int32), slots),
            pl.ds(pl.multiple_of(lax.rem(device, total // 2) * piece, piece), piece),
        ]

    def piece_at(device, index):
        return right.at[
            slots * (device >= total // 2).astype(jnp.int32) + index,
            pl.ds(pl.multiple_of(lax.rem(device, total // 2) * piece, piece), piece),
        ]

    def block(index):
        return left.at[:, pl.ds(pl.multiple_of(index * half_rows, 128), half_rows)]

    def expert_message(kind, at, src, dst, target):
        sem = starts[kind] + at
        return pltpu.make_async_remote_copy(
            src_ref=src,
            dst_ref=dst,
            send_sem=esend.at[sem],
            recv_sem=erecv.at[sem],
            device_id=target,
            device_id_type=MESH,
        )

    def in_group(device):
        return {"ctx": device, "grp": group}

    def owner(index):
        return {"ctx": me, "grp": index}

    def expert_messages(kind):
        if kind == E_ACTS:
            return [
                expert_message(
                    kind,
                    r,
                    acts.at[own_slots + r, :, pl.ds(0, half_rows)],
                    block(own_slots + r),
                    owner(lax.rem(group + r + 1, groups)),
                )
                for r in range(replicas)
            ]
        if kind == E_ROWS:
            return [
                expert_message(
                    kind,
                    r,
                    pieces.at[own_slots + r],
                    piece_at(me, own_slots + r),
                    {"ctx": me if r % 2 else level, "grp": lax.rem(group + r + 1, groups)},
                )
                for r in range(replicas)
            ]
        if kind == E_HIGH:
            place = lax.rem(twin - group + groups, groups)
            return [expert_message(kind, 0, high, block(slots + 1 + place), owner(twin))]
        if kind == E_SPREAD:
            place = lax.rem(group - twin + groups, groups)
            found = []
            for m in range(1, owners):
                to = owner(lax.rem(group + 2 * m, groups))
                found.append(
                    expert_message(kind, 2 * m - 2, high, block(slots + 1 + 2 * m), to)
                )
                found.append(
                    expert_message(
                        kind,
                        2 * m - 1,
                        block(slots + 1 + place),
                        block(slots + 1 + lax.rem(place + 2 * m, groups)),
                        to,
                    )
                )
            return found
        if kind == E_LEVEL:
            found = []
            for index in range(slots):
                away = index >= own_slots and (index - own_slots) % 2 == 0
                held = piece_at(level if away else me, index)
                found.append(expert_message(kind, index, held, held, in_group(level)))
            return found
        if kind == E_AROUND:
            return [
                expert_message(
                    kind,
                    2 * m - 2 + which,
                    unit(device),
                    unit(device),
                    in_group(lax.rem(me + 4 * m, total)),
                )
                for m in range(1, columns)
                for which, device in enumerate((me, level))
            ]
        return [
            expert_message(kind, m, unit(2 * m + core), unit(2 * m + core), in_group(other))
            for m in range(2 * columns)
        ]

    def own_copies():
        found = [
            pltpu.make_async_copy(
                acts.at[slot, :, pl.ds(0, half_rows)], block(slot), own_sem.at[slot]
            )
            for slot in range(own_slots)
        ]
        found.append(pltpu.make_async_copy(high, block(slots + 1), own_sem.at[own_slots]))
        place = pl.ds(pl.multiple_of(lax.rem(me, total // 2) * piece, piece), piece)
        for slot in range(own_slots):
            found.append(
                pltpu.make_async_copy(
                    pieces.at[slot],
                    right.at[slots * upper + slot, place],
                    own_sem.at[own_slots + 1 + slot],
                )
            )
        return found

    def begin(*kinds):
        for kind in kinds:
            for each in expert_messages(kind):
                each.start()

    def arrived(*kinds):
        for kind in kinds:
            for each in expert_messages(kind):
                each.wait_recv()

    def left_behind(*kinds):
        for kind in kinds:
            for each in expert_messages(kind):
                each.wait_send()

    width = min(expert.shape[2], 256)
    parts = expert.shape[2] // width

    def expert_step(index):
        mask = lanes[lax.div(index, parts)][0:1].astype(left.dtype)
        cols = pl.ds(pl.multiple_of(lax.rem(index, parts) * width, 128), width)
        result = None
        for low, count in ((0, slots), (slots + 1, slots - 1)):
            here = slice(low * half_rows, (low + count) * half_rows)
            a = left[:, here] * mask[:, here]
            b = right[low : low + count, :, cols].reshape(count * half_rows, width)
            product = plain(a, b)
            result = product if result is None else result + product
        expert[lax.div(index, parts), :, cols] = result

    barrier = pltpu.get_barrier_semaphore()
    partners = [in_group(partner) for partner in (behind_chip, ahead_chip, other, level)]
    partners += [in_group(lax.rem(me + 4 * m, total)) for m in range(1, columns)]
    partners += [owner(lax.rem(group + m, groups)) for m in range(1, groups)]
    partners += [{"ctx": level, "grp": lax.rem(group + m, groups)} for m in range(1, groups, 2)]
    for partner in partners:
        pl.semaphore_signal(barrier, inc=1, device_id=partner, device_id_type=MESH)
    pl.semaphore_wait(barrier, len(partners))

    @pl.when(jnp.logical_not(has_ahead))
    def _():
        qn[...] = jnp.zeros_like(qn)
        gn[...] = jnp.zeros_like(gn)
        dotn[...] = jnp.zeros_like(dotn)
        wr[...] = jnp.zeros_like(wr)

    @pl.when(jnp.logical_not(has_behind))
    def _():
        msr[...] = jnp.zeros_like(msr)
        dq[...] = jnp.zeros_like(dq)

    def send_chunk(pair):
        message(M_K, pair).start()
        message(M_V, pair).start()
        via = sends_q_via(pair)

        @pl.when(has_behind & jnp.logical_not(via))
        def _():
            message(M_Q, pair).start()
            message(M_G, pair).start()

        @pl.when(via)
        def _():
            message(M_Q_VIA, pair).start()
            message(M_G_VIA, pair).start()

    def pass_q_on(pair):
        @pl.when((pair < pairs) & passes_q_on(pair))
        def _():
            message(M_Q_VIA, pair).wait_recv()
            message(M_Q_ON, pair).start()
            message(M_G_VIA, pair).wait_recv()
            message(M_G_ON, pair).start()

    def pass_dq_on(pair):
        @pl.when(passes_dq_on(pair))
        def _():
            message(M_DQ_VIA, pair).wait_recv()
            message(M_DQ_ON, pair).start()

    send_chunk(0)
    for pair in range(pairs):
        rest[pair] = rest_rows[2 * pair : 2 * pair + 2]
        dot[pair] = dot_rows[2 * pair : 2 * pair + 2]

    @pl.when(has_behind)
    def _():
        message(M_DOT, 0).start()

    cap = acts.shape[2]
    full = [jnp.where(counts[group, slot] == cap, 1.0, 0.0) for slot in range(slots)]
    row_ids = lax.broadcasted_iota(jnp.int32, (1, half_rows), 1)

    def mark(expert_id, index, value):
        lanes[expert_id, 0:1, index * half_rows : (index + 1) * half_rows] = value

    for k_ in range(own_slots):
        for slot in range(own_slots):
            live = row_ids < counts[group, slot]
            mark(k_, slot, jnp.where(live, 1.0, 0.0) if slot == k_ else jnp.zeros(row_ids.shape))
        mark(k_, slots, jnp.zeros(row_ids.shape))
        mark(k_, slots + 1, jnp.zeros(row_ids.shape) + full[k_])
        for r in range(replicas):
            source = lax.rem(group + groups - 1 - r, groups)
            held = counts[source, own_slots + r]
            wanted = jnp.where(lists[source, r] == k_, 1.0, 0.0)
            mark(k_, own_slots + r, jnp.where(row_ids < held, wanted, 0.0))
            whole = jnp.where(held == cap, wanted, 0.0)
            mark(k_, slots + 2 + r, jnp.zeros(row_ids.shape) + whole)

    lane = lax.broadcasted_iota(jnp.int32, (1, 128), 1)
    low_lanes = jnp.where(lane < 64, 1.0, 0.0).astype(jnp.bfloat16)
    high_lanes = jnp.where(lane < 64, 0.0, 1.0).astype(jnp.bfloat16)
    is_low = lane < 64

    def pick_second(pair):
        @pl.when(core_zero)
        def _():
            q2[...] = qn[:, qk_cols(pair)]
            g2[...] = gn[:, v_cols(pair)]

        @pl.when(jnp.logical_not(core_zero))
        def _():
            q2[...] = q[:, qk_cols(pair)]
            g2[...] = g[:, v_cols(pair)]

    def v_head(ref, pair, head):
        return ref[:, pl.ds(pl.multiple_of(pair * PAIR_V + head * V_DIM, 128), V_DIM)]

    def first_phase(pair):
        @pl.when(pair == 0)
        def _():
            for load in loads[:4]:
                load.wait()

        slot = lax.rem(pair, 3)
        start = pl.multiple_of(pair * PAIR_QK, 128)
        k_own = heads_of(k, start, low_lanes, high_lanes)
        q_own = heads_of(q, start, low_lanes, high_lanes)
        key_pos = lax.broadcasted_iota(jnp.int32, (rows, rows), 0)
        query_pos = lax.broadcasted_iota(jnp.int32, (rows, rows), 1)
        allowed = key_pos <= query_pos
        dot_own = dot[pair]

        def keep(head, task, prob, grad):
            pring[slot, head * 3 + task] = prob.astype(jnp.bfloat16)
            dring[slot, head * 3 + task] = grad.astype(jnp.bfloat16)

        tops_own, sums_own = [], []
        for head in range(2):
            s3 = rows_by_rows(k_own[head], q_own[head]) * SCALE
            s3 = jnp.where(allowed, s3, -1e30)
            m3 = jnp.max(s3, 0, keepdims=True)
            p3 = jnp.exp(s3 - m3)
            g3 = rows_by_rows(v_head(v, pair, head), v_head(g, pair, head))
            keep(head, 2, p3, p3 * (g3 - dot_own[head : head + 1]))
            tops_own.append(m3)
            sums_own.append(jnp.sum(p3, 0, keepdims=True))

        pl.when(pair == 0)(lambda: send_chunk(1))
        message(M_K, pair).wait_recv()
        message(M_V, pair).wait_recv()

        @pl.when(has_ahead)
        def _():
            message(M_Q, pair).wait_recv()
            message(M_G, pair).wait_recv()

        @pl.when((pair == 0) & has_ahead)
        def _():
            message(M_DOT, 0).wait_recv()

        pl.when(pair + 2 < pairs)(lambda: send_chunk(pair + 2))

        pick_second(pair)
        k_oth = heads_of(ko, start, low_lanes, high_lanes)
        q_new = heads_of(qn, start, low_lanes, high_lanes)
        q_sec = heads_of(q2, 0, low_lanes, high_lanes)
        dot_new = dotn[pair]
        dot_sec = c0 * dot_new + c1 * dot_own
        lses, tops_sec, sums_sec, dq_heads = [], [], [], []
        for head in range(2):
            s1 = rows_by_rows(k_own[head], q_new[head]) * SCALE
            s2 = rows_by_rows(k_oth[head], q_sec[head]) * SCALE
            m1 = jnp.max(s1, 0, keepdims=True)
            m2 = jnp.max(s2, 0, keepdims=True)
            top_new = jnp.maximum(m1, jnp.where(core_zero, m2, LOW))
            top_sec = jnp.where(core_zero, top_new, m2)
            p1 = jnp.exp(s1 - top_new)
            p2 = jnp.exp(s2 - top_sec)
            z1 = jnp.sum(p1, 0, keepdims=True)
            z2 = jnp.sum(p2, 0, keepdims=True)
            sum_new = z1 + c0 * z2
            lses.append(top_new + jnp.log(sum_new))
            inverse = 1.0 / sum_new
            p1 = p1 * inverse
            p2 = p2 * jnp.where(core_zero, inverse, 1.0)
            tops_sec.append(jnp.where(core_zero, LOW, m2))
            sums_sec.append(z2)
            g1 = rows_by_rows(v_head(v, pair, head), v_head(gn, pair, head))
            g2_ = rows_by_rows(v_head(vo, pair, head), g2[:, head * V_DIM : (head + 1) * V_DIM])
            d1 = (p1 * (g1 - dot_new[head : head + 1])).astype(jnp.bfloat16)
            d2 = (p2 * (g2_ - dot_sec[head : head + 1])).astype(jnp.bfloat16)
            keep(head, 0, p1, d1)
            keep(head, 1, p2, d2)
            dq_heads.append(columns_by_rows(d1, k_own[head]) + c0 * columns_by_rows(d2, k_oth[head]))
        mss[pair] = jnp.concatenate(lses, 0)
        own_ms[pair] = jnp.concatenate(tops_own + sums_own + tops_sec + sums_sec, 0)
        store_pair(dqs, start, *dq_heads)
        via = sends_dq_via(pair)

        @pl.when(has_ahead)
        def _():
            message(M_MS, pair).start()

        @pl.when(has_ahead & jnp.logical_not(via))
        def _():
            message(M_DQ, pair).start()

        @pl.when(via)
        def _():
            message(M_DQ_VIA, pair).start()

        pl.when(pair >= 1)(lambda: pass_q_on(pair + 1))

    def second_phase(pair):
        pass_dq_on(pair)

        @pl.when(has_behind)
        def _():
            message(M_MS, pair).wait_recv()

        theirs = msr[pair]
        ours = own_ms[pair]
        away = rest[pair]
        top_far = jnp.where(has_behind, theirs, LOW)
        top = jnp.maximum(jnp.maximum(ours[0:2], ours[4:6]), jnp.maximum(away, top_far))
        whole = (
            ours[2:4] * jnp.exp(ours[0:2] - top)
            + ours[6:8] * jnp.exp(ours[4:6] - top)
            + jnp.exp(away - top)
            + jnp.exp(top_far - top)
        )
        total_lse = top + jnp.log(whole)
        ws[pair] = jnp.exp(top_far - total_lse)
        zero = jnp.zeros((4, rows), jnp.float32)
        fo[pair] = jnp.concatenate(
            [jnp.exp(ours[0:2] - total_lse), jnp.exp(ours[4:6] - total_lse), zero], 0
        )

        @pl.when(has_behind)
        def _():
            message(M_W, pair).start()

    def third_phase(pair):
        slot = lax.rem(pair, 3)
        start = pl.multiple_of(pair * PAIR_QK, 128)
        k_own = heads_of(k, start, low_lanes, high_lanes)
        q_own = heads_of(q, start, low_lanes, high_lanes)
        own_weight = fo[pair]
        far_weight = ws[pair]
        eye = lax.broadcasted_iota(jnp.int32, (rows, rows), 0) == lax.broadcasted_iota(
            jnp.int32, (rows, rows), 1
        )
        acc = lax.rem(pair, 2)

        def scaled(head, task, weight):
            prob = pring[slot, head * 3 + task].astype(jnp.float32) * weight
            grad = dring[slot, head * 3 + task].astype(jnp.float32) * (weight * SCALE)
            return prob.astype(jnp.bfloat16), grad.astype(jnp.bfloat16)

        dq_own, dk_own, columns = [], [], []
        for head in range(2):
            prob, grad = scaled(head, 2, own_weight[head : head + 1])
            accv[acc, :, head * V_DIM : (head + 1) * V_DIM] = plain(prob, v_head(g, pair, head))
            dk_own.append(plain(grad, q_own[head]))
            dq_own.append(columns_by_rows(grad, k_own[head]))
            columns.append(
                jnp.sum(jnp.where(eye, far_weight[head : head + 1] * SCALE, 0.0), 1, keepdims=True)
            )
        store_pair(acck.at[acc], 0, *dk_own)

        @pl.when(has_ahead)
        def _():
            message(M_W, pair).wait_recv()

        pick_second(pair)
        k_oth = heads_of(ko, start, low_lanes, high_lanes)
        q_new = heads_of(qn, start, low_lanes, high_lanes)
        q_sec = heads_of(q2, 0, low_lanes, high_lanes)
        new_weight = wr[pair]
        sec_weight = c0 * new_weight + c1 * own_weight[2:4]
        dq_heads, dk_heads, dko_heads = [], [], []
        for head in range(2):
            prob, grad = scaled(head, 1, sec_weight[head : head + 1])
            dvs[:, pl.ds(pl.multiple_of(pair * PAIR_V + head * V_DIM, 128), V_DIM)] = plain(
                prob, g2[:, head * V_DIM : (head + 1) * V_DIM]
            ).astype(jnp.bfloat16)
            dko_heads.append(plain(grad, q_sec[head]))
            dq_heads.append(dq_own[head] + c1 * columns_by_rows(grad, k_oth[head]))
        store_pair(dks, start, *dko_heads)
        message(M_DV, pair).start()
        message(M_DK, pair).start()
        for head in range(2):
            prob, grad = scaled(head, 0, new_weight[head : head + 1])
            accv[acc, :, head * V_DIM : (head + 1) * V_DIM] += plain(prob, v_head(gn, pair, head))
            dk_heads.append(plain(grad, q_new[head]))
        even, odd = dk_heads
        acck[acc, :, :128] += even[:, :128]
        acck[acc, :, 128:256] += even[:, 128:] + odd[:, :128]
        acck[acc, :, 256:] += odd[:, 128:]

        @pl.when(has_behind)
        def _():
            message(M_DQ, pair).wait_recv()

        first = pl.ds(start, 128)
        middle = pl.ds(pl.multiple_of(start + 128, 128), 128)
        last = pl.ds(pl.multiple_of(start + 256, 128), 128)
        even, odd = dq_heads
        dq[:, first] = (even[:, :128] + columns[0] * dq[:, first].astype(jnp.float32)).astype(dq.dtype)
        dq[:, middle] = (
            even[:, 128:]
            + odd[:, :128]
            + jnp.where(is_low, columns[0], columns[1]) * dq[:, middle].astype(jnp.float32)
        ).astype(dq.dtype)
        dq[:, last] = (odd[:, 128:] + columns[1] * dq[:, last].astype(jnp.float32)).astype(dq.dtype)

    def fourth_phase(pair):
        message(M_DK, pair).wait_recv()
        message(M_DV, pair).wait_recv()
        acc = lax.rem(pair, 2)
        dk[:, qk_cols(pair)] = (acck[acc] + dk[:, qk_cols(pair)].astype(jnp.float32)).astype(dk.dtype)
        dv[:, v_cols(pair)] = (accv[acc] + dv[:, v_cols(pair)].astype(jnp.float32)).astype(dv.dtype)

    def step(at, carry):
        for lag, phase in enumerate((first_phase, second_phase, third_phase, fourth_phase)):
            @pl.when((at >= lag) & (at < pairs + lag))
            def _(lag=lag, phase=phase):
                phase(at - lag)

        return carry

    def first_stage():
        for load in loads[4:]:
            load.wait()
        full_high, full_piece = 0.0, 0.0
        for slot in range(slots):
            full_high = full_high + full[slot] * acts[slot, :, half_rows:].astype(jnp.float32)
            full_piece = full_piece + full[slot] * grads[slot].astype(jnp.float32)
        high[...] = full_high.astype(high.dtype)
        is_upper = jnp.where(upper == 1, 1.0, 0.0)
        for slot in range(slots):
            mixed = is_upper * full_piece + (1.0 - is_upper) * grads[slot].astype(jnp.float32)
            pieces[slot] = mixed.astype(pieces.dtype)
        for each in own_copies():
            each.start()
        begin(E_ROWS, E_HIGH)

    def second_stage():
        for each in own_copies():
            each.wait()
        arrived(E_ROWS, E_HIGH)
        begin(E_LEVEL, E_SPREAD)

    def third_stage():
        arrived(E_LEVEL)

    def fourth_stage():
        arrived(E_AROUND)
        begin(E_OTHER)

    def fifth_stage():
        arrived(E_OTHER, E_ACTS, E_SPREAD)

    stages = {0: first_stage, 2: second_stage, 3: third_stage, 10: fourth_stage, 11: fifth_stage}
    spread_out = [(1 + at, each) for at, each in enumerate(expert_messages(E_ACTS))]
    spread_out += [(3 + at, each) for at, each in enumerate(expert_messages(E_AROUND))]
    products = own_slots * parts
    product_at, at_once = 11, 2

    def drain(pair, carry):
        def settle(condition, *kinds):
            @pl.when(condition)
            def _():
                for kind in kinds:
                    message(kind, pair).wait_send()

        settle(pair >= 0, M_K, M_V, M_DK, M_DV)
        settle(has_behind, M_W)
        settle(has_ahead, M_MS)
        settle(has_behind & jnp.logical_not(sends_q_via(pair)), M_Q, M_G)
        settle(sends_q_via(pair), M_Q_VIA, M_G_VIA)
        settle(passes_q_on(pair), M_Q_ON, M_G_ON)
        settle(has_ahead & jnp.logical_not(sends_dq_via(pair)), M_DQ)
        settle(sends_dq_via(pair), M_DQ_VIA)
        settle(passes_dq_on(pair), M_DQ_ON)
        return carry

    def sixth_stage():
        left_behind(E_ACTS, E_ROWS, E_HIGH, E_SPREAD, E_LEVEL, E_AROUND, E_OTHER)

    stages[product_at + products // at_once] = sixth_stage
    steps = max(pairs + 3, product_at + products // at_once + 1)
    settled = min(max(steps - DRAIN_LAG, 0), pairs)

    def step_with_experts(at, carry):
        step(at, carry)
        for when, stage in stages.items():
            pl.when(at == when)(stage)

        for when, each in spread_out:
            pl.when(at == when)(each.start)

        @pl.when((at >= product_at) & (at < product_at + products // at_once))
        def _():
            for part in range(at_once):
                expert_step((at - product_at) * at_once + part)

        pl.when((at >= DRAIN_LAG) & (at < settled + DRAIN_LAG))(lambda: drain(at - DRAIN_LAG, None))
        return carry

    lax.fori_loop(0, steps, step_with_experts, 0)

    @pl.when(has_behind)
    def _():
        message(M_DOT, 0).wait_send()

    lax.fori_loop(settled, pairs, drain, 0)


def gradients(queries, key_states, value_states, out_grad, lse_rest, out_dot, acts, grads, counts, lists):
    rows, qk = queries.shape
    vv = value_states.shape[1]
    pairs = qk // PAIR_QK
    slots, features, cap = acts.shape
    hidden = grads.shape[2]
    experts = slots - lists.shape[1]
    groups = lax.axis_size("grp")
    columns = lax.axis_size("ctx") // 4
    _, sems = first_sems(slots, groups - 1, groups // 2, columns)
    half = jnp.bfloat16
    vmem = pl.BlockSpec(memory_space=pltpu.VMEM)
    anywhere = pl.BlockSpec(memory_space=pl.ANY)
    small = pltpu.VMEM((pairs, 8, rows), jnp.float32)
    two_rows = pltpu.VMEM((pairs, 2, rows), jnp.float32)
    wide = pltpu.VMEM((rows, qk), half)
    narrow = pltpu.VMEM((rows, vv), half)
    return pl.pallas_call(
        functools.partial(attention_kernel, pairs),
        out_shape=[
            pltpu.VMEM((rows, qk), half),
            pltpu.VMEM((rows, qk), half),
            pltpu.VMEM((rows, vv), half),
            pltpu.VMEM((experts, features, hidden), jnp.float32),
            jax.ShapeDtypeStruct((rows, qk), half),
            jax.ShapeDtypeStruct((rows, vv), half),
            jax.ShapeDtypeStruct((rows, qk), half),
        ],
        in_specs=[anywhere] * 4 + [vmem] * 2 + [anywhere] * 2 + [pl.BlockSpec(memory_space=pltpu.SMEM)] * 2,
        out_specs=[vmem] * 4 + [anywhere] * 3,
        scratch_shapes=[
            wide,
            narrow,
            pltpu.VMEM((pairs, 2, rows), jnp.float32),
            wide,
            narrow,
            wide,
            wide,
            narrow,
            two_rows,
            two_rows,
            small,
            two_rows,
            two_rows,
            small,
            pltpu.VMEM((3, 6, rows, rows), half),
            pltpu.VMEM((3, 6, rows, rows), half),
            pltpu.VMEM((2, rows, PAIR_QK), jnp.float32),
            pltpu.VMEM((2, rows, PAIR_V), jnp.float32),
            pltpu.VMEM((rows, PAIR_QK), half),
            pltpu.VMEM((rows, PAIR_V), half),
            pltpu.VMEM((features, slots * cap), half),
            pltpu.VMEM((2 * slots, cap // 2, hidden), half),
            pltpu.VMEM((pairs, 2, rows), jnp.float32),
            pltpu.VMEM((pairs, 2, rows), jnp.float32),
            pltpu.VMEM((features, cap // 2), half),
            pltpu.VMEM(grads.shape, half),
            pltpu.VMEM((experts, 8, slots * cap), jnp.float32),
            wide,
            wide,
            narrow,
            narrow,
            pltpu.VMEM(acts.shape, half),
            pltpu.VMEM(grads.shape, half),
            pltpu.SemaphoreType.DMA((6,)),
            pltpu.SemaphoreType.DMA((KINDS, pairs)),
            pltpu.SemaphoreType.DMA((KINDS, pairs)),
            pltpu.SemaphoreType.DMA((sems,)),
            pltpu.SemaphoreType.DMA((sems,)),
            pltpu.SemaphoreType.DMA((2 * experts + 1,)),
        ],
        compiler_params=pltpu.CompilerParams(
            collective_id=0, has_side_effects=True, vmem_limit_bytes=LIMIT_MIB * 2**20
        ),
        name="window_grads",
    )(
        queries,
        key_states,
        value_states,
        out_grad,
        lse_rest,
        out_dot,
        acts,
        grads,
        counts,
        lists,
    )[:4]


def out_kernel(count, *refs):
    copies = [
        pltpu.make_async_copy(refs[at], refs[count + at].at[0], refs[2 * count].at[at])
        for at in range(count)
    ]
    for copy in copies:
        copy.start()
    for copy in copies:
        copy.wait()


def written_out(found):
    anywhere = pl.BlockSpec(memory_space=pl.ANY)
    count = len(found)
    return pl.pallas_call(
        functools.partial(out_kernel, count),
        out_shape=[jax.ShapeDtypeStruct((1, *each.shape), each.dtype) for each in found],
        in_specs=[pl.BlockSpec(memory_space=pltpu.VMEM)] * count,
        out_specs=[anywhere] * count,
        scratch_shapes=[pltpu.SemaphoreType.DMA((count,))],
        compiler_params=pltpu.CompilerParams(vmem_limit_bytes=24 * 2**20),
        name="written_out",
    )(*found)


def local(queries, key_states, value_states, out_grad, lse_rest, out_dot, moe_acts, moe_grads, counts, replica_list):
    found = gradients(
        queries[0],
        key_states[0],
        value_states[0],
        out_grad[0],
        lse_rest[0],
        out_dot[0],
        moe_acts[0],
        moe_grads[0],
        counts,
        replica_list,
    )
    return tuple(written_out(found))


def solution(mesh):
    return jax.shard_map(
        local,
        mesh=mesh,
        in_specs=(
            P("grp", "ctx", None),
            P("grp", "ctx", None),
            P("grp", "ctx", None),
            P("grp", "ctx", None),
            P("grp", None, "ctx"),
            P("grp", None, "ctx"),
            P("grp", None, "ctx", None),
            P("grp", None, "ctx", None),
            P(),
            P(),
        ),
        out_specs=(
            P("grp", "ctx", None),
            P("grp", "ctx", None),
            P("grp", "ctx", None),
            P("grp", None, "ctx", None),
        ),
        check_vma=False,
    )
```

```python
import functools

import jax
import jax.numpy as jnp
from jax import lax
from jax.experimental import pallas as pl
from jax.experimental.pallas import tpu as pltpu
from jax.sharding import PartitionSpec as P

QK_DIM = 192
V_DIM = 128
PAIR_QK = 2 * QK_DIM
PAIR_V = 2 * V_DIM
SCALE = QK_DIM**-0.5
LOW = -1e38
MESH = pl.DeviceIdType.MESH

M_Q, M_G, M_K, M_V, M_DQ, M_MS, M_W, M_DK, M_DV, M_DOT = range(10)
M_Q_VIA, M_G_VIA, M_DQ_VIA, M_Q_ON, M_G_ON, M_DQ_ON = range(10, 16)
KINDS = 16
LIMIT_MIB = 48
DRAIN_LAG = 5

E_ACTS, E_ROWS, E_HIGH, E_SPREAD, E_LEVEL, E_AROUND, E_OTHER = range(7)


def first_sems(slots, replicas, owners, columns):
    sizes = {
        E_ACTS: replicas,
        E_ROWS: replicas,
        E_HIGH: 1,
        E_SPREAD: 2 * (owners - 1),
        E_LEVEL: slots,
        E_AROUND: 2 * (columns - 1),
        E_OTHER: 2 * columns,
    }
    starts, total = {}, 0
    for kind, size in sizes.items():
        starts[kind] = total
        total += size
    return starts, total


def rows_by_rows(a, b):
    return lax.dot_general(a, b, (((1,), (1,)), ((), ())), preferred_element_type=jnp.float32)


def plain(a, b):
    return lax.dot_general(a, b, (((1,), (0,)), ((), ())), preferred_element_type=jnp.float32)


def columns_by_rows(a, b):
    return lax.dot_general(a, b, (((0,), (0,)), ((), ())), preferred_element_type=jnp.float32)


def heads_of(ref, start, low_lanes, high_lanes):
    first = ref[:, pl.ds(start, 128)]
    middle = ref[:, pl.ds(pl.multiple_of(start + 128, 128), 128)]
    last = ref[:, pl.ds(pl.multiple_of(start + 256, 128), 128)]
    return (
        jnp.concatenate([first, middle * low_lanes], 1),
        jnp.concatenate([middle * high_lanes, last], 1),
    )


def store_pair(ref, index, even, odd):
    start = index
    kind = ref.dtype
    ref[:, pl.ds(start, 128)] = even[:, :128].astype(kind)
    ref[:, pl.ds(pl.multiple_of(start + 128, 128), 128)] = (even[:, 128:] + odd[:, :128]).astype(kind)
    ref[:, pl.ds(pl.multiple_of(start + 256, 128), 128)] = odd[:, 128:].astype(kind)


def attention_kernel(
    pairs,
    q_in,
    k_in,
    v_in,
    g_in,
    rest_rows,
    dot_rows,
    acts_in,
    grads_in,
    counts,
    lists,
    dq,
    dk,
    dv,
    expert,
    q_via,
    g_via,
    dq_via,
    qn,
    gn,
    dotn,
    ko,
    vo,
    dqs,
    dks,
    dvs,
    mss,
    msr,
    own_ms,
    ws,
    wr,
    fo,
    pring,
    dring,
    acck,
    accv,
    q2,
    g2,
    left,
    right,
    rest,
    dot,
    high,
    pieces,
    lanes,
    q,
    k,
    v,
    g,
    acts,
    grads,
    in_sem,
    send,
    recv,
    esend,
    erecv,
    own_sem,
):
    rows = q.shape[0]
    loads = [
        pltpu.make_async_copy(source, held, in_sem.at[at])
        for at, (source, held) in enumerate(
            ((k_in, k), (v_in, v), (q_in, q), (g_in, g), (acts_in, acts), (grads_in, grads))
        )
    ]
    for load in loads:
        load.start()
    me = lax.axis_index("ctx")
    total = lax.axis_size("ctx")
    core = lax.rem(me, 2)
    ahead_chip = lax.rem(me + 2, total)
    behind_chip = lax.rem(me + total - 2, total)
    other = me + 1 - 2 * core
    core_zero = core == 0
    c0 = jnp.where(core_zero, 1.0, 0.0).astype(jnp.float32)
    c1 = 1.0 - c0
    has_behind = me >= 2
    has_ahead = me < total - 2
    column = lax.div(me, 4)
    low_level = lax.rem(me, 4) < 2
    level = me + 2 - 4 * lax.div(lax.rem(me, 4), 2)
    last_column = total // 4 - 1

    def q_detour(boundary, pair):
        return (lax.rem(pair, 4) <= boundary) & (pair >= 2)

    def dq_detour(boundary, pair):
        return lax.rem(pair, 4) < 3 - boundary

    def sends_q_via(pair):
        return low_level & (column >= 1) & q_detour(column - 1, pair)

    def passes_q_on(pair):
        return jnp.logical_not(low_level) & (column >= 1) & q_detour(column - 1, pair)

    def sends_dq_via(pair):
        return jnp.logical_not(low_level) & (column < last_column) & dq_detour(column, pair)

    def passes_dq_on(pair):
        return low_level & (column < last_column) & dq_detour(column, pair)

    def qk_cols(pair):
        return pl.ds(pl.multiple_of(pair * PAIR_QK, 128), PAIR_QK)

    def v_cols(pair):
        return pl.ds(pl.multiple_of(pair * PAIR_V, 128), PAIR_V)

    def message(kind, pair):
        src, dst, target = {
            M_Q: lambda: (q_in.at[:, qk_cols(pair)], qn.at[:, qk_cols(pair)], behind_chip),
            M_G: lambda: (g_in.at[:, v_cols(pair)], gn.at[:, v_cols(pair)], behind_chip),
            M_K: lambda: (k_in.at[:, qk_cols(pair)], ko.at[:, qk_cols(pair)], other),
            M_V: lambda: (v_in.at[:, v_cols(pair)], vo.at[:, v_cols(pair)], other),
            M_DQ: lambda: (dqs.at[:, qk_cols(pair)], dq.at[:, qk_cols(pair)], ahead_chip),
            M_MS: lambda: (mss.at[pair], msr.at[pair], ahead_chip),
            M_W: lambda: (ws.at[pair], wr.at[pair], behind_chip),
            M_DK: lambda: (dks.at[:, qk_cols(pair)], dk.at[:, qk_cols(pair)], other),
            M_DV: lambda: (dvs.at[:, v_cols(pair)], dv.at[:, v_cols(pair)], other),
            M_DOT: lambda: (dot, dotn, behind_chip),
            M_Q_VIA: lambda: (q_in.at[:, qk_cols(pair)], q_via.at[:, qk_cols(pair)], level),
            M_G_VIA: lambda: (g_in.at[:, v_cols(pair)], g_via.at[:, v_cols(pair)], level),
            M_DQ_VIA: lambda: (dqs.at[:, qk_cols(pair)], dq_via.at[:, qk_cols(pair)], level),
            M_Q_ON: lambda: (
                q_via.at[:, qk_cols(pair)],
                qn.at[:, qk_cols(pair)],
                lax.rem(me + total - 4, total),
            ),
            M_G_ON: lambda: (
                g_via.at[:, v_cols(pair)],
                gn.at[:, v_cols(pair)],
                lax.rem(me + total - 4, total),
            ),
            M_DQ_ON: lambda: (
                dq_via.at[:, qk_cols(pair)],
                dq.at[:, qk_cols(pair)],
                lax.rem(me + 4, total),
            ),
        }[kind]()
        lands_as = {M_Q_ON: M_Q, M_G_ON: M_G, M_DQ_ON: M_DQ}.get(kind, kind)
        return pltpu.make_async_remote_copy(
            src_ref=src,
            dst_ref=dst,
            send_sem=send.at[kind, pair],
            recv_sem=recv.at[lands_as, pair],
            device_id={"ctx": target},
            device_id_type=MESH,
        )

    group = lax.axis_index("grp")
    groups = lax.axis_size("grp")
    slots = acts.shape[0]
    replicas = groups - 1
    own_slots = slots - replicas
    half_rows = left.shape[1] // (2 * slots)
    piece = pieces.shape[1]
    columns = total // 4
    owners = groups // 2
    upper = (me >= total // 2).astype(jnp.int32)
    twin = group + 1 - 2 * lax.rem(group, 2)
    starts, _ = first_sems(slots, replicas, owners, columns)

    def unit(device):
        return right.at[
            pl.ds(slots * (device >= total // 2).astype(jnp.int32), slots),
            pl.ds(pl.multiple_of(lax.rem(device, total // 2) * piece, piece), piece),
        ]

    def piece_at(device, index):
        return right.at[
            slots * (device >= total // 2).astype(jnp.int32) + index,
            pl.ds(pl.multiple_of(lax.rem(device, total // 2) * piece, piece), piece),
        ]

    def block(index):
        return left.at[:, pl.ds(pl.multiple_of(index * half_rows, 128), half_rows)]

    def expert_message(kind, at, src, dst, target):
        sem = starts[kind] + at
        return pltpu.make_async_remote_copy(
            src_ref=src,
            dst_ref=dst,
            send_sem=esend.at[sem],
            recv_sem=erecv.at[sem],
            device_id=target,
            device_id_type=MESH,
        )

    def in_group(device):
        return {"ctx": device, "grp": group}

    def owner(index):
        return {"ctx": me, "grp": index}

    def expert_messages(kind):
        if kind == E_ACTS:
            return [
                expert_message(
                    kind,
                    r,
                    acts.at[own_slots + r, :, pl.ds(0, half_rows)],
                    block(own_slots + r),
                    owner(lax.rem(group + r + 1, groups)),
                )
                for r in range(replicas)
            ]
        if kind == E_ROWS:
            return [
                expert_message(
                    kind,
                    r,
                    pieces.at[own_slots + r],
                    piece_at(me, own_slots + r),
                    {"ctx": me if r % 2 else level, "grp": lax.rem(group + r + 1, groups)},
                )
                for r in range(replicas)
            ]
        if kind == E_HIGH:
            place = lax.rem(twin - group + groups, groups)
            return [expert_message(kind, 0, high, block(slots + 1 + place), owner(twin))]
        if kind == E_SPREAD:
            place = lax.rem(group - twin + groups, groups)
            found = []
            for m in range(1, owners):
                to = owner(lax.rem(group + 2 * m, groups))
                found.append(
                    expert_message(kind, 2 * m - 2, high, block(slots + 1 + 2 * m), to)
                )
                found.append(
                    expert_message(
                        kind,
                        2 * m - 1,
                        block(slots + 1 + place),
                        block(slots + 1 + lax.rem(place + 2 * m, groups)),
                        to,
                    )
                )
            return found
        if kind == E_LEVEL:
            found = []
            for index in range(slots):
                away = index >= own_slots and (index - own_slots) % 2 == 0
                held = piece_at(level if away else me, index)
                found.append(expert_message(kind, index, held, held, in_group(level)))
            return found
        if kind == E_AROUND:
            return [
                expert_message(
                    kind,
                    2 * m - 2 + which,
                    unit(device),
                    unit(device),
                    in_group(lax.rem(me + 4 * m, total)),
                )
                for m in range(1, columns)
                for which, device in enumerate((me, level))
            ]
        return [
            expert_message(kind, m, unit(2 * m + core), unit(2 * m + core), in_group(other))
            for m in range(2 * columns)
        ]

    def own_copies():
        found = [
            pltpu.make_async_copy(
                acts.at[slot, :, pl.ds(0, half_rows)], block(slot), own_sem.at[slot]
            )
            for slot in range(own_slots)
        ]
        found.append(pltpu.make_async_copy(high, block(slots + 1), own_sem.at[own_slots]))
        place = pl.ds(pl.multiple_of(lax.rem(me, total // 2) * piece, piece), piece)
        for slot in range(own_slots):
            found.append(
                pltpu.make_async_copy(
                    pieces.at[slot],
                    right.at[slots * upper + slot, place],
                    own_sem.at[own_slots + 1 + slot],
                )
            )
        return found

    def begin(*kinds):
        for kind in kinds:
            for each in expert_messages(kind):
                each.start()

    def arrived(*kinds):
        for kind in kinds:
            for each in expert_messages(kind):
                each.wait_recv()

    def left_behind(*kinds):
        for kind in kinds:
            for each in expert_messages(kind):
                each.wait_send()

    width = min(expert.shape[2], 256)
    parts = expert.shape[2] // width

    def expert_step(index):
        mask = lanes[lax.div(index, parts)][0:1].astype(left.dtype)
        cols = pl.ds(pl.multiple_of(lax.rem(index, parts) * width, 128), width)
        result = None
        for low, count in ((0, slots), (slots + 1, slots - 1)):
            here = slice(low * half_rows, (low + count) * half_rows)
            a = left[:, here] * mask[:, here]
            b = right[low : low + count, :, cols].reshape(count * half_rows, width)
            product = plain(a, b)
            result = product if result is None else result + product
        expert[lax.div(index, parts), :, cols] = result

    barrier = pltpu.get_barrier_semaphore()
    partners = [in_group(partner) for partner in (behind_chip, ahead_chip, other, level)]
    partners += [in_group(lax.rem(me + 4 * m, total)) for m in range(1, columns)]
    partners += [owner(lax.rem(group + m, groups)) for m in range(1, groups)]
    partners += [{"ctx": level, "grp": lax.rem(group + m, groups)} for m in range(1, groups, 2)]
    for partner in partners:
        pl.semaphore_signal(barrier, inc=1, device_id=partner, device_id_type=MESH)
    pl.semaphore_wait(barrier, len(partners))

    def send_chunk(pair):
        via = sends_q_via(pair)

        @pl.when(has_behind & jnp.logical_not(via))
        def _():
            message(M_Q, pair).start()
            message(M_G, pair).start()

        @pl.when(via)
        def _():
            message(M_Q_VIA, pair).start()
            message(M_G_VIA, pair).start()

        message(M_K, pair).start()
        message(M_V, pair).start()

    def pass_q_on(pair):
        @pl.when((pair < pairs) & passes_q_on(pair))
        def _():
            message(M_Q_VIA, pair).wait_recv()
            message(M_Q_ON, pair).start()
            message(M_G_VIA, pair).wait_recv()
            message(M_G_ON, pair).start()

    def pass_dq_on(pair):
        @pl.when(passes_dq_on(pair))
        def _():
            message(M_DQ_VIA, pair).wait_recv()
            message(M_DQ_ON, pair).start()

    send_chunk(0)

    @pl.when(jnp.logical_not(has_ahead))
    def _():
        qn[...] = jnp.zeros_like(qn)
        gn[...] = jnp.zeros_like(gn)
        dotn[...] = jnp.zeros_like(dotn)
        wr[...] = jnp.zeros_like(wr)

    @pl.when(jnp.logical_not(has_behind))
    def _():
        msr[...] = jnp.zeros_like(msr)
        dq[...] = jnp.zeros_like(dq)

    for pair in range(pairs):
        rest[pair] = rest_rows[2 * pair : 2 * pair + 2]
        dot[pair] = dot_rows[2 * pair : 2 * pair + 2]

    @pl.when(has_behind)
    def _():
        message(M_DOT, 0).start()

    cap = acts.shape[2]
    full = [jnp.where(counts[group, slot] == cap, 1.0, 0.0) for slot in range(slots)]
    row_ids = lax.broadcasted_iota(jnp.int32, (1, half_rows), 1)

    def mark(expert_id, index, value):
        lanes[expert_id, 0:1, index * half_rows : (index + 1) * half_rows] = value

    for k_ in range(own_slots):
        for slot in range(own_slots):
            live = row_ids < counts[group, slot]
            mark(k_, slot, jnp.where(live, 1.0, 0.0) if slot == k_ else jnp.zeros(row_ids.shape))
        mark(k_, slots, jnp.zeros(row_ids.shape))
        mark(k_, slots + 1, jnp.zeros(row_ids.shape) + full[k_])
        for r in range(replicas):
            source = lax.rem(group + groups - 1 - r, groups)
            held = counts[source, own_slots + r]
            wanted = jnp.where(lists[source, r] == k_, 1.0, 0.0)
            mark(k_, own_slots + r, jnp.where(row_ids < held, wanted, 0.0))
            whole = jnp.where(held == cap, wanted, 0.0)
            mark(k_, slots + 2 + r, jnp.zeros(row_ids.shape) + whole)

    lane = lax.broadcasted_iota(jnp.int32, (1, 128), 1)
    low_lanes = jnp.where(lane < 64, 1.0, 0.0).astype(jnp.bfloat16)
    high_lanes = jnp.where(lane < 64, 0.0, 1.0).astype(jnp.bfloat16)
    is_low = lane < 64

    def pick_second(pair):
        @pl.when(core_zero)
        def _():
            q2[...] = qn[:, qk_cols(pair)]
            g2[...] = gn[:, v_cols(pair)]

        @pl.when(jnp.logical_not(core_zero))
        def _():
            q2[...] = q[:, qk_cols(pair)]
            g2[...] = g[:, v_cols(pair)]

    def v_head(ref, pair, head):
        return ref[:, pl.ds(pl.multiple_of(pair * PAIR_V + head * V_DIM, 128), V_DIM)]

    def first_phase(pair):
        @pl.when(pair == 0)
        def _():
            for load in loads[:4]:
                load.wait()

        slot = lax.rem(pair, 3)
        start = pl.multiple_of(pair * PAIR_QK, 128)
        k_own = heads_of(k, start, low_lanes, high_lanes)
        q_own = heads_of(q, start, low_lanes, high_lanes)
        key_pos = lax.broadcasted_iota(jnp.int32, (rows, rows), 0)
        query_pos = lax.broadcasted_iota(jnp.int32, (rows, rows), 1)
        allowed = key_pos <= query_pos
        dot_own = dot[pair]

        def keep(head, task, prob, grad):
            pring[slot, head * 3 + task] = prob.astype(jnp.bfloat16)
            dring[slot, head * 3 + task] = grad.astype(jnp.bfloat16)

        tops_own, sums_own = [], []
        for head in range(2):
            s3 = rows_by_rows(k_own[head], q_own[head]) * SCALE
            s3 = jnp.where(allowed, s3, -1e30)
            m3 = jnp.max(s3, 0, keepdims=True)
            p3 = jnp.exp(s3 - m3)
            g3 = rows_by_rows(v_head(v, pair, head), v_head(g, pair, head))
            keep(head, 2, p3, p3 * (g3 - dot_own[head : head + 1]))
            tops_own.append(m3)
            sums_own.append(jnp.sum(p3, 0, keepdims=True))

        pl.when(pair == 0)(lambda: send_chunk(1))
        message(M_K, pair).wait_recv()
        message(M_V, pair).wait_recv()

        @pl.when(has_ahead)
        def _():
            message(M_Q, pair).wait_recv()
            message(M_G, pair).wait_recv()

        @pl.when((pair == 0) & has_ahead)
        def _():
            message(M_DOT, 0).wait_recv()

        pl.when(pair + 2 < pairs)(lambda: send_chunk(pair + 2))

        pick_second(pair)
        k_oth = heads_of(ko, start, low_lanes, high_lanes)
        q_new = heads_of(qn, start, low_lanes, high_lanes)
        q_sec = heads_of(q2, 0, low_lanes, high_lanes)
        dot_new = dotn[pair]
        dot_sec = c0 * dot_new + c1 * dot_own
        lses, tops_sec, sums_sec, dq_heads = [], [], [], []
        for head in range(2):
            s1 = rows_by_rows(k_own[head], q_new[head]) * SCALE
            s2 = rows_by_rows(k_oth[head], q_sec[head]) * SCALE
            m1 = jnp.max(s1, 0, keepdims=True)
            m2 = jnp.max(s2, 0, keepdims=True)
            top_new = jnp.maximum(m1, jnp.where(core_zero, m2, LOW))
            top_sec = jnp.where(core_zero, top_new, m2)
            p1 = jnp.exp(s1 - top_new)
            p2 = jnp.exp(s2 - top_sec)
            z1 = jnp.sum(p1, 0, keepdims=True)
            z2 = jnp.sum(p2, 0, keepdims=True)
            sum_new = z1 + c0 * z2
            lses.append(top_new + jnp.log(sum_new))
            inverse = 1.0 / sum_new
            p1 = p1 * inverse
            p2 = p2 * jnp.where(core_zero, inverse, 1.0)
            tops_sec.append(jnp.where(core_zero, LOW, m2))
            sums_sec.append(z2)
            g1 = rows_by_rows(v_head(v, pair, head), v_head(gn, pair, head))
            g2_ = rows_by_rows(v_head(vo, pair, head), g2[:, head * V_DIM : (head + 1) * V_DIM])
            d1 = (p1 * (g1 - dot_new[head : head + 1])).astype(jnp.bfloat16)
            d2 = (p2 * (g2_ - dot_sec[head : head + 1])).astype(jnp.bfloat16)
            keep(head, 0, p1, d1)
            keep(head, 1, p2, d2)
            dq_heads.append(columns_by_rows(d1, k_own[head]) + c0 * columns_by_rows(d2, k_oth[head]))
        mss[pair] = jnp.concatenate(lses, 0)
        own_ms[pair] = jnp.concatenate(tops_own + sums_own + tops_sec + sums_sec, 0)
        store_pair(dqs, start, *dq_heads)
        via = sends_dq_via(pair)

        @pl.when(has_ahead)
        def _():
            message(M_MS, pair).start()

        @pl.when(has_ahead & jnp.logical_not(via))
        def _():
            message(M_DQ, pair).start()

        @pl.when(via)
        def _():
            message(M_DQ_VIA, pair).start()

        pl.when(pair >= 1)(lambda: pass_q_on(pair + 1))

    def second_phase(pair):
        pass_dq_on(pair)

        @pl.when(has_behind)
        def _():
            message(M_MS, pair).wait_recv()

        theirs = msr[pair]
        ours = own_ms[pair]
        away = rest[pair]
        top_far = jnp.where(has_behind, theirs, LOW)
        top = jnp.maximum(jnp.maximum(ours[0:2], ours[4:6]), jnp.maximum(away, top_far))
        whole = (
            ours[2:4] * jnp.exp(ours[0:2] - top)
            + ours[6:8] * jnp.exp(ours[4:6] - top)
            + jnp.exp(away - top)
            + jnp.exp(top_far - top)
        )
        total_lse = top + jnp.log(whole)
        ws[pair] = jnp.exp(top_far - total_lse)
        zero = jnp.zeros((4, rows), jnp.float32)
        fo[pair] = jnp.concatenate(
            [jnp.exp(ours[0:2] - total_lse), jnp.exp(ours[4:6] - total_lse), zero], 0
        )

        @pl.when(has_behind)
        def _():
            message(M_W, pair).start()

    def third_phase(pair):
        slot = lax.rem(pair, 3)
        start = pl.multiple_of(pair * PAIR_QK, 128)
        k_own = heads_of(k, start, low_lanes, high_lanes)
        q_own = heads_of(q, start, low_lanes, high_lanes)
        own_weight = fo[pair]
        far_weight = ws[pair]
        eye = lax.broadcasted_iota(jnp.int32, (rows, rows), 0) == lax.broadcasted_iota(
            jnp.int32, (rows, rows), 1
        )
        acc = lax.rem(pair, 2)

        def scaled(head, task, weight):
            prob = pring[slot, head * 3 + task].astype(jnp.float32) * weight
            grad = dring[slot, head * 3 + task].astype(jnp.float32) * (weight * SCALE)
            return prob.astype(jnp.bfloat16), grad.astype(jnp.bfloat16)

        dq_own, dk_own, columns = [], [], []
        for head in range(2):
            prob, grad = scaled(head, 2, own_weight[head : head + 1])
            accv[acc, :, head * V_DIM : (head + 1) * V_DIM] = plain(prob, v_head(g, pair, head))
            dk_own.append(plain(grad, q_own[head]))
            dq_own.append(columns_by_rows(grad, k_own[head]))
            columns.append(
                jnp.sum(jnp.where(eye, far_weight[head : head + 1] * SCALE, 0.0), 1, keepdims=True)
            )
        store_pair(acck.at[acc], 0, *dk_own)

        @pl.when(has_ahead)
        def _():
            message(M_W, pair).wait_recv()

        pick_second(pair)
        k_oth = heads_of(ko, start, low_lanes, high_lanes)
        q_new = heads_of(qn, start, low_lanes, high_lanes)
        q_sec = heads_of(q2, 0, low_lanes, high_lanes)
        new_weight = wr[pair]
        sec_weight = c0 * new_weight + c1 * own_weight[2:4]
        dq_heads, dk_heads, dko_heads = [], [], []
        for head in range(2):
            prob, grad = scaled(head, 1, sec_weight[head : head + 1])
            dvs[:, pl.ds(pl.multiple_of(pair * PAIR_V + head * V_DIM, 128), V_DIM)] = plain(
                prob, g2[:, head * V_DIM : (head + 1) * V_DIM]
            ).astype(jnp.bfloat16)
            dko_heads.append(plain(grad, q_sec[head]))
            dq_heads.append(dq_own[head] + c1 * columns_by_rows(grad, k_oth[head]))
        store_pair(dks, start, *dko_heads)
        message(M_DV, pair).start()
        message(M_DK, pair).start()
        for head in range(2):
            prob, grad = scaled(head, 0, new_weight[head : head + 1])
            accv[acc, :, head * V_DIM : (head + 1) * V_DIM] += plain(prob, v_head(gn, pair, head))
            dk_heads.append(plain(grad, q_new[head]))
        even, odd = dk_heads
        acck[acc, :, :128] += even[:, :128]
        acck[acc, :, 128:256] += even[:, 128:] + odd[:, :128]
        acck[acc, :, 256:] += odd[:, 128:]

        @pl.when(has_behind)
        def _():
            message(M_DQ, pair).wait_recv()

        first = pl.ds(start, 128)
        middle = pl.ds(pl.multiple_of(start + 128, 128), 128)
        last = pl.ds(pl.multiple_of(start + 256, 128), 128)
        even, odd = dq_heads
        dq[:, first] = (even[:, :128] + columns[0] * dq[:, first].astype(jnp.float32)).astype(dq.dtype)
        dq[:, middle] = (
            even[:, 128:]
            + odd[:, :128]
            + jnp.where(is_low, columns[0], columns[1]) * dq[:, middle].astype(jnp.float32)
        ).astype(dq.dtype)
        dq[:, last] = (odd[:, 128:] + columns[1] * dq[:, last].astype(jnp.float32)).astype(dq.dtype)

    def fourth_phase(pair):
        message(M_DK, pair).wait_recv()
        message(M_DV, pair).wait_recv()
        acc = lax.rem(pair, 2)
        dk[:, qk_cols(pair)] = (acck[acc] + dk[:, qk_cols(pair)].astype(jnp.float32)).astype(dk.dtype)
        dv[:, v_cols(pair)] = (accv[acc] + dv[:, v_cols(pair)].astype(jnp.float32)).astype(dv.dtype)

    def step(at, carry):
        for lag, phase in enumerate((first_phase, second_phase, third_phase, fourth_phase)):
            @pl.when((at >= lag) & (at < pairs + lag))
            def _(lag=lag, phase=phase):
                phase(at - lag)

        return carry

    def first_stage():
        for load in loads[4:]:
            load.wait()
        full_high, full_piece = 0.0, 0.0
        for slot in range(slots):
            full_high = full_high + full[slot] * acts[slot, :, half_rows:].astype(jnp.float32)
            full_piece = full_piece + full[slot] * grads[slot].astype(jnp.float32)
        high[...] = full_high.astype(high.dtype)
        is_upper = jnp.where(upper == 1, 1.0, 0.0)
        for slot in range(slots):
            mixed = is_upper * full_piece + (1.0 - is_upper) * grads[slot].astype(jnp.float32)
            pieces[slot] = mixed.astype(pieces.dtype)
        for each in own_copies():
            each.start()
        begin(E_ROWS, E_HIGH)

    def second_stage():
        for each in own_copies():
            each.wait()
        arrived(E_ROWS, E_HIGH)
        begin(E_LEVEL, E_SPREAD)

    def third_stage():
        arrived(E_LEVEL)

    def fourth_stage():
        arrived(E_AROUND)
        begin(E_OTHER)

    def fifth_stage():
        arrived(E_OTHER, E_ACTS, E_SPREAD)

    stages = {0: first_stage, 2: second_stage, 3: third_stage, 10: fourth_stage, 11: fifth_stage}
    spread_out = [(1 + at, each) for at, each in enumerate(expert_messages(E_ACTS))]
    spread_out += [(3 + at, each) for at, each in enumerate(expert_messages(E_AROUND))]
    products = own_slots * parts
    product_at, at_once = 11, 2

    def drain(pair, carry):
        def settle(condition, *kinds):
            @pl.when(condition)
            def _():
                for kind in kinds:
                    message(kind, pair).wait_send()

        settle(pair >= 0, M_K, M_V, M_DK, M_DV)
        settle(has_behind, M_W)
        settle(has_ahead, M_MS)
        settle(has_behind & jnp.logical_not(sends_q_via(pair)), M_Q, M_G)
        settle(sends_q_via(pair), M_Q_VIA, M_G_VIA)
        settle(passes_q_on(pair), M_Q_ON, M_G_ON)
        settle(has_ahead & jnp.logical_not(sends_dq_via(pair)), M_DQ)
        settle(sends_dq_via(pair), M_DQ_VIA)
        settle(passes_dq_on(pair), M_DQ_ON)
        return carry

    def sixth_stage():
        left_behind(E_ACTS, E_ROWS, E_HIGH, E_SPREAD, E_LEVEL, E_AROUND, E_OTHER)

    stages[product_at + products // at_once] = sixth_stage
    steps = max(pairs + 3, product_at + products // at_once + 1)
    settled = min(max(steps - DRAIN_LAG, 0), pairs)

    def step_with_experts(at, carry):
        step(at, carry)
        for when, stage in stages.items():
            pl.when(at == when)(stage)

        for when, each in spread_out:
            pl.when(at == when)(each.start)

        @pl.when((at >= product_at) & (at < product_at + products // at_once))
        def _():
            for part in range(at_once):
                expert_step((at - product_at) * at_once + part)

        pl.when((at >= DRAIN_LAG) & (at < settled + DRAIN_LAG))(lambda: drain(at - DRAIN_LAG, None))
        return carry

    lax.fori_loop(0, steps, step_with_experts, 0)

    @pl.when(has_behind)
    def _():
        message(M_DOT, 0).wait_send()

    lax.fori_loop(settled, pairs, drain, 0)


def gradients(queries, key_states, value_states, out_grad, lse_rest, out_dot, acts, grads, counts, lists):
    rows, qk = queries.shape
    vv = value_states.shape[1]
    pairs = qk // PAIR_QK
    slots, features, cap = acts.shape
    hidden = grads.shape[2]
    experts = slots - lists.shape[1]
    groups = lax.axis_size("grp")
    columns = lax.axis_size("ctx") // 4
    _, sems = first_sems(slots, groups - 1, groups // 2, columns)
    half = jnp.bfloat16
    vmem = pl.BlockSpec(memory_space=pltpu.VMEM)
    anywhere = pl.BlockSpec(memory_space=pl.ANY)
    small = pltpu.VMEM((pairs, 8, rows), jnp.float32)
    two_rows = pltpu.VMEM((pairs, 2, rows), jnp.float32)
    wide = pltpu.VMEM((rows, qk), half)
    narrow = pltpu.VMEM((rows, vv), half)
    return pl.pallas_call(
        functools.partial(attention_kernel, pairs),
        out_shape=[
            pltpu.VMEM((rows, qk), half),
            pltpu.VMEM((rows, qk), half),
            pltpu.VMEM((rows, vv), half),
            pltpu.VMEM((experts, features, hidden), jnp.float32),
            jax.ShapeDtypeStruct((rows, qk), half),
            jax.ShapeDtypeStruct((rows, vv), half),
            jax.ShapeDtypeStruct((rows, qk), half),
        ],
        in_specs=[anywhere] * 4 + [vmem] * 2 + [anywhere] * 2 + [pl.BlockSpec(memory_space=pltpu.SMEM)] * 2,
        out_specs=[vmem] * 4 + [anywhere] * 3,
        scratch_shapes=[
            wide,
            narrow,
            pltpu.VMEM((pairs, 2, rows), jnp.float32),
            wide,
            narrow,
            wide,
            wide,
            narrow,
            two_rows,
            two_rows,
            small,
            two_rows,
            two_rows,
            small,
            pltpu.VMEM((3, 6, rows, rows), half),
            pltpu.VMEM((3, 6, rows, rows), half),
            pltpu.VMEM((2, rows, PAIR_QK), jnp.float32),
            pltpu.VMEM((2, rows, PAIR_V), jnp.float32),
            pltpu.VMEM((rows, PAIR_QK), half),
            pltpu.VMEM((rows, PAIR_V), half),
            pltpu.VMEM((features, slots * cap), half),
            pltpu.VMEM((2 * slots, cap // 2, hidden), half),
            pltpu.VMEM((pairs, 2, rows), jnp.float32),
            pltpu.VMEM((pairs, 2, rows), jnp.float32),
            pltpu.VMEM((features, cap // 2), half),
            pltpu.VMEM(grads.shape, half),
            pltpu.VMEM((experts, 8, slots * cap), jnp.float32),
            wide,
            wide,
            narrow,
            narrow,
            pltpu.VMEM(acts.shape, half),
            pltpu.VMEM(grads.shape, half),
            pltpu.SemaphoreType.DMA((6,)),
            pltpu.SemaphoreType.DMA((KINDS, pairs)),
            pltpu.SemaphoreType.DMA((KINDS, pairs)),
            pltpu.SemaphoreType.DMA((sems,)),
            pltpu.SemaphoreType.DMA((sems,)),
            pltpu.SemaphoreType.DMA((2 * experts + 1,)),
        ],
        compiler_params=pltpu.CompilerParams(
            collective_id=0, has_side_effects=True, vmem_limit_bytes=LIMIT_MIB * 2**20
        ),
        name="window_grads",
    )(
        queries,
        key_states,
        value_states,
        out_grad,
        lse_rest,
        out_dot,
        acts,
        grads,
        counts,
        lists,
    )[:4]


def out_kernel(count, *refs):
    copies = [
        pltpu.make_async_copy(refs[at], refs[count + at].at[0], refs[2 * count].at[at])
        for at in range(count)
    ]
    for copy in copies:
        copy.start()
    for copy in copies:
        copy.wait()


def written_out(found):
    anywhere = pl.BlockSpec(memory_space=pl.ANY)
    count = len(found)
    return pl.pallas_call(
        functools.partial(out_kernel, count),
        out_shape=[jax.ShapeDtypeStruct((1, *each.shape), each.dtype) for each in found],
        in_specs=[pl.BlockSpec(memory_space=pltpu.VMEM)] * count,
        out_specs=[anywhere] * count,
        scratch_shapes=[pltpu.SemaphoreType.DMA((count,))],
        compiler_params=pltpu.CompilerParams(vmem_limit_bytes=24 * 2**20),
        name="written_out",
    )(*found)


def local(queries, key_states, value_states, out_grad, lse_rest, out_dot, moe_acts, moe_grads, counts, replica_list):
    found = gradients(
        queries[0],
        key_states[0],
        value_states[0],
        out_grad[0],
        lse_rest[0],
        out_dot[0],
        moe_acts[0],
        moe_grads[0],
        counts,
        replica_list,
    )
    return tuple(written_out(found))


def solution(mesh):
    return jax.shard_map(
        local,
        mesh=mesh,
        in_specs=(
            P("grp", "ctx", None),
            P("grp", "ctx", None),
            P("grp", "ctx", None),
            P("grp", "ctx", None),
            P("grp", None, "ctx"),
            P("grp", None, "ctx"),
            P("grp", None, "ctx", None),
            P("grp", None, "ctx", None),
            P(),
            P(),
        ),
        out_specs=(
            P("grp", "ctx", None),
            P("grp", "ctx", None),
            P("grp", "ctx", None),
            P("grp", None, "ctx", None),
        ),
        check_vma=False,
    )
```
